32 devices in a mesh: lev: 4 (over x, core), tile: 8 (over z, y).
Axes of the slice: x: 2, y: 2, z: 4, core: 2. Of those that a mesh axis runs over, the one named last changes fastest.
Arguments:
- inputs: bfloat16 [2, 8, 128, 72, 192], P(None, 'lev', 'tile'), may hold values from -6 to 6
- out_grad: bfloat16 [2, 8, 128, 72, 192], P(None, None, 'tile', 'lev'), may hold values from -6 to 6
- lowest_level: int32 [2, 128, 72], P(None, 'tile', 'lev'), may hold values from 0 to 3
- bias_index: int32 [72, 72], replicated, may hold values from 0 to 827, as said below
- first_gain: bfloat16 [192], P('tile'), may hold values from 0.5 to 1.5
- first_shift: bfloat16 [192], P('tile'), may hold values from -2 to 2
- window_in: bfloat16 [192, 576], P('tile'), may hold values from -0.4375 to 0.4375
- window_out: bfloat16 [192, 192], P('tile'), may hold values from -1.25 to 1.25
- earth_bias: bfloat16 [52992, 6], P('tile'), may hold values from -4 to 4
- second_gain: bfloat16 [192], P('tile'), may hold values from 0.5 to 1.5
- second_shift: bfloat16 [192], P('tile'), may hold values from -2 to 2
- column_in: bfloat16 [192, 576], P('tile'), may hold values from -0.4375 to 0.4375
- column_out: bfloat16 [192, 192], P('tile'), may hold values from -0.75 to 0.75
- third_gain: bfloat16 [192], P('tile'), may hold values from 0.5 to 1.5
- third_shift: bfloat16 [192], P('tile'), may hold values from -2 to 2
- expand_weight: bfloat16 [192, 768], P('tile'), may hold values from -0.4375 to 0.4375
- reduce_weight: bfloat16 [768, 192], P('tile'), may hold values from -0.21875 to 0.21875
Outputs:
- output: bfloat16 [2, 8, 128, 72, 192], P(None, None, 'tile', 'lev')
- input_grad: bfloat16 [2, 8, 128, 72, 192], P(None, 'lev', 'tile')
- first_gain_grad: float32 [192], P('tile')
- first_shift_grad: float32 [192], P('tile')
- window_in_grad: float32 [192, 576], P('tile')
- window_out_grad: float32 [192, 192], P('tile')
- earth_bias_grad: float32 [52992, 6], P('tile')
- second_gain_grad: float32 [192], P('tile')
- second_shift_grad: float32 [192], P('tile')
- column_in_grad: float32 [192, 576], P('tile')
- column_out_grad: float32 [192, 192], P('tile')
- third_gain_grad: float32 [192], P('tile')
- third_shift_grad: float32 [192], P('tile')
- expand_weight_grad: float32 [192, 768], P('tile')
- reduce_weight_grad: float32 [768, 192], P('tile')
The draws below stay inside these ranges and needn't reach their ends.
Inputs may be any that keep to these rules, and one draw needn't show every extreme that they name: `bias_index`: bias entry of a query cell and a key cell within a latitude band's 828 entries; every entry is named. `lowest_level`: levels below it are absent from the column and are never attended to.
All inputs are finite; a program needn't handle non-finite values.
Results may differ from the reference program's by a relative error of at most 0.022.
Values may be sent and summed in bfloat16 or wider, within the bound.
A program may use at most 256 MiB of HBM per device.

```python
import jax
import jax.numpy as jnp
from jax import lax

D = 192
HEADS = 6
HEAD_DIM = 32
FF = 768
LEVELS = 8
WIN = 72
RELB = 828
NWLON = 2
MB = 2
NWIN = 128
BIAS_ROWS = 52992


def draw_bias_index(key, part):
    key = jax.random.fold_in(key, 11)
    order = jax.random.permutation(key, WIN * WIN)
    return (order % RELB).reshape(WIN, WIN).astype(jnp.int32)


def touch_ends(entries, stream_key, low, largest):
    place = [jax.random.randint(jax.random.fold_in(stream_key, axis), (), 0, length) for axis, length in enumerate(entries.shape)]
    main_axis = entries.shape.index(max(entries.shape))
    beside = place[:main_axis] + [(place[main_axis] + 1) % entries.shape[main_axis]] + place[main_axis + 1:]
    return entries.at[tuple(place)].set(low).at[tuple(beside)].set(largest)


def block_levels(rng, extent, pieces, smallest, top_value):
    loudness = 1.0
    for axis_at, parts in pieces:
        steps = jax.random.uniform(jax.random.fold_in(jax.random.fold_in(rng, 6), axis_at), (parts,), jnp.float32, smallest / len(pieces), top_value / len(pieces))
        loudness = loudness * jnp.repeat(jnp.exp(steps), extent[axis_at] // parts).reshape((-1,) + (1,) * (len(extent) - 1 - axis_at))
    return loudness


def bell_draw(key, shape, scale, most, pieces=(), kind=jnp.bfloat16):
    array = jax.random.normal(key, shape, jnp.float32) * scale
    if len(pieces) > 0:
        array = block_levels(key, shape, pieces, -0.22, 0.18) * array
    return jnp.clip(array, min=-most, max=most).astype(kind)


def setup_inputs(seed: int = 0) -> dict:
    splits = jax.random.split(jax.random.key(seed), 18)
    inputs = bell_draw(splits[0], (MB, LEVELS, NWIN, WIN, D), 1.0, 6.0, ((1, 4), (2, 8)))
    out_grad = bell_draw(splits[1], (MB, LEVELS, NWIN, WIN, D), 1.0, 6.0, ((2, 8), (3, 4)))
    lowest_level = touch_ends(jax.random.randint(splits[2], (MB, NWIN, WIN), 0, 4), jax.random.fold_in(splits[2], 1), 0, 3).astype(jnp.int32)
    bias_index = draw_bias_index(jax.random.fold_in(splits[17], 71), 0)
    first_gain = jnp.clip(1.0 + 0.1 * jax.random.normal(splits[4], (D,), jnp.float32), 0.5, 1.5).astype(jnp.bfloat16)
    first_shift = bell_draw(splits[5], (D,), 0.3, 2.0, ((0, 8),))
    window_in = bell_draw(splits[6], (D, 3 * D), D ** -0.5, 0.4375, ((0, 8),))
    window_out = bell_draw(splits[7], (D, D), (D // 8) ** -0.5, 1.25, ((0, 8),))
    earth_bias = bell_draw(splits[8], (BIAS_ROWS, HEADS), 1.0, 4.0, ((0, 8),))
    second_gain = jnp.clip(1.0 + 0.1 * jax.random.normal(splits[9], (D,), jnp.float32), 0.5, 1.5).astype(jnp.bfloat16)
    second_shift = bell_draw(splits[10], (D,), 0.3, 2.0, ((0, 8),))
    column_in = bell_draw(splits[11], (D, 3 * D), D ** -0.5, 0.4375, ((0, 8),))
    column_out = bell_draw(splits[12], (D, D), (D // 3) ** -0.5, 0.75, ((0, 8),))
    third_gain = jnp.clip(1.0 + 0.1 * jax.random.normal(splits[13], (D,), jnp.float32), 0.5, 1.5).astype(jnp.bfloat16)
    third_shift = bell_draw(splits[14], (D,), 0.3, 2.0, ((0, 8),))
    expand_weight = bell_draw(splits[15], (D, FF), D ** -0.5, 0.4375, ((0, 8),))
    reduce_weight = bell_draw(splits[16], (FF, D), FF ** -0.5, 0.21875, ((0, 8),))
    return dict(inputs=inputs, out_grad=out_grad, lowest_level=lowest_level, bias_index=bias_index, first_gain=first_gain, first_shift=first_shift, window_in=window_in, window_out=window_out, earth_bias=earth_bias, second_gain=second_gain, second_shift=second_shift, column_in=column_in, column_out=column_out, third_gain=third_gain, third_shift=third_shift, expand_weight=expand_weight, reduce_weight=reduce_weight)


EPSILON = 1e-05
MASKED = -1e+30
PRECISE = lax.Precision.HIGHEST

@jax.custom_vjp
def low(v):
    return lax.optimization_barrier(v.astype(jnp.bfloat16)).astype(jnp.float32)

@jax.custom_vjp
def low_back(v):
    return v

def low_keep(v):
    return (low(v), None)

def low_pass(kept, grad):
    return (grad,)

def back_keep(v):
    return (v, None)

def back_low(kept, grad):
    return (low(grad),)
low.defvjp(low_keep, low_pass)
low_back.defvjp(back_keep, back_low)

def layer_norm(values, gain, shift):
    center = lax.optimization_barrier(jnp.mean(values, axis=-1, keepdims=True))
    centred = values - center
    spread = lax.optimization_barrier(jnp.mean(centred * centred, axis=-1, keepdims=True))
    return centred * lax.rsqrt(spread + EPSILON) * gain + shift

def project(values, weight):
    return jnp.einsum('...d,de->...e', values, weight, precision=PRECISE)

def window_branch(level_tokens, gain, shift, weight_in, weight_out, table, bias_rows):
    normed = low(layer_norm(level_tokens, gain, shift))
    packed = low(low_back(project(normed, weight_in)))
    packed = packed.reshape(level_tokens.shape[:-1] + (3, HEADS, HEAD_DIM))
    queries = packed[..., 0, :, :]
    key_vecs = packed[..., 1, :, :]
    value_vecs = packed[..., 2, :, :]
    bias = jnp.transpose(table[bias_rows], (0, 3, 1, 2))
    scores = jnp.einsum('wqhe,wkhe->whqk', queries, key_vecs, precision=PRECISE) * HEAD_DIM ** (-0.5) + bias
    scores = low_back(scores)
    weights_soft = low(jax.nn.softmax(scores, axis=-1))
    mixed = jnp.einsum('whqk,wkhe->wqhe', weights_soft, value_vecs, precision=PRECISE)
    mixed = low(low_back(mixed.reshape(level_tokens.shape)))
    return low_back(project(mixed, weight_out))

def sample_forward(sample_tokens, lowest_sample, params, bias_rows):
    first_gain, first_shift, window_in, window_out, earth_bias, second_gain, second_shift, column_in, column_out, third_gain, third_shift, expand_weight, reduce_weight = params
    branch = jax.checkpoint(window_branch)

    def one_level(level_tokens):
        return branch(level_tokens, first_gain, first_shift, window_in, window_out, earth_bias, bias_rows)
    window_result = lax.map(one_level, sample_tokens)
    middle = low(low_back(sample_tokens + window_result))
    normed = low(layer_norm(middle, second_gain, second_shift))
    packed = low(low_back(project(normed, column_in)))
    packed = packed.reshape(middle.shape[:-1] + (3, HEADS, HEAD_DIM))
    queries = packed[..., 0, :, :]
    key_vecs = packed[..., 1, :, :]
    value_vecs = packed[..., 2, :, :]
    scores = jnp.einsum('lwthe,mwthe->wthlm', queries, key_vecs, precision=PRECISE) * HEAD_DIM ** (-0.5)
    scores = low_back(scores)
    present = jnp.arange(LEVELS, dtype=jnp.int32)[None, None, :] >= lowest_sample[:, :, None]
    scores = jnp.where(present[:, :, None, None, :], scores, MASKED)
    weights_soft = low(jax.nn.softmax(scores, axis=-1))
    mixed = jnp.einsum('wthlm,mwthe->lwthe', weights_soft, value_vecs, precision=PRECISE)
    mixed = low(low_back(mixed.reshape(middle.shape)))
    second = middle + low_back(project(mixed, column_out))
    normed_ff = low(layer_norm(second, third_gain, third_shift))
    hidden = low(jax.nn.gelu(low_back(project(normed_ff, expand_weight)), approximate=True))
    return second + low_back(project(hidden, reduce_weight))

def reference(inputs, out_grad, lowest_level, bias_index, first_gain, first_shift, window_in, window_out, earth_bias, second_gain, second_shift, column_in, column_out, third_gain, third_shift, expand_weight, reduce_weight):
    params = tuple((p.astype(jnp.float32) for p in (first_gain, first_shift, window_in, window_out, earth_bias, second_gain, second_shift, column_in, column_out, third_gain, third_shift, expand_weight, reduce_weight)))
    bands = jnp.arange(NWIN, dtype=jnp.int32) // NWLON
    bias_rows = (bands[:, None, None] * RELB + bias_index[None, :, :]).astype(jnp.int32)
    tokens_wide = inputs.astype(jnp.float32)

    def forward(all_tokens, all_params):
        results = [sample_forward(all_tokens[sample], lowest_level[sample], all_params, bias_rows) for sample in range(MB)]
        return jnp.stack(results)
    result, pullback = jax.vjp(forward, tokens_wide, params)
    token_grad, grads = pullback(out_grad.astype(jnp.float32))
    return (result.astype(jnp.bfloat16), token_grad.astype(jnp.bfloat16), grads[0], grads[1], grads[2], grads[3], grads[4], grads[5], grads[6], grads[7], grads[8], grads[9], grads[10], grads[11], grads[12])
```

```python
import functools
import jax, jax.numpy as jnp
from jax import lax
from jax.experimental import pallas as pl
from jax.experimental.pallas import tpu as pltpu
from jax.sharding import PartitionSpec as P
HEADS=6; RELB=828; NWLON=2; HD=32; WIN=72; D=192
EPS=1e-5
SCALE=HD**-0.5
LOG2E=1.4426950408889634
F32=jnp.float32; BF=jnp.bfloat16

def dot(a,b,ca=1,cb=0):
    return lax.dot_general(a,b,(((ca,),(cb,)),((),())),preferred_element_type=F32)

def head_masks():
    lane=lax.broadcasted_iota(jnp.int32,(1,D),1)
    return [(lane//HD==h).astype(F32) for h in range(HEADS)]

def spread(v,masks):
    return jnp.concatenate([v*m for m in masks],axis=0).astype(BF)

def gather_heads(r,masks,n):
    tot=r[:n]*masks[0]
    for h in range(1,HEADS):
        tot=tot+r[h*n:(h+1)*n]*masks[h]
    return tot

def ln(x):
    mean=jnp.sum(x,-1,keepdims=True)*(1.0/D)
    c=x-mean
    var=jnp.sum(c*c,-1,keepdims=True)*(1.0/D)
    r=lax.rsqrt(var+EPS)
    return c*r, r

def put(ref,rows,v):
    n=v.shape[0]
    ref[0,rows,:]=v[:,:128]
    ref[1,rows,:]=jnp.concatenate([v[:,128:],jnp.zeros((n,64),F32)],axis=1)

def take(ref,rows):
    return jnp.concatenate([ref[0,rows,:],ref[1,rows,:][:,:64]],axis=1)

def wf_kernel(G,x_ref,bias_ref,win_ref,wout_ref,gs_ref,x1_ref,q_ref,k_ref,v_ref,p_ref,o_ref,mid_ref):
    W=x_ref.shape[2]
    masks=head_masks()
    gain=gs_ref[0:1,:]; shift=gs_ref[1:2,:]
    def group(gi,_):
        x=x_ref[0,0,pl.ds(gi*G,G)].astype(F32).reshape(G*WIN,D)
        xh,_r=ln(x)
        n1=(xh*gain+shift).astype(BF)
        q=dot(n1,win_ref[0]); k=dot(n1,win_ref[1]); v=dot(n1,win_ref[2])
        os=[]
        for w in range(G):
            sl=slice(w*WIN,(w+1)*WIN)
            qw=q[sl]; kb=k[sl].astype(BF); vb=v[sl].astype(BF)
            q_ref[0,0,gi*G+w]=qw.astype(BF); k_ref[0,0,gi*G+w]=kb; v_ref[0,0,gi*G+w]=vb
            st=dot(kb,spread(qw,masks),1,1)*(SCALE*LOG2E)+bias_ref[(gi*G+w)//2]
            m=jnp.max(st,0,keepdims=True)
            e=jnp.exp2(st-m)
            l=jnp.sum(e,0,keepdims=True)
            pb=(e*(1.0/l)).astype(BF)
            p_ref[0,0,gi*G+w]=pb
            r=dot(pb,vb,0,0)
            os.append(gather_heads(r,masks,WIN))
        o=jnp.concatenate(os,axis=0).astype(BF)
        o_ref[0,0,pl.ds(gi*G,G)]=o.astype(F32).reshape(G,WIN,D).astype(BF)
        x1=x+dot(o,wout_ref[...])
        for w in range(G):
            put(mid_ref,pl.ds(gi*G+w,WIN,stride=W),x1[w*WIN:(w+1)*WIN])
        return 0
    lax.fori_loop(0,W//G,group,0)
    x1_ref[0,0]=take(mid_ref,slice(None)).astype(BF)

def wf(x,bias,win,wout,gs,G=4):
    S,L,W=x.shape[:3]
    f=pl.pallas_call(functools.partial(wf_kernel,G),
      grid=(S,L),
      in_specs=[pl.BlockSpec((1,1,W,WIN,D),lambda s,l:(s,l,0,0,0)),
        pl.BlockSpec(bias.shape,lambda s,l:(0,0,0)),
        pl.BlockSpec((3,D,D),lambda s,l:(0,0,0)),
        pl.BlockSpec((D,D),lambda s,l:(0,0)),
        pl.BlockSpec(gs.shape,lambda s,l:(0,0))],
      out_specs=[pl.BlockSpec((1,1,W*WIN,D),lambda s,l:(s,l,0,0))]+[pl.BlockSpec((1,1,W,WIN,D),lambda s,l:(s,l,0,0,0))]*3+
        [pl.BlockSpec((1,1,W,WIN,HEADS*WIN),lambda s,l:(s,l,0,0,0)),pl.BlockSpec((1,1,W,WIN,D),lambda s,l:(s,l,0,0,0))],
      out_shape=[jax.ShapeDtypeStruct((S,L,W*WIN,D),BF)]+[jax.ShapeDtypeStruct((S,L,W,WIN,D),BF)]*3+
        [jax.ShapeDtypeStruct((S,L,W,WIN,HEADS*WIN),BF),jax.ShapeDtypeStruct((S,L,W,WIN,D),BF)],
      scratch_shapes=[pltpu.VMEM((2,W*WIN,128),F32)],
      compiler_params=pltpu.CompilerParams(vmem_limit_bytes=60<<20),
      name="wf")
    return f(x,bias,win,wout,gs)

def ln_back(xh,r,dn,gain):
    t=dn*gain
    a=jnp.sum(t,-1,keepdims=True)*(1.0/D)
    b=jnp.sum(t*xh,-1,keepdims=True)*(1.0/D)
    return r*(t-a-xh*b), jnp.sum(dn*xh,0,keepdims=True), jnp.sum(dn,0,keepdims=True)

def acc(ref,first,val,idx=None):
    idx=Ellipsis if idx is None else idx
    @pl.when(first)
    def _(): ref[idx]=val
    @pl.when(jnp.logical_not(first))
    def _(): ref[idx]=ref[idx]+val

def wb_kernel(G,d_ref,x_ref,q_ref,k_ref,v_ref,p_ref,o_ref,win_ref,wout_ref,gs_ref,
              dx_ref,dwin_ref,dwout_ref,dgs_ref,db_ref,mid_ref):
    W=x_ref.shape[2]
    masks=head_masks()
    gain=gs_ref[0:1,:]; shift=gs_ref[1:2,:]
    first=(pl.program_id(0)==0)&(pl.program_id(1)==0)
    @pl.when(first)
    def _():
        for r in (dwin_ref,dwout_ref,dgs_ref,db_ref): r[...]=jnp.zeros(r.shape,F32)
    dall=d_ref[0,0].astype(F32)
    put(mid_ref,slice(None),dall)
    dgain=jnp.zeros((1,D),F32); dshift=jnp.zeros((1,D),F32)
    n1s=[];dqs=[];dks=[];dvs=[];d1s=[];os=[]
    for g in range(W//G):
        d1=jnp.concatenate([take(mid_ref,pl.ds(g*G+w,WIN,stride=W)) for w in range(G)],axis=0)
        d1b=d1.astype(BF)
        do=dot(d1b,wout_ref[...],1,1)
        dq=[];dk=[];dv=[]
        for w in range(G):
            i=g*G+w
            qw=q_ref[0,0,i].astype(F32); kb=k_ref[0,0,i]; vb=v_ref[0,0,i]; pb=p_ref[0,0,i]
            pf=pb.astype(F32)
            dob=spread(do[w*WIN:(w+1)*WIN],masks)
            dpt=dot(vb,dob,1,1)
            inner=jnp.sum(dpt*pf,0,keepdims=True)
            ds=pf*(dpt-inner)
            dsb=ds.astype(BF)
            db_ref[i//2]=db_ref[i//2]+ds
            dv.append(dot(pb,dob))
            dk.append(dot(dsb,spread(qw,masks))*SCALE)
            dq.append(gather_heads(dot(dsb,kb,0,0),masks,WIN)*SCALE)
        dq=jnp.concatenate(dq,0).astype(BF); dk=jnp.concatenate(dk,0).astype(BF); dv=jnp.concatenate(dv,0).astype(BF)
        x=x_ref[0,0,g*G:(g+1)*G].astype(F32).reshape(G*WIN,D)
        xh,r=ln(x)
        n1s.append((xh*gain+shift).astype(BF))
        dn=dot(dq,win_ref[0],1,1)+dot(dk,win_ref[1],1,1)+dot(dv,win_ref[2],1,1)
        dx,a,b=ln_back(xh,r,dn,gain)
        dgain+=a; dshift+=b
        dx_ref[0,0,g*G:(g+1)*G]=(d1+dx).reshape(G,WIN,D).astype(BF)
        dqs.append(dq);dks.append(dk);dvs.append(dv);d1s.append(d1b)
        os.append(o_ref[0,0,g*G:(g+1)*G].astype(F32).reshape(G*WIN,D).astype(BF))
    n1=jnp.concatenate(n1s,0)
    for j,z in enumerate((dqs,dks,dvs)):
        dwin_ref[j]=dwin_ref[j]+dot(n1,jnp.concatenate(z,0),0,0)
    dwout_ref[...]=dwout_ref[...]+dot(jnp.concatenate(os,0),jnp.concatenate(d1s,0),0,0)
    dgs_ref[0:1,:]=dgs_ref[0:1,:]+dgain
    dgs_ref[1:2,:]=dgs_ref[1:2,:]+dshift

def wb(d,x,q,k,v,p,o,win,wout,gs,G=4):
    S,L,W=x.shape[:3]
    tok=pl.BlockSpec((1,1,W,WIN,D),lambda s,l:(s,l,0,0,0))
    def full(*sh): return pl.BlockSpec(sh,lambda s,l:(0,)*len(sh))
    f=pl.pallas_call(functools.partial(wb_kernel,G),
      grid=(S,L),
      in_specs=[pl.BlockSpec((1,1,W*WIN,D),lambda s,l:(s,l,0,0)),tok,tok,tok,tok,
        pl.BlockSpec((1,1,W,WIN,HEADS*WIN),lambda s,l:(s,l,0,0,0)),tok,
        full(3,D,D),full(D,D),full(8,D)],
      out_specs=[tok,full(3,D,D),full(D,D),full(8,D),full(W//2,WIN,HEADS*WIN)],
      out_shape=[jax.ShapeDtypeStruct((S,L,W,WIN,D),BF),jax.ShapeDtypeStruct((3,D,D),F32),jax.ShapeDtypeStruct((D,D),F32),
        jax.ShapeDtypeStruct((8,D),F32),jax.ShapeDtypeStruct((W//2,WIN,HEADS*WIN),F32)],
      scratch_shapes=[pltpu.VMEM((2,W*WIN,128),F32)],
      compiler_params=pltpu.CompilerParams(vmem_limit_bytes=60<<20),
      name="wb")
    return f(d,x,q,k,v,p,o,win,wout,gs)

def col_kernel(T,x1_ref,g_ref,low_ref,key_ref,cin_ref,cout_ref,ew_ref,rw_ref,gs_ref,
               out_ref,dx1_ref,dcin_ref,dcout_ref,dew_ref,drw_ref,dgs_ref):
    L=x1_ref.shape[1]; C=x1_ref.shape[2]
    NG=C//8; R=L*C; GR=L*8
    masks=head_masks()
    g2=gs_ref[2:3,:]; s2=gs_ref[3:4,:]; g3=gs_ref[4:5,:]; s3=gs_ref[5:6,:]
    first=(pl.program_id(0)==0)&(pl.program_id(1)==0)
    @pl.when(first)
    def _():
        for r in (dcin_ref,dcout_ref,dew_ref,drw_ref,dgs_ref): r[...]=jnp.zeros(r.shape,F32)
    def cols(v,j):
        return v.reshape(L,C,D)[:,j*8:(j+1)*8,:].reshape(GR,D)
    def join(parts):
        return jnp.concatenate([p.reshape(L,8,D) for p in parts],axis=1).reshape(R,D)
    x1=x1_ref[0].astype(F32).reshape(R,D)
    xh2,r2=ln(x1)
    n2=(xh2*g2+s2).astype(BF)
    q=dot(n2,cin_ref[0]);k=dot(n2,cin_ref[1]);v=dot(n2,cin_ref[2])
    key=key_ref[...]
    saved=[];o=[]
    for j in range(NG):
        qw=cols(q,j); kb=cols(k,j).astype(BF); vb=cols(v,j).astype(BF)
        qb=spread(qw,masks)
        st=dot(kb,qb,1,1)*(SCALE*LOG2E)
        st=jnp.where(key>=low_ref[0,j:j+1,:],st,-1e30)
        m=jnp.max(st,0,keepdims=True)
        e=jnp.exp2(st-m)
        l=jnp.sum(e,0,keepdims=True)
        p=e*(1.0/l)
        pb=p.astype(BF)
        o.append(gather_heads(dot(pb,vb,0,0),masks,GR))
        saved.append((qb,kb,vb,pb))
    o2=join(o).astype(BF)
    x2=x1+dot(o2,cout_ref[...])
    xh3,r3=ln(x2)
    n3=(xh3*g3+s3).astype(BF)
    gb=g_ref[0].astype(F32).reshape(R,D).astype(BF)
    u=dot(n3,ew_ref[...])
    dh=dot(gb,rw_ref[...],1,1)
    c=0.7978845608028654
    uu=u*u
    t=jnp.tanh(u*(c+(c*0.044715)*uu))
    hp=0.5+0.5*t
    hid=(u*hp).astype(BF)
    du=(dh*(hp+(0.5*u)*(1.0-t*t)*(c+(3*c*0.044715)*uu))).astype(BF)
    out_ref[0]=(x2+dot(hid,rw_ref[...])).reshape(L,C,D).astype(BF)
    drw_ref[...]=drw_ref[...]+dot(hid,gb,0,0)
    dew_ref[...]=dew_ref[...]+dot(n3,du,0,0)
    dn3=dot(du,ew_ref[...],1,1)
    dx,a3,b3=ln_back(xh3,r3,dn3,g3)
    dx2=gb.astype(F32)+dx
    dx2b=dx2.astype(BF)
    dcout_ref[...]=dcout_ref[...]+dot(o2,dx2b,0,0)
    do=dot(dx2b,cout_ref[...],1,1)
    dq=[];dk=[];dv=[]
    for j in range(NG):
        qb,kb,vb,pb=saved[j]
        pf=pb.astype(F32)
        dob=spread(cols(do,j),masks)
        dpt=dot(vb,dob,1,1)
        inner=jnp.sum(dpt*pf,0,keepdims=True)
        dsb=(pf*(dpt-inner)).astype(BF)
        dv.append(dot(pb,dob))
        dk.append(dot(dsb,qb)*SCALE)
        dq.append(gather_heads(dot(dsb,kb,0,0),masks,GR)*SCALE)
    dn2=0.0
    for j,z in enumerate((dq,dk,dv)):
        zb=join(z).astype(BF)
        dcin_ref[j]=dcin_ref[j]+dot(n2,zb,0,0)
        dn2=dn2+dot(zb,cin_ref[j],1,1)
    dx,a2,b2=ln_back(xh2,r2,dn2,g2)
    dx1_ref[0]=(dx2+dx).reshape(L,C,D).astype(BF)
    dgs_ref[2:3,:]=dgs_ref[2:3,:]+a2
    dgs_ref[3:4,:]=dgs_ref[3:4,:]+b2
    dgs_ref[4:5,:]=dgs_ref[4:5,:]+a3
    dgs_ref[5:6,:]=dgs_ref[5:6,:]+b3

def col(x1,g,low,key,cin,cout,ew,rw,gs,T=3):
    S,L,CC=x1.shape[:3]
    C=T*16
    FF=ew.shape[1]
    GR=L*8
    tok=pl.BlockSpec((1,L,C,D),lambda s,c:(s,0,c,0))
    def full(*sh): return pl.BlockSpec(sh,lambda s,c:(0,)*len(sh))
    low=low.reshape(S*(CC//C),C//8,HEADS*GR)
    nb=CC//C
    f=pl.pallas_call(functools.partial(col_kernel,T),
      grid=(S,nb),
      in_specs=[tok,tok,pl.BlockSpec((1,C//8,HEADS*GR),lambda s,c:(s*nb+c,0,0)),full(GR,HEADS*GR),
        full(3,D,D),full(D,D),full(D,FF),full(FF,D),full(8,D)],
      out_specs=[tok,tok,full(3,D,D),full(D,D),full(D,FF),full(FF,D),full(8,D)],
      out_shape=[jax.ShapeDtypeStruct((S,L,CC,D),BF)]*2+[jax.ShapeDtypeStruct(z,F32) for z in ((3,D,D),(D,D),(D,FF),(FF,D),(8,D))],
      compiler_params=pltpu.CompilerParams(vmem_limit_bytes=60<<20),
      name="col")
    return f(x1,g,low,key,cin,cout,ew,rw,gs)


def body(lev_count,tile_count,inputs,out_grad,lowest_level,bias_index,first_gain,first_shift,window_in,window_out,earth_bias,
         second_gain,second_shift,column_in,column_out,third_gain,third_shift,expand_weight,reduce_weight):
    S,L,W=inputs.shape[:3]
    LV=out_grad.shape[1]
    cells=out_grad.shape[3]
    bands=W//NWLON
    rows=D//tile_count
    FF=expand_weight.shape[1]
    vecs=jnp.stack([first_gain,first_shift,second_gain,second_shift,third_gain,third_shift],axis=1)
    packed=jnp.concatenate([window_in,window_out,column_in,column_out,expand_weight,reduce_weight.reshape(rows,FF),vecs],axis=1)
    full=lax.all_gather(packed,"tile",axis=0,tiled=True)
    def heads3(m): return m.reshape(D,3,D).transpose(1,0,2)
    win=heads3(full[:,0:3*D]); wout=full[:,3*D:4*D]
    cin=heads3(full[:,4*D:7*D]); cout=full[:,7*D:8*D]
    ew=full[:,8*D:8*D+FF]; rw=full[:,8*D+FF:8*D+2*FF].reshape(FF,D)
    gs=jnp.pad(full[:,8*D+2*FF:].astype(F32).T,((0,2),(0,0)))
    select=(bias_index.T.reshape(-1)[:,None]==jnp.arange(RELB,dtype=jnp.int32)[None,:]).astype(BF)
    table=earth_bias.T.reshape(HEADS*bands,RELB)
    bias=jnp.einsum("ar,kr->ak",table,select,preferred_element_type=F32)*LOG2E
    bias=bias.reshape(HEADS,bands,WIN,WIN).transpose(1,2,0,3).reshape(bands,WIN,HEADS*WIN)
    x1,q,k,v,p,o=wf(inputs,bias,win,wout,gs,G=W)
    x1c=lax.all_to_all(x1,"lev",split_axis=2,concat_axis=1,tiled=True)
    g=out_grad.transpose(0,1,3,2,4).reshape(S,LV,cells*W,D)
    low=lowest_level.transpose(0,2,1).reshape(S,cells*W//8,1,8)
    low=jnp.broadcast_to(low,(S,cells*W//8,HEADS*LV,8)).reshape(S,cells*W//8,HEADS*LV*8)
    i0=lax.broadcasted_iota(jnp.int32,(LV*8,HEADS*LV*8),0); i1=lax.broadcasted_iota(jnp.int32,(LV*8,HEADS*LV*8),1)
    key=jnp.where(i0%8==i1%8,i0//8,-1)
    T=6 if cells%6==0 else 3
    out,dx1c,dcin,dcout,dew,drw,dgsc=col(x1c,g,low,key,cin,cout,ew,rw,gs,T=T)
    dx1=lax.all_to_all(dx1c,"lev",split_axis=1,concat_axis=2,tiled=True)
    dx,dwin,dwout,dgsw,db=wb(dx1,inputs,q,k,v,p,o,win,wout,gs,G=4)
    dbt=db.reshape(bands,WIN,HEADS,WIN).transpose(2,0,1,3).reshape(HEADS*bands,WIN*WIN).astype(BF)
    dtab=jnp.einsum("ak,kr->ar",dbt,select,preferred_element_type=F32).astype(BF).reshape(HEADS,bands*RELB)
    dtab=lax.psum(dtab,"lev").astype(F32).T
    def flat3(m): return m.transpose(1,0,2).reshape(D,3*D)
    gpack=jnp.concatenate([flat3(dwin),dwout,flat3(dcin),dcout,dew,drw.reshape(D,FF),(dgsc+dgsw)[:6].T],axis=1).astype(BF)
    share=lax.psum_scatter(gpack,"tile",scatter_dimension=0,tiled=True)
    share=lax.psum(share,"lev").astype(F32)
    sv=share[:,8*D+2*FF:]
    output=out.reshape(S,LV,cells,W,D).transpose(0,1,3,2,4)
    return (output,dx,sv[:,0],sv[:,1],share[:,:3*D],share[:,3*D:4*D],dtab,sv[:,2],sv[:,3],share[:,4*D:7*D],share[:,7*D:8*D],
            sv[:,4],sv[:,5],share[:,8*D:8*D+FF],share[:,8*D+FF:8*D+2*FF].reshape(reduce_weight.shape))

def solution(mesh):
    t=P("tile"); t2=P("tile",None)
    tok_in=P(None,"lev","tile",None,None); tok_out=P(None,None,"tile","lev",None)
    placed=(tok_in,tok_out,P(None,"tile","lev"),P(),t,t,t2,t2,t2,t,t,t2,t2,t,t,t2,t2)
    outs=(tok_out,tok_in,t,t,t2,t2,t2,t,t,t2,t2,t,t,t2,t2)
    return jax.shard_map(functools.partial(body,mesh.shape["lev"],mesh.shape["tile"]),mesh=mesh,in_specs=placed,out_specs=outs,check_vma=False)
```

```python
import functools

import jax
import jax.numpy as jnp
from jax import lax
from jax.experimental import pallas as pl
from jax.experimental.pallas import tpu as pltpu
from jax.sharding import PartitionSpec as P

HEADS = 6
HEAD_DIM = 32
D = HEADS * HEAD_DIM
WIN = 72
RELB = 828
RELP = 832
NWLON = 2
EPSILON = 1e-05
SCALE = HEAD_DIM ** (-0.5)
LOG2E = 1.4426950408889634
MASKED = -1e30
F32 = jnp.float32
BF = jnp.bfloat16
MESH = pl.DeviceIdType.MESH
VMEM_LIMIT = 60 << 20


def dot(a, b, ca=1, cb=0):
    return lax.dot_general(a, b, (((ca,), (cb,)), ((), ())), preferred_element_type=F32)


def head_masks():
    lane = lax.broadcasted_iota(jnp.int32, (1, D), 1)
    return [(lane // HEAD_DIM == h).astype(F32) for h in range(HEADS)]


def spread(v, masks):
    return jnp.concatenate([v * m for m in masks], axis=0).astype(BF)


def gather_heads(r, masks, n):
    total = r[:n] * masks[0]
    for h in range(1, HEADS):
        total = total + r[h * n : (h + 1) * n] * masks[h]
    return total


def norm(x):
    mean = jnp.sum(x, -1, keepdims=True) * (1.0 / D)
    c = x - mean
    var = jnp.sum(c * c, -1, keepdims=True) * (1.0 / D)
    r = lax.rsqrt(var + EPSILON)
    return c * r, r


def norm_back(xh, r, dn, gain):
    t = dn * gain
    a = jnp.sum(t, -1, keepdims=True) * (1.0 / D)
    b = jnp.sum(t * xh, -1, keepdims=True) * (1.0 / D)
    return r * (t - a - xh * b), jnp.sum(dn * xh, 0, keepdims=True), jnp.sum(dn, 0, keepdims=True)


def softmax2(st):
    e = jnp.exp2(st - jnp.max(st, 0, keepdims=True))
    return e * (1.0 / jnp.sum(e, 0, keepdims=True))


def put(ref, rows, v):
    n = v.shape[0]
    ref[0, rows, :] = v[:, :128]
    ref[1, rows, :] = jnp.concatenate([v[:, 128:], jnp.zeros((n, 256 - D), F32)], axis=1)


def take(ref, rows):
    return jnp.concatenate([ref[0, rows, :], ref[1, rows, :][:, : D - 128]], axis=1)


def fold(ref, at, v):
    c = v.shape[0]
    ref[at + (slice(0, c),)] = v[:, :128].astype(BF)
    tail = jnp.concatenate([v[: c // 2, 128:], v[c // 2 :, 128:]], axis=1)
    ref[at + (slice(c, c + c // 2),)] = tail.astype(BF)


def unfold(block):
    c = block.shape[0] * 2 // 3
    wide = block.astype(F32)
    tail = wide[c:]
    return jnp.concatenate([wide[:c], jnp.concatenate([tail[:, :64], tail[:, 64:]], axis=0)], axis=1)


def one_hot(idx_ref, j):
    entry = lax.broadcasted_iota(jnp.int32, (RELP, 128), 0)
    return (entry == idx_ref[j : j + 1, :]).astype(F32).astype(BF)


def barrier(axes):
    sem = pltpu.get_barrier_semaphore()
    count = 0
    for axis, size in axes:
        me = lax.axis_index(axis)
        for j in range(1, size):
            pl.semaphore_signal(sem, inc=1, device_id={axis: lax.rem(me + j, size)}, device_id_type=MESH)
            count += 1
    pl.semaphore_wait(sem, count)


def to_peer(axis, size, j, src, dst, send, recv):
    me = lax.axis_index(axis)
    return pltpu.make_async_remote_copy(
        src_ref=src, dst_ref=dst, send_sem=send, recv_sem=recv,
        device_id={axis: lax.rem(me + j, size)}, device_id_type=MESH,
    )


def fold_rows(m):
    n = m.shape[0]
    if n % 32 == 0:
        return jnp.concatenate([m[: n // 2], m[n // 2 :]], axis=1)
    return m


def unfold_rows(m):
    if m.shape[1] == D:
        return m
    return jnp.concatenate([m[:, :D], m[:, D:]], axis=0)


class Sizes:
    def __init__(self, mesh, inputs, out_grad, expand):
        self.nl = mesh.shape["lev"]
        self.nt = mesh.shape["tile"]
        self.S, self.L, self.W = inputs.shape[:3]
        self.LV = out_grad.shape[1]
        self.cells = out_grad.shape[3]
        self.bands = self.W // NWLON
        self.rows = D // self.nt
        self.rpad = -(-self.rows // 8) * 8
        self.FF = expand.shape[1]
        self.frows = self.FF // self.nt
        self.T = 6 if self.cells % 6 == 0 else 3
        self.NCH = self.cells // self.T
        self.C = self.T * self.W
        self.CB = self.C * 3 // 2
        self.fshape = (self.frows // 2, 2 * D) if self.frows % 32 == 0 else (self.frows, D)


def window_forward_kernel(z, x_ref, idx_ref, tab_ref, wi_ref, wo_ref, ci_ref, co_ref, ew_ref, rw_ref, vec_ref,
                          x1_ref, q_ref, k_ref, v_ref, p_ref, o_ref, win_ref, wout_ref, cin_ref, cout_ref, ewf_ref, rwf_ref, gs_ref,
                          bias_ref, bbuf_ref, mid_ref, xs_ref, w1s, w1r, w2s, w2r, w3s, w3r, wide, widef,
                          xsend, xrecv, xloc, wsend, wrecv):
    s, l = pl.program_id(0), pl.program_id(1)
    step = s * z.L + l
    me_l, me_t = lax.axis_index("lev"), lax.axis_index("tile")
    W = z.W
    masks = head_masks()
    weights = ((w1s, w1r), (w2s, w2r), (w3s, w3r))

    def weight_copy(i, j):
        src, dst = weights[i]
        return to_peer("tile", z.nt, j, src, dst.at[me_t], wsend.at[i, j - 1], wrecv.at[i, j - 1])

    @pl.when(step == 0)
    def _():
        w1s[...] = jnp.zeros(w1s.shape, BF)
        w1s[0 : z.rows, 0 : 3 * D] = wi_ref[...]
        w1s[0 : z.rows, 3 * D : 4 * D] = wo_ref[...]
        w1s[z.rpad : z.rpad + 8, 0 : z.rows] = vec_ref[...]
        w2s[:, 0 : 3 * D] = ci_ref[...]
        w2s[:, 3 * D : 4 * D] = co_ref[...]
        w2s[:, 4 * D : 4 * D + z.FF] = ew_ref[...]
        w3s[...] = fold_rows(rw_ref[...].astype(F32)).astype(BF)
        barrier((("lev", z.nl), ("tile", z.nt)))
        for i in range(3):
            for j in range(1, z.nt):
                weight_copy(i, j).start()
        for src, dst in weights:
            dst[pl.ds(me_t, 1)] = src[...][None]
        table = tab_ref[...].astype(F32)
        pads = jnp.zeros((8, RELP - RELB), F32)
        table = jnp.concatenate(
            [jnp.concatenate([table[:, b * RELB : (b + 1) * RELB], pads], axis=1) for b in range(z.bands)], axis=0
        )
        table = (table * 1.0).astype(BF)
        n = z.bands * 8
        for j in range(0, WIN, 2):
            both = jnp.concatenate([one_hot(idx_ref, j), one_hot(idx_ref, j + 1)], axis=1)
            vals = dot(table, both) * LOG2E
            bbuf_ref[pl.ds(j, n, stride=WIN), :] = vals[:, :128]
            bbuf_ref[pl.ds(j + 1, n, stride=WIN), :] = vals[:, 128:]
        for b in range(z.bands):
            bias_ref[b] = jnp.concatenate(
                [bbuf_ref[(b * 8 + h) * WIN : (b * 8 + h + 1) * WIN, :][:, :WIN] for h in range(HEADS)], axis=1
            )
        for j in range(1, z.nt):
            weight_copy(0, j).wait_recv()
        for t in range(z.nt):
            wide[t * z.rows : (t + 1) * z.rows, 0 : 4 * D] = w1r[t, 0 : z.rows, :].astype(F32)
        for i in range(3):
            win_ref[i] = wide[:, i * D : (i + 1) * D].astype(BF)
        wout_ref[...] = wide[:, 3 * D : 4 * D].astype(BF)
        gs_ref[...] = jnp.concatenate([w1r[t, z.rpad : z.rpad + 8, :].astype(F32)[:, : z.rows] for t in range(z.nt)], axis=1)

    gain, shift = gs_ref[0:1, :], gs_ref[1:2, :]
    x = x_ref[0, 0].astype(F32).reshape(W * WIN, D)
    xh, _ = norm(x)
    n1 = (xh * gain + shift).astype(BF)
    q, k, v = (dot(n1, win_ref[i]) for i in range(3))
    mixed = []
    for w in range(W):
        rows = slice(w * WIN, (w + 1) * WIN)
        qw, kb, vb = q[rows], k[rows].astype(BF), v[rows].astype(BF)
        q_ref[0, 0, w] = qw.astype(BF)
        k_ref[0, 0, w] = kb
        v_ref[0, 0, w] = vb
        st = dot(kb, spread(qw, masks), 1, 1) * (SCALE * LOG2E) + bias_ref[w // NWLON]
        pb = softmax2(st).astype(BF)
        p_ref[0, 0, w] = pb
        mixed.append(gather_heads(dot(pb, vb, 0, 0), masks, WIN))
    o = jnp.concatenate(mixed, axis=0).astype(BF)
    o_ref[0, 0] = o.astype(F32).reshape(W, WIN, D).astype(BF)
    x1 = x + dot(o, wout_ref[...])
    for w in range(W):
        put(mid_ref, pl.ds(w, WIN, stride=W), x1[w * WIN : (w + 1) * WIN])
    for d in range(z.nl):
        for c in range(z.NCH):
            at = (d * z.NCH + c) * z.C
            fold(xs_ref, (step, d, c), take(mid_ref, slice(at, at + z.C)))

    def stream_copy(st_, s_, l_, j):
        return to_peer("lev", z.nl, j, xs_ref.at[st_, lax.rem(me_l + j, z.nl)], x1_ref.at[s_, me_l * z.L + l_],
                       xsend.at[st_, j - 1], xrecv.at[st_, j - 1])

    def stream_own(st_, s_, l_):
        return pltpu.make_async_copy(xs_ref.at[st_, me_l], x1_ref.at[s_, me_l * z.L + l_], xloc.at[st_])

    for j in range(1, z.nl):
        stream_copy(step, s, l, j).start()
    stream_own(step, s, l).start()

    @pl.when(step == z.S * z.L - 1)
    def _():
        for i in (1, 2):
            for j in range(1, z.nt):
                weight_copy(i, j).wait_recv()
        for t in range(z.nt):
            wide[t * z.rows : (t + 1) * z.rows, :] = w2r[t].astype(F32)
            widef[t * z.frows : (t + 1) * z.frows, :] = unfold_rows(w3r[t].astype(F32))
        for i in range(3):
            cin_ref[i] = wide[:, i * D : (i + 1) * D].astype(BF)
        cout_ref[...] = wide[:, 3 * D : 4 * D].astype(BF)
        ewf_ref[...] = wide[:, 4 * D : 4 * D + z.FF].astype(BF)
        rwf_ref[...] = widef[...].astype(BF)
        for i in range(3):
            for j in range(1, z.nt):
                weight_copy(i, j).wait_send()
        for s_ in range(z.S):
            for l_ in range(z.L):
                stream_own(s_ * z.L + l_, s_, l_).wait()
                for j in range(1, z.nl):
                    stream_copy(s_ * z.L + l_, s_, l_, j).wait()


def full_spec(*shape):
    return pl.BlockSpec(shape, lambda s, l: (0,) * len(shape))


def dma(*shape):
    return pltpu.SemaphoreType.DMA(shape)


def window_forward(z, x, idx, tab, wi, wo, ci, co, ew, rw, vec):
    S, L, W, A = z.S, z.L, z.W, HEADS * WIN
    tok = pl.BlockSpec((1, 1, W, WIN, D), lambda s, l: (s, l, 0, 0, 0))
    prob = pl.BlockSpec((1, 1, W, WIN, A), lambda s, l: (s, l, 0, 0, 0))
    ins = (idx, tab, wi, wo, ci, co, ew, rw, vec)
    tokens = jax.ShapeDtypeStruct((S, L, W, WIN, D), BF)
    fulls = ((3, D, D), (D, D), (3, D, D), (D, D), (D, z.FF), (z.FF, D))
    lanes2 = 4 * D + z.FF
    return pl.pallas_call(
        functools.partial(window_forward_kernel, z),
        grid=(S, L),
        in_specs=[tok] + [full_spec(*a.shape) for a in ins],
        out_specs=[pl.BlockSpec(memory_space=pl.ANY), tok, tok, tok, prob, tok] + [full_spec(*f) for f in fulls] + [full_spec(8, D)],
        out_shape=[jax.ShapeDtypeStruct((S, z.LV, z.NCH, z.CB, 128), BF), tokens, tokens, tokens,
                   jax.ShapeDtypeStruct((S, L, W, WIN, A), BF), tokens]
        + [jax.ShapeDtypeStruct(f, BF) for f in fulls] + [jax.ShapeDtypeStruct((8, D), F32)],
        scratch_shapes=[
            pltpu.VMEM((z.bands, WIN, A), F32),
            pltpu.VMEM((z.bands * 8 * WIN, 128), F32),
            pltpu.VMEM((2, W * WIN, 128), F32),
            pltpu.VMEM((S * L, z.nl, z.NCH, z.CB, 128), BF),
            pltpu.VMEM((z.rpad + 8, 4 * D), BF), pltpu.VMEM((z.nt, z.rpad + 8, 4 * D), BF),
            pltpu.VMEM((z.rows, lanes2), BF), pltpu.VMEM((z.nt, z.rows, lanes2), BF),
            pltpu.VMEM(z.fshape, BF), pltpu.VMEM((z.nt,) + z.fshape, BF),
            pltpu.VMEM((D, lanes2), F32), pltpu.VMEM((z.FF, D), F32),
            dma(S * L, z.nl - 1), dma(S * L, z.nl - 1), dma(S * L), dma(3, z.nt - 1), dma(3, z.nt - 1),
        ],
        compiler_params=pltpu.CompilerParams(vmem_limit_bytes=VMEM_LIMIT, collective_id=0, has_side_effects=True),
        name="window_forward",
    )(x, *ins)


def column_kernel(z, x1_ref, g_ref, low_ref, key_ref, cin_ref, cout_ref, ew_ref, rw_ref, gs_ref,
                  out_ref, dx1_ref, dcin_ref, dcout_ref, dew_ref, drw_ref, dgs_ref, xs_ref, xsend, xrecv, xloc):
    s, ch = pl.program_id(0), pl.program_id(1)
    step = s * z.NCH + ch
    me_l = lax.axis_index("lev")
    L, C = z.LV, z.C
    groups, R, GR = C // 8, L * C, L * 8
    masks = head_masks()
    g2, s2, g3, s3 = (gs_ref[i : i + 1, :] for i in range(2, 6))

    @pl.when(step == 0)
    def _():
        for ref in (dcin_ref, dcout_ref, dew_ref, drw_ref, dgs_ref):
            ref[...] = jnp.zeros(ref.shape, F32)
        barrier((("lev", z.nl),))

    def cols(v, j):
        return v.reshape(L, C, D)[:, j * 8 : (j + 1) * 8, :].reshape(GR, D)

    def join(parts):
        return jnp.concatenate([p.reshape(L, 8, D) for p in parts], axis=1).reshape(R, D)

    x1 = jnp.concatenate([unfold(x1_ref[0, i, 0]) for i in range(L)], axis=0)
    xh2, r2 = norm(x1)
    n2 = (xh2 * g2 + s2).astype(BF)
    q, k, v = (dot(n2, cin_ref[i]) for i in range(3))
    key = key_ref[...]
    saved = []
    mixed = []
    for j in range(groups):
        kb, vb = cols(k, j).astype(BF), cols(v, j).astype(BF)
        qb = spread(cols(q, j), masks)
        st = dot(kb, qb, 1, 1) * (SCALE * LOG2E)
        pb = softmax2(jnp.where(key >= low_ref[0, j : j + 1, :], st, MASKED)).astype(BF)
        mixed.append(gather_heads(dot(pb, vb, 0, 0), masks, GR))
        saved.append((qb, kb, vb, pb))
    o2 = join(mixed).astype(BF)
    x2 = x1 + dot(o2, cout_ref[...])
    xh3, r3 = norm(x2)
    n3 = (xh3 * g3 + s3).astype(BF)
    gb = g_ref[0].astype(F32).reshape(R, D).astype(BF)
    u = dot(n3, ew_ref[...])
    dh = dot(gb, rw_ref[...], 1, 1)
    c = 0.7978845608028654
    uu = u * u
    t = jnp.tanh(u * (c + (c * 0.044715) * uu))
    hp = 0.5 + 0.5 * t
    hid = (u * hp).astype(BF)
    du = (dh * (hp + (0.5 * u) * (1.0 - t * t) * (c + (3 * c * 0.044715) * uu))).astype(BF)
    out_ref[0] = (x2 + dot(hid, rw_ref[...])).reshape(L, C, D).astype(BF)
    drw_ref[...] = drw_ref[...] + dot(hid, gb, 0, 0)
    dew_ref[...] = dew_ref[...] + dot(n3, du, 0, 0)
    dn3 = dot(du, ew_ref[...], 1, 1)
    dx, a3, b3 = norm_back(xh3, r3, dn3, g3)
    dx2 = gb.astype(F32) + dx
    dx2b = dx2.astype(BF)
    dcout_ref[...] = dcout_ref[...] + dot(o2, dx2b, 0, 0)
    do = dot(dx2b, cout_ref[...], 1, 1)
    dq, dk, dv = [], [], []
    for j in range(groups):
        qb, kb, vb, pb = saved[j]
        pf = pb.astype(F32)
        dob = spread(cols(do, j), masks)
        dpt = dot(vb, dob, 1, 1)
        dsb = (pf * (dpt - jnp.sum(dpt * pf, 0, keepdims=True))).astype(BF)
        dv.append(dot(pb, dob))
        dk.append(dot(dsb, qb) * SCALE)
        dq.append(gather_heads(dot(dsb, kb, 0, 0), masks, GR) * SCALE)
    dn2 = 0.0
    for i, part in enumerate((dq, dk, dv)):
        pack = join(part).astype(BF)
        dcin_ref[i] = dcin_ref[i] + dot(n2, pack, 0, 0)
        dn2 = dn2 + dot(pack, cin_ref[i], 1, 1)
    dx, a2, b2 = norm_back(xh2, r2, dn2, g2)
    dx1 = dx2 + dx
    for i in range(L):
        fold(xs_ref, (step, i), dx1[i * C : (i + 1) * C])
    for i, part in enumerate((a2, b2, a3, b3)):
        dgs_ref[i + 2 : i + 3, :] = dgs_ref[i + 2 : i + 3, :] + part

    def levels(d):
        return pl.ds(d * z.L, z.L)

    def stream_copy(st_, s_, c_, j):
        return to_peer("lev", z.nl, j, xs_ref.at[st_, levels(lax.rem(me_l + j, z.nl))], dx1_ref.at[s_, :, me_l, c_],
                       xsend.at[st_, j - 1], xrecv.at[st_, j - 1])

    def stream_own(st_, s_, c_):
        return pltpu.make_async_copy(xs_ref.at[st_, levels(me_l)], dx1_ref.at[s_, :, me_l, c_], xloc.at[st_])

    for j in range(1, z.nl):
        stream_copy(step, s, ch, j).start()
    stream_own(step, s, ch).start()

    @pl.when(step == z.S * z.NCH - 1)
    def _():
        for s_ in range(z.S):
            for c_ in range(z.NCH):
                stream_own(s_ * z.NCH + c_, s_, c_).wait()
                for j in range(1, z.nl):
                    stream_copy(s_ * z.NCH + c_, s_, c_, j).wait()


def column(z, x1, g, low, key, cin, cout, ew, rw, gs):
    S, LV, NCH, C, CB = z.S, z.LV, z.NCH, z.C, z.CB
    steps = S * NCH
    tok = pl.BlockSpec((1, LV, C, D), lambda s, c: (s, 0, c, 0))
    ins = (key, cin, cout, ew, rw, gs)
    fulls = ((3, D, D), (D, D), (D, z.FF), (z.FF, D), (8, D))
    return pl.pallas_call(
        functools.partial(column_kernel, z),
        grid=(S, NCH),
        in_specs=[pl.BlockSpec((1, LV, 1, CB, 128), lambda s, c: (s, 0, c, 0, 0)), tok,
                  pl.BlockSpec((1,) + low.shape[1:], lambda s, c: (s * NCH + c, 0, 0))] + [full_spec(*a.shape) for a in ins],
        out_specs=[tok, pl.BlockSpec(memory_space=pl.ANY)] + [full_spec(*f) for f in fulls],
        out_shape=[jax.ShapeDtypeStruct(g.shape, BF), jax.ShapeDtypeStruct((S, z.L, z.nl, NCH, CB, 128), BF)]
        + [jax.ShapeDtypeStruct(f, F32) for f in fulls],
        scratch_shapes=[pltpu.VMEM((steps, LV, CB, 128), BF), dma(steps, z.nl - 1), dma(steps, z.nl - 1), dma(steps)],
        compiler_params=pltpu.CompilerParams(vmem_limit_bytes=VMEM_LIMIT, collective_id=1, has_side_effects=True),
        name="column",
    )(x1, g, low, *ins)


def window_backward_kernel(z, d_ref, x_ref, q_ref, k_ref, v_ref, p_ref, o_ref, win_ref, wout_ref, gs_ref, idx_ref,
                           dcin_ref, dcout_ref, dew_ref, drw_ref, dgsc_ref,
                           dx_ref, owi_ref, owo_ref, oci_ref, oco_ref, oew_ref, orw_ref, ovec_ref, otab_ref,
                           mid_ref, db_ref, dwin_ref, dwout_ref, dgs_ref, bbuf_ref,
                           g1s, g1r, g2s, g2r, g3s, g3r, h1s, h1r, h2s, h2r, h3s, h3r, ts, tr,
                           gsend, grecv, hsend, hrecv, tsend, trecv):
    s, l = pl.program_id(0), pl.program_id(1)
    step = s * z.L + l
    last = z.S * z.L - 1
    me_t = lax.axis_index("tile")
    W = z.W
    masks = head_masks()
    gain, shift = gs_ref[0:1, :], gs_ref[1:2, :]
    first_stage = ((g1s, g1r), (g2s, g2r), (g3s, g3r))
    second_stage = ((h1s, h1r), (h2s, h2r), (h3s, h3r))

    def tile_copy(i, j):
        src, dst = first_stage[i]
        return to_peer("tile", z.nt, j, src.at[lax.rem(me_t + j, z.nt)], dst.at[j - 1], gsend.at[i, j - 1], grecv.at[i, j - 1])

    def lev_copy(i, j):
        src, dst = second_stage[i]
        return to_peer("lev", z.nl, j, src, dst.at[j - 1], hsend.at[i, j - 1], hrecv.at[i, j - 1])

    def tab_copy(j):
        return to_peer("lev", z.nl, j, ts, tr.at[j - 1], tsend.at[j - 1], trecv.at[j - 1])

    def tile_sum(i):
        src, dst = first_stage[i]
        for j in range(1, z.nt):
            tile_copy(i, j).wait_recv()
        total = src[pl.ds(me_t, 1)][0].astype(F32)
        for j in range(1, z.nt):
            total = total + dst[j - 1].astype(F32)
        second_stage[i][0][...] = total.astype(BF)
        for j in range(1, z.nl):
            lev_copy(i, j).start()

    def lev_sum(i):
        src, dst = second_stage[i]
        total = src[...].astype(F32)
        for j in range(1, z.nl):
            lev_copy(i, j).wait_recv()
            total = total + dst[j - 1].astype(F32)
        return total

    @pl.when(step == 0)
    def _():
        for ref in (dwin_ref, dwout_ref, dgs_ref, db_ref):
            ref[...] = jnp.zeros(ref.shape, F32)
        for t in range(z.nt):
            rows = slice(t * z.rows, (t + 1) * z.rows)
            for i in range(3):
                g2s[t, :, i * D : (i + 1) * D] = dcin_ref[i, rows, :].astype(BF)
            g2s[t, :, 3 * D : 4 * D] = dcout_ref[rows, :].astype(BF)
            g2s[t, :, 4 * D :] = dew_ref[rows, :].astype(BF)
            g3s[t] = fold_rows(drw_ref[t * z.frows : (t + 1) * z.frows, :]).astype(BF)
        barrier((("lev", z.nl), ("tile", z.nt)))
        for i in (1, 2):
            for j in range(1, z.nt):
                tile_copy(i, j).start()

    for d in range(z.nl):
        for c in range(z.NCH):
            at = (d * z.NCH + c) * z.C
            put(mid_ref, slice(at, at + z.C), unfold(d_ref[0, 0, d, c]))
    G = 4
    dgain, dshift = jnp.zeros((1, D), F32), jnp.zeros((1, D), F32)
    n1s, dqs, dks, dvs, d1s, os = [], [], [], [], [], []
    for g in range(W // G):
        d1 = jnp.concatenate([take(mid_ref, pl.ds(g * G + w, WIN, stride=W)) for w in range(G)], axis=0)
        d1b = d1.astype(BF)
        do = dot(d1b, wout_ref[...], 1, 1)
        dq, dk, dv = [], [], []
        for w in range(G):
            i = g * G + w
            kb, vb, pb = k_ref[0, 0, i], v_ref[0, 0, i], p_ref[0, 0, i]
            pf = pb.astype(F32)
            dob = spread(do[w * WIN : (w + 1) * WIN], masks)
            dpt = dot(vb, dob, 1, 1)
            ds = pf * (dpt - jnp.sum(dpt * pf, 0, keepdims=True))
            dsb = ds.astype(BF)
            db_ref[i // NWLON] = db_ref[i // NWLON] + ds
            dv.append(dot(pb, dob))
            dk.append(dot(dsb, spread(q_ref[0, 0, i].astype(F32), masks)) * SCALE)
            dq.append(gather_heads(dot(dsb, kb, 0, 0), masks, WIN) * SCALE)
        dq, dk, dv = (jnp.concatenate(a, axis=0).astype(BF) for a in (dq, dk, dv))
        x = x_ref[0, 0, g * G : (g + 1) * G].astype(F32).reshape(G * WIN, D)
        xh, r = norm(x)
        n1s.append((xh * gain + shift).astype(BF))
        dn = dot(dq, win_ref[0], 1, 1) + dot(dk, win_ref[1], 1, 1) + dot(dv, win_ref[2], 1, 1)
        dx, a, b = norm_back(xh, r, dn, gain)
        dgain, dshift = dgain + a, dshift + b
        dx_ref[0, 0, g * G : (g + 1) * G] = (d1 + dx).reshape(G, WIN, D).astype(BF)
        dqs.append(dq), dks.append(dk), dvs.append(dv), d1s.append(d1b)
        os.append(o_ref[0, 0, g * G : (g + 1) * G].astype(F32).reshape(G * WIN, D).astype(BF))
    n1 = jnp.concatenate(n1s, axis=0)
    for i, part in enumerate((dqs, dks, dvs)):
        dwin_ref[i] = dwin_ref[i] + dot(n1, jnp.concatenate(part, axis=0), 0, 0)
    dwout_ref[...] = dwout_ref[...] + dot(jnp.concatenate(os, axis=0), jnp.concatenate(d1s, axis=0), 0, 0)
    dgs_ref[0:1, :] = dgs_ref[0:1, :] + dgain
    dgs_ref[1:2, :] = dgs_ref[1:2, :] + dshift

    @pl.when(step == last)
    def _():
        vec = dgs_ref[...] + dgsc_ref[...]
        for t in range(z.nt):
            rows = slice(t * z.rows, (t + 1) * z.rows)
            g1s[t] = jnp.zeros(g1s.shape[1:], BF)
            for i in range(3):
                g1s[t, 0 : z.rows, i * D : (i + 1) * D] = dwin_ref[i, rows, :].astype(BF)
            g1s[t, 0 : z.rows, 3 * D : 4 * D] = dwout_ref[rows, :].astype(BF)
            g1s[t, z.rpad : z.rpad + 8, 0 : z.rows] = vec[:, rows].astype(BF)
        for j in range(1, z.nt):
            tile_copy(0, j).start()
        for i in (1, 2):
            tile_sum(i)
        n = z.bands * 8
        pads = jnp.zeros((WIN, 128 - WIN), F32)
        for b in range(z.bands):
            for h in range(8):
                at = (b * 8 + h) * WIN
                if h < HEADS:
                    bbuf_ref[at : at + WIN, :] = jnp.concatenate([db_ref[b, :, h * WIN : (h + 1) * WIN], pads], axis=1)
                else:
                    bbuf_ref[at : at + WIN, :] = jnp.zeros((WIN, 128), F32)
        tab = jnp.zeros((n, RELP), F32)
        for j in range(0, WIN, 2):
            both = jnp.concatenate([one_hot(idx_ref, j), one_hot(idx_ref, j + 1)], axis=1)
            pair = jnp.concatenate([bbuf_ref[pl.ds(j, n, stride=WIN), :], bbuf_ref[pl.ds(j + 1, n, stride=WIN), :]], axis=1)
            tab = tab + dot(pair.astype(BF), both, 1, 1)
        for b in range(z.bands):
            ts[:, b * RELB : (b + 1) * RELB] = tab[b * 8 : (b + 1) * 8, :RELB].astype(BF)
        for j in range(1, z.nl):
            tab_copy(j).start()
        tile_sum(0)
        two = lev_sum(1)
        oci_ref[...] = two[:, 0 : 3 * D]
        oco_ref[...] = two[:, 3 * D : 4 * D]
        oew_ref[...] = two[:, 4 * D :]
        orw_ref[...] = unfold_rows(lev_sum(2))
        total = ts[...].astype(F32)
        for j in range(1, z.nl):
            tab_copy(j).wait_recv()
            total = total + tr[j - 1].astype(F32)
        otab_ref[...] = total
        one = lev_sum(0)
        owi_ref[...] = one[0 : z.rows, 0 : 3 * D]
        owo_ref[...] = one[0 : z.rows, 3 * D : 4 * D]
        ovec_ref[...] = one[z.rpad : z.rpad + 8, 0 : z.rows]
        for i in range(3):
            for j in range(1, z.nt):
                tile_copy(i, j).wait_send()
            for j in range(1, z.nl):
                lev_copy(i, j).wait_send()
        for j in range(1, z.nl):
            tab_copy(j).wait_send()


def window_backward(z, d, x, q, k, v, p, o, win, wout, gs, idx, dcin, dcout, dew, drw, dgsc):
    S, L, W, A = z.S, z.L, z.W, HEADS * WIN
    tok = pl.BlockSpec((1, 1, W, WIN, D), lambda s, l: (s, l, 0, 0, 0))
    ins = (win, wout, gs, idx, dcin, dcout, dew, drw, dgsc)
    lanes2 = 4 * D + z.FF
    outs = ((z.rows, 3 * D), (z.rows, D), (z.rows, 3 * D), (z.rows, D), (z.rows, z.FF), (z.frows, D), (8, z.rows), (8, z.bands * RELB))
    slabs = ((z.rpad + 8, 4 * D), (z.rows, lanes2), z.fshape)
    scratch = [pltpu.VMEM((2, W * WIN, 128), F32), pltpu.VMEM((z.bands, WIN, A), F32), pltpu.VMEM((3, D, D), F32),
               pltpu.VMEM((D, D), F32), pltpu.VMEM((8, D), F32), pltpu.VMEM((z.bands * 8 * WIN, 128), F32)]
    for sh in slabs:
        scratch += [pltpu.VMEM((z.nt,) + sh, BF), pltpu.VMEM((z.nt - 1,) + sh, BF)]
    for sh in slabs:
        scratch += [pltpu.VMEM(sh, BF), pltpu.VMEM((z.nl - 1,) + sh, BF)]
    scratch += [pltpu.VMEM((8, z.bands * RELB), BF), pltpu.VMEM((z.nl - 1, 8, z.bands * RELB), BF)]
    scratch += [dma(3, z.nt - 1), dma(3, z.nt - 1), dma(3, z.nl - 1), dma(3, z.nl - 1), dma(z.nl - 1), dma(z.nl - 1)]
    return pl.pallas_call(
        functools.partial(window_backward_kernel, z),
        grid=(S, L),
        in_specs=[pl.BlockSpec((1, 1, z.nl, z.NCH, z.CB, 128), lambda s, l: (s, l, 0, 0, 0, 0)), tok, tok, tok, tok,
                  pl.BlockSpec((1, 1, W, WIN, A), lambda s, l: (s, l, 0, 0, 0)), tok] + [full_spec(*a.shape) for a in ins],
        out_specs=[tok] + [full_spec(*f) for f in outs],
        out_shape=[jax.ShapeDtypeStruct((S, L, W, WIN, D), BF)] + [jax.ShapeDtypeStruct(f, F32) for f in outs],
        scratch_shapes=scratch,
        compiler_params=pltpu.CompilerParams(vmem_limit_bytes=VMEM_LIMIT, collective_id=2, has_side_effects=True),
        name="window_backward",
    )(d, x, q, k, v, p, o, *ins)


def body(mesh, inputs, out_grad, lowest_level, bias_index, first_gain, first_shift, window_in, window_out, earth_bias,
         second_gain, second_shift, column_in, column_out, third_gain, third_shift, expand_weight, reduce_weight):
    z = Sizes(mesh, inputs, out_grad, expand_weight)
    S, W, LV = z.S, z.W, z.LV
    vec = jnp.stack([first_gain, first_shift, second_gain, second_shift, third_gain, third_shift, third_gain, third_gain])
    idx = jnp.pad(bias_index.T, ((0, 0), (0, 128 - WIN)), constant_values=-1)
    tab = jnp.pad(earth_bias.T, ((0, 2), (0, 0)))
    x1, q, k, v, p, o, win, wout, cin, cout, ew, rw, gs = window_forward(
        z, inputs, idx, tab, window_in, window_out, column_in, column_out, expand_weight, reduce_weight, vec)
    g = out_grad.transpose(0, 1, 3, 2, 4).reshape(S, LV, z.cells * W, D)
    low = lowest_level.transpose(0, 2, 1).reshape(S * z.NCH, z.C // 8, 1, 8)
    low = jnp.broadcast_to(low, (S * z.NCH, z.C // 8, HEADS * LV, 8)).reshape(S * z.NCH, z.C // 8, HEADS * LV * 8)
    i0 = lax.broadcasted_iota(jnp.int32, (LV * 8, HEADS * LV * 8), 0)
    i1 = lax.broadcasted_iota(jnp.int32, (LV * 8, HEADS * LV * 8), 1)
    key = jnp.where(i0 % 8 == i1 % 8, i0 // 8, -1)
    out, dx1, dcin, dcout, dew, drw, dgs = column(z, x1, g, low, key, cin, cout, ew, rw, gs)
    dx, gwi, gwo, gci, gco, gew, grw, gvec, gtab = window_backward(
        z, dx1, inputs, q, k, v, p, o, win, wout, gs, idx, dcin, dcout, dew, drw, dgs)
    output = out.reshape(S, LV, z.cells, W, D).transpose(0, 1, 3, 2, 4)
    return (output, dx, gvec[0], gvec[1], gwi, gwo, gtab[:HEADS].T, gvec[2], gvec[3], gci, gco, gvec[4], gvec[5], gew, grw)


def solution(mesh):
    t, t2 = P("tile"), P("tile", None)
    level_tokens = P(None, "lev", "tile", None, None)
    column_tokens = P(None, None, "tile", "lev", None)
    placed = (level_tokens, column_tokens, P(None, "tile", "lev"), P(), t, t, t2, t2, t2, t, t, t2, t2, t, t, t2, t2)
    outs = (column_tokens, level_tokens, t, t, t2, t2, t2, t, t, t2, t2, t, t, t2, t2)
    return jax.shard_map(functools.partial(body, mesh), mesh=mesh, in_specs=placed, out_specs=outs, check_vma=False)
```

```python
import functools

import jax
import jax.numpy as jnp
from jax import lax
from jax.experimental import pallas as pl
from jax.experimental.pallas import tpu as pltpu
from jax.sharding import PartitionSpec as P

HEADS = 6
HEAD_DIM = 32
D = HEADS * HEAD_DIM
WIN = 72
RELB = 828
RELP = 832
NWLON = 2
EPSILON = 1e-05
SCALE = HEAD_DIM ** (-0.5)
LOG2E = 1.4426950408889634
MASKED = -1e30
F32 = jnp.float32
BF = jnp.bfloat16
MESH = pl.DeviceIdType.MESH
VMEM_LIMIT = 60 << 20
BATCH_F, BATCH_C, BATCH_B = 8, 12, 8


def dot(a, b, ca=1, cb=0):
    return lax.dot_general(a, b, (((ca,), (cb,)), ((), ())), preferred_element_type=F32)


def lane_heads():
    lane = lax.broadcasted_iota(jnp.int32, (1, 128), 1)
    return [(lane // HEAD_DIM == h).astype(F32) for h in range(4)], [lane < HEAD_DIM * (h + 1) for h in range(3)]


def spread(v, marks, factor=None):
    n = v.shape[0]
    low, high = v[:, :128], v[:, 128:]
    tops = [m if factor is None else m * factor for m in marks]
    if n == 64:
        low, high = low.astype(BF), high.astype(BF)
        tops = [m.astype(BF) for m in tops]
        first = jnp.concatenate([low * m for m in tops], axis=0)
        return first, jnp.concatenate([high * m[:, :64] for m in tops[:2]], axis=0)
    parts = [low * m for m in tops]
    cut = 256 - 3 * n
    first = jnp.concatenate(parts[:3] + [parts[3][:cut]], axis=0).astype(BF)
    head3 = jnp.concatenate([parts[3][cut:], jnp.zeros((n - cut, 64), F32)], axis=1)
    blank = jnp.zeros((n, 128), F32)
    rest = [jnp.concatenate([blank, high * m[:, :64]], axis=1) for m in tops[:2]]
    return first, jnp.concatenate([head3] + rest, axis=0).astype(BF)


def scores(k, spread_q):
    first, rest = spread_q
    right = k[:, 128:] if rest.shape[1] == 64 else k
    return jnp.concatenate([dot(k[:, :128], first, 1, 1), dot(right, rest, 1, 1)], axis=1)


def weigh(p, spread_v):
    first, rest = spread_v
    low, high = dot(p[:, :256], first), dot(p[:, 256:], rest)
    if rest.shape[1] == 64:
        return jnp.concatenate([low, high], axis=1)
    return jnp.concatenate([low + high[:, :128], high[:, 128:]], axis=1)


def mix(p, v, bounds):
    n = v.shape[0]
    first = dot(p[:, :256], v[:, :128], 0, 0)
    if n == 64:
        rest = dot(p[:, 256:], v[:, 128:], 0, 0)
        head3, tail = first[3 * n :], rest
    else:
        rest = dot(p[:, 256:], v, 0, 0)
        cut = 4 * n - 256
        head3, tail = jnp.concatenate([first[3 * n :], rest[:cut, :128]], axis=0), rest[cut:, 128:]
    low = jnp.where(bounds[0], first[:n], jnp.where(bounds[1], first[n : 2 * n], jnp.where(bounds[2], first[2 * n : 3 * n], head3)))
    high = jnp.where(bounds[0][:, :64], tail[:n], tail[n:])
    return jnp.concatenate([low, high], axis=1)


def norm(x):
    mean = jnp.sum(x, -1, keepdims=True) * (1.0 / D)
    c = x - mean
    var = jnp.sum(c * c, -1, keepdims=True) * (1.0 / D)
    r = lax.rsqrt(var + EPSILON)
    return c * r, r


def norm_back(xh, r, dn, gain):
    t = dn * gain
    a = jnp.sum(t, -1, keepdims=True) * (1.0 / D)
    b = jnp.sum(t * xh, -1, keepdims=True) * (1.0 / D)
    return r * (t - a - xh * b), jnp.sum(dn * xh, 0, keepdims=True), jnp.sum(dn, 0, keepdims=True)


def softmax2(st):
    e = jnp.exp2(st - jnp.max(st, 0, keepdims=True))
    return e * (1.0 / jnp.sum(e, 0, keepdims=True))


def put(ref, rows, v):
    n = v.shape[0]
    ref[0, rows, :] = v[:, :128]
    ref[1, rows, :] = jnp.concatenate([v[:, 128:], jnp.zeros((n, 256 - D), F32)], axis=1)


def take(ref, rows):
    return jnp.concatenate([ref[0, rows, :], ref[1, rows, :][:, : D - 128]], axis=1)


def fold(ref, at, v):
    c = v.shape[0]
    ref[at + (slice(0, c),)] = v[:, :128].astype(BF)
    tail = jnp.concatenate([v[: c // 2, 128:], v[c // 2 :, 128:]], axis=1)
    ref[at + (slice(c, c + c // 2),)] = tail.astype(BF)


def unfold(block):
    c = block.shape[0] * 2 // 3
    wide = block.astype(F32)
    tail = wide[c:]
    return jnp.concatenate([wide[:c], jnp.concatenate([tail[:, :64], tail[:, 64:]], axis=0)], axis=1)


def one_hot(idx_ref, j):
    entry = lax.broadcasted_iota(jnp.int32, (RELP, 128), 0)
    return (entry == idx_ref[j : j + 1, :]).astype(F32).astype(BF)


def barrier(axes):
    sem = pltpu.get_barrier_semaphore()
    count = 0
    for axis, size in axes:
        me = lax.axis_index(axis)
        for j in range(1, size):
            pl.semaphore_signal(sem, inc=1, device_id={axis: lax.rem(me + j, size)}, device_id_type=MESH)
            count += 1
    pl.semaphore_wait(sem, count)


def to_peer(axis, size, j, src, dst, send, recv):
    me = lax.axis_index(axis)
    return pltpu.make_async_remote_copy(
        src_ref=src, dst_ref=dst, send_sem=send, recv_sem=recv,
        device_id={axis: lax.rem(me + j, size)}, device_id_type=MESH,
    )


def fold_rows(m):
    n = m.shape[0]
    if n % 32 == 0:
        return jnp.concatenate([m[: n // 2], m[n // 2 :]], axis=1)
    return m


def unfold_rows(m):
    if m.shape[1] == D:
        return m
    return jnp.concatenate([m[:, :D], m[:, D:]], axis=0)


class Sizes:
    def __init__(self, mesh, inputs, out_grad, expand):
        self.nl = mesh.shape["lev"]
        self.nt = mesh.shape["tile"]
        self.S, self.L, self.W = inputs.shape[:3]
        self.LV = out_grad.shape[1]
        self.cells = out_grad.shape[3]
        self.bands = self.W // NWLON
        self.rows = D // self.nt
        self.rpad = -(-self.rows // 8) * 8
        self.FF = expand.shape[1]
        self.frows = self.FF // self.nt
        self.T = 6 if self.cells % 6 == 0 else 3
        self.NCH = self.cells // self.T
        self.C = self.T * self.W
        self.CB = self.C * 3 // 2
        self.fshape = (self.frows // 2, 2 * D) if self.frows % 32 == 0 else (self.frows, D)


def lane_pad(m, width, value=0.0):
    if m.shape[1] == width:
        return m
    return jnp.concatenate([m, jnp.full((m.shape[0], width - m.shape[1]), value, F32)], axis=1)


class Sems:
    pass


def layer_kernel(z, names, *refs):
    r = Sems()
    for name, ref in zip(names, refs):
        setattr(r, name, ref)
    me_l, me_t = lax.axis_index("lev"), lax.axis_index("tile")
    S, L, LV, W, C, NCH = z.S, z.L, z.LV, z.W, z.C, z.NCH
    TOK = W * WIN
    marks, bounds = lane_heads()

    def load_x(i):
        return pltpu.make_async_copy(r.x.at[i // L, lax.rem(i, L)], r.xv.at[i], r.x_sem.at[i])

    def store_x(i):
        return pltpu.make_async_copy(r.xv.at[i], r.dx.at[i // L, lax.rem(i, L)], r.dx_sem.at[i])

    def load_g(i):
        rows = pl.ds(pl.multiple_of(lax.rem(i, NCH) * C, 16), C)
        return pltpu.make_async_copy(r.g.at[i // NCH, :, rows, :], r.gv.at[i], r.g_sem.at[i])

    def store_out(i):
        rows = pl.ds(pl.multiple_of(lax.rem(i, NCH) * C, 16), C)
        return pltpu.make_async_copy(r.gv.at[i], r.out.at[i // NCH, :, rows, :], r.out_sem.at[i])

    weights = ((r.w1s, r.w1r), (r.w2s, r.w2r), (r.w3s, r.w3r), (r.w4s, r.w4r))

    def weight_copy(i, j):
        src, dst = weights[i]
        return to_peer("tile", z.nt, j, src, dst.at[me_t], r.w_send.at[i, j - 1], r.w_recv.at[i, j - 1])

    def stream_copy(i, j):
        return to_peer("lev", z.nl, j, r.xs.at[i, lax.rem(me_l + j, z.nl)], r.x1r.at[i // L, me_l * L + lax.rem(i, L)],
                       r.s_send.at[i, j - 1], r.s_recv.at[i, j - 1])

    def stream_own(i):
        return pltpu.make_async_copy(r.xs.at[i, me_l], r.x1r.at[i // L, me_l * L + lax.rem(i, L)], r.s_own.at[i])

    def back_copy(i, j):
        return to_peer("lev", z.nl, j, r.ys.at[i, pl.ds(lax.rem(me_l + j, z.nl) * L, L)],
                       r.dxr.at[i // NCH, :, me_l, lax.rem(i, NCH)], r.b_send.at[i, j - 1], r.b_recv.at[i, j - 1])

    def back_own(i):
        return pltpu.make_async_copy(r.ys.at[i, pl.ds(me_l * L, L)], r.dxr.at[i // NCH, :, me_l, lax.rem(i, NCH)], r.b_own.at[i])

    first_stage = ((r.g1s, r.g1r), (r.g2s, r.g2r), (r.g3s, r.g3r), (r.g4s, r.g4r))
    second_stage = ((r.h1s, r.h1r), (r.h2s, r.h2r), (r.h3s, r.h3r), (r.h4s, r.h4r))

    def tile_copy(i, j):
        src, dst = first_stage[i]
        return to_peer("tile", z.nt, j, src.at[lax.rem(me_t + j, z.nt)], dst.at[j - 1], r.g_send.at[i, j - 1], r.g_recv.at[i, j - 1])

    def lev_copy(i, j):
        src, dst = second_stage[i]
        return to_peer("lev", z.nl, j, src, dst.at[j - 1], r.h_send.at[i, j - 1], r.h_recv.at[i, j - 1])

    def tab_copy(j):
        return to_peer("lev", z.nl, j, r.ts, r.tr.at[j - 1], r.t_send.at[j - 1], r.t_recv.at[j - 1])

    def tile_start(i):
        for j in range(1, z.nt):
            tile_copy(i, j).start()

    def tile_sum(i):
        src, dst = first_stage[i]
        total = src[pl.ds(me_t, 1)][0].astype(F32)
        for j in range(1, z.nt):
            tile_copy(i, j).wait_recv()
            total = total + dst[j - 1].astype(F32)
        second_stage[i][0][...] = total.astype(BF)
        for j in range(1, z.nl):
            lev_copy(i, j).start()

    def lev_sum(i):
        src, dst = second_stage[i]
        total = src[...].astype(F32)
        for j in range(1, z.nl):
            lev_copy(i, j).wait_recv()
            total = total + dst[j - 1].astype(F32)
        return total

    def weight_wait(i):
        for j in range(1, z.nt):
            weight_copy(i, j).wait_recv()

    for i in range(S * L):
        load_x(i).start()
    for i in range(S * NCH):
        load_g(i).start()
    r.w1s[...] = jnp.zeros(r.w1s.shape, BF)
    r.w1s[0 : z.rows, 0 : 3 * D] = r.wi[...]
    for i, vec in enumerate((r.v0, r.v1, r.v2, r.v3, r.v4, r.v5)):
        r.w1s[z.rpad + i : z.rpad + i + 1, 0 : z.rows] = vec[...]
    r.w2s[...] = r.wo[...]
    r.w3s[:, 0 : 3 * D] = r.ci[...]
    r.w3s[:, 3 * D : 4 * D] = r.co[...]
    r.w3s[:, 4 * D :] = r.ew[...]
    r.w4s[...] = fold_rows(r.rw[...].astype(F32)).astype(BF)
    barrier((("lev", z.nl), ("tile", z.nt)))
    for i in range(4):
        for j in range(1, z.nt):
            weight_copy(i, j).start()
    for src, dst in weights:
        dst[pl.ds(me_t, 1)] = src[...][None]
    for ref in (r.dcin, r.dcout, r.dew, r.drw, r.dwin, r.dwout, r.dgs):
        ref[...] = jnp.zeros(ref.shape, F32)
    entries = lane_pad(r.idx[...].astype(F32), 128, -1.0)
    entries = jnp.concatenate([entries, jnp.full((128 - WIN, 128), -1.0, F32)], axis=0)
    r.idxt[...] = jnp.transpose(entries).astype(jnp.int32)
    cells8 = lax.broadcasted_iota(jnp.int32, (LV * 8, HEADS * LV * 8), 0)
    lane8 = lax.broadcasted_iota(jnp.int32, (LV * 8, HEADS * LV * 8), 1)
    r.key[...] = jnp.where(cells8 % 8 == lane8 % 8, (cells8 // 8).astype(F32), -1.0)
    wrow = lax.broadcasted_iota(jnp.int32, (W, HEADS * LV * 8), 0)
    wlane = lax.broadcasted_iota(jnp.int32, (W, HEADS * LV * 8), 1)
    for half in range(W // 8):
        pick = (wrow == wlane % 8 + 8 * half).astype(F32).astype(BF)
        for s in range(S):
            r.low[s, half] = dot(r.lowest[s].astype(F32).astype(BF), pick, 0, 0)
    table = r.tab[...].astype(F32)
    pads = jnp.zeros((8 - HEADS, RELP), F32)
    table = jnp.concatenate(
        [jnp.concatenate([lane_pad(table[:, b * RELB : (b + 1) * RELB], RELP), pads], axis=0) for b in range(z.bands)], axis=0
    ).astype(BF)
    n8 = z.bands * 8
    for j in range(0, WIN, 2):
        both = jnp.concatenate([one_hot(r.idxt, j), one_hot(r.idxt, j + 1)], axis=1)
        vals = dot(table, both) * LOG2E
        r.bbuf[pl.ds(j, n8, stride=WIN), :] = vals[:, :128]
        r.bbuf[pl.ds(j + 1, n8, stride=WIN), :] = vals[:, 128:]
    for b in range(z.bands):
        r.bias[b] = jnp.concatenate(
            [r.bbuf[(b * 8 + h) * WIN : (b * 8 + h + 1) * WIN, :][:, :WIN] for h in range(HEADS)], axis=1
        )
    weight_wait(0)
    for t in range(z.nt):
        r.wide[t * z.rows : (t + 1) * z.rows, 0 : 3 * D] = r.w1r[t, 0 : z.rows, :].astype(F32)
    for i in range(3):
        r.win[i] = r.wide[:, i * D : (i + 1) * D].astype(BF)
    r.gs[...] = jnp.concatenate([r.w1r[t, z.rpad : z.rpad + 8, :].astype(F32)[:, : z.rows] for t in range(z.nt)], axis=1)
    gain1, shift1, g2, s2, g3, s3 = (r.gs[i : i + 1, :] for i in range(6))

    def window_step(i, _):
        load_x(i).wait()
        x = r.xv[i].astype(F32).reshape(TOK, D)
        xh, _ = norm(x)
        n1 = (xh * gain1 + shift1).astype(BF)
        q, k, v = (dot(n1, r.win[m]) for m in range(3))
        mixed = []
        for b0 in range(0, W, BATCH_F):
            batch = range(b0, b0 + BATCH_F)
            cut = {w: slice(w * WIN, (w + 1) * WIN) for w in batch}
            kb = {w: k[cut[w]].astype(BF) for w in batch}
            vb = {w: v[cut[w]].astype(BF) for w in batch}
            for w in batch:
                r.qv[i, w] = q[cut[w]].astype(BF)
                r.kv[i, w] = kb[w]
                r.vv[i, w] = vb[w]
            sq = {w: spread(q[cut[w]], marks, SCALE * LOG2E) for w in batch}
            st = {w: scores(kb[w], sq[w]) + r.bias[w // NWLON] for w in batch}
            pb = {w: softmax2(st[w]).astype(BF) for w in batch}
            for w in batch:
                r.pv[i, w] = pb[w]
            mixed += [mix(pb[w], vb[w], bounds) for w in batch]
        o = jnp.concatenate(mixed, axis=0).astype(BF)
        r.ov[i] = o.astype(F32).reshape(W, WIN, D).astype(BF)

        @pl.when(i == 0)
        def _():
            weight_wait(1)
            for t in range(z.nt):
                r.wide[t * z.rows : (t + 1) * z.rows, 0:D] = r.w2r[t].astype(F32)
            r.wout[...] = r.wide[:, 0:D].astype(BF)

        x1 = r.xv[i].astype(F32).reshape(TOK, D) + dot(r.ov[i].astype(F32).reshape(TOK, D).astype(BF), r.wout[...])
        for w in range(W):
            put(r.mid, pl.ds(w, WIN, stride=W), x1[w * WIN : (w + 1) * WIN])
        for d in range(z.nl):
            for c in range(NCH):
                at = (d * NCH + c) * C
                fold(r.xs, (i, d, c), take(r.mid, slice(at, at + C)))
        for j in range(1, z.nl):
            stream_copy(i, j).start()
        stream_own(i).start()
        return 0

    lax.fori_loop(0, S * L, window_step, 0)

    weight_wait(2)
    weight_wait(3)
    for t in range(z.nt):
        r.wide[t * z.rows : (t + 1) * z.rows, :] = r.w3r[t].astype(F32)
        r.widef[t * z.frows : (t + 1) * z.frows, :] = unfold_rows(r.w4r[t].astype(F32))
    for i in range(3):
        r.cin[i] = r.wide[:, i * D : (i + 1) * D].astype(BF)
    r.cout[...] = r.wide[:, 3 * D : 4 * D].astype(BF)
    r.ewf[...] = r.wide[:, 4 * D :].astype(BF)
    r.rwf[...] = r.widef[...].astype(BF)
    r.bias[...] = jnp.zeros(r.bias.shape, F32)

    groups, R, GR = C // 8, LV * C, LV * 8
    halves = W // 8

    def cols(m, j):
        return m.reshape(LV, C, D)[:, j * 8 : (j + 1) * 8, :].reshape(GR, D)

    def join(parts):
        return jnp.concatenate([p.reshape(LV, 8, D) for p in parts], axis=1).reshape(R, D)

    def column_step(i, _):
        s, ch = i // NCH, lax.rem(i, NCH)

        @pl.when(ch == 0)
        def _():
            for l in range(L):
                stream_own(s * L + l).wait()
                for j in range(1, z.nl):
                    stream_copy(s * L + l, j).wait_recv()

        x1 = jnp.concatenate([unfold(r.x1r[s, m, ch]) for m in range(LV)], axis=0)
        xh2, r2 = norm(x1)
        n2 = (xh2 * g2 + s2).astype(BF)
        q, k, v = (dot(n2, r.cin[m]) for m in range(3))
        key = r.key[...]
        mixed = []
        qb, kb, vb, pb = {}, {}, {}, {}
        for b0 in range(0, groups, BATCH_C):
            batch = range(b0, min(b0 + BATCH_C, groups))
            for j in batch:
                kb[j], vb[j] = cols(k, j).astype(BF), cols(v, j).astype(BF)
                qb[j] = spread(cols(q, j), marks, SCALE * LOG2E)
            st = {j: scores(kb[j], qb[j]) for j in batch}
            for j in batch:
                low = r.low[s, j % halves, pl.ds(ch * z.T + j // halves, 1), :]
                pb[j] = softmax2(jnp.where(key >= low, st[j], MASKED)).astype(BF)
            mixed += [mix(pb[j], vb[j], bounds) for j in batch]
        o2 = join(mixed).astype(BF)
        x2 = x1 + dot(o2, r.cout[...])
        xh3, r3 = norm(x2)
        n3 = (xh3 * g3 + s3).astype(BF)
        load_g(i).wait()
        gb = r.gv[i].astype(F32).reshape(R, D).astype(BF)
        u = dot(n3, r.ewf[...] * 0.5)
        dh = dot(gb, r.rwf[...] * 0.5, 1, 1)
        c = 0.7978845608028654
        a = 2 * c + (8 * c * 0.044715) * (u * u)
        t = jnp.tanh(u * a)
        up = 1.0 + t
        hid = u * up
        du = (dh * (up + hid * (1.0 - t) * (3.0 * a - 4.0 * c))).astype(BF)
        hid = hid.astype(BF)
        r.gv[i] = (x2 + dot(hid, r.rwf[...])).reshape(LV, C, D).astype(BF)
        store_out(i).start()
        r.drw[...] = r.drw[...] + dot(hid, gb, 0, 0)
        r.dew[...] = r.dew[...] + dot(n3, du, 0, 0)
        dn3 = dot(du, r.ewf[...], 1, 1)
        dx, a3, b3 = norm_back(xh3, r3, dn3, g3)
        dx2 = gb.astype(F32) + dx
        dx2b = dx2.astype(BF)
        r.dcout[...] = r.dcout[...] + dot(o2, dx2b, 0, 0)
        do = dot(dx2b, r.cout[...], 1, 1)
        dq, dk, dv = [], [], []
        for b0 in range(0, groups, BATCH_C):
            batch = range(b0, min(b0 + BATCH_C, groups))
            dob = {j: spread(cols(do, j), marks) for j in batch}
            dpt = {j: scores(vb[j], dob[j]) for j in batch}
            dv += [weigh(pb[j], dob[j]) for j in batch]
            dsb = {}
            for j in batch:
                pf = pb[j].astype(F32)
                dsb[j] = (pf * (dpt[j] - jnp.sum(dpt[j] * pf, 0, keepdims=True))).astype(BF)
            dk += [weigh(dsb[j], qb[j]) * (1.0 / LOG2E) for j in batch]
            dq += [mix(dsb[j], kb[j], bounds) * SCALE for j in batch]
        dn2 = 0.0
        for m, part in enumerate((dq, dk, dv)):
            pack = join(part).astype(BF)
            r.dcin[m] = r.dcin[m] + dot(n2, pack, 0, 0)
            dn2 = dn2 + dot(pack, r.cin[m], 1, 1)
        dx, a2, b2 = norm_back(xh2, r2, dn2, g2)
        dx1 = dx2 + dx
        for m in range(LV):
            fold(r.ys, (i, m), dx1[m * C : (m + 1) * C])
        for m, part in enumerate((a2, b2, a3, b3)):
            r.dgs[m + 2 : m + 3, :] = r.dgs[m + 2 : m + 3, :] + part
        for j in range(1, z.nl):
            back_copy(i, j).start()
        back_own(i).start()
        return 0

    lax.fori_loop(0, S * NCH, column_step, 0)

    for t in range(z.nt):
        rows = slice(t * z.rows, (t + 1) * z.rows)
        for i in range(3):
            r.g2s[t, :, i * D : (i + 1) * D] = r.dcin[i, rows, :].astype(BF)
        r.g2s[t, :, 3 * D : 4 * D] = r.dcout[rows, :].astype(BF)
        r.g2s[t, :, 4 * D :] = r.dew[rows, :].astype(BF)
        r.g3s[t] = fold_rows(r.drw[t * z.frows : (t + 1) * z.frows, :]).astype(BF)
    tile_start(1)
    tile_start(2)

    def back_step(i, _):
        s, l = i // L, lax.rem(i, L)

        @pl.when(l == 0)
        def _():
            for c in range(NCH):
                back_own(s * NCH + c).wait()
                for j in range(1, z.nl):
                    back_copy(s * NCH + c, j).wait_recv()

        for d in range(z.nl):
            for c in range(NCH):
                at = (d * NCH + c) * C
                put(r.mid, slice(at, at + C), unfold(r.dxr[s, l, d, c]))
        n1s, dqs, dks, dvs, d1s, os = [], [], [], [], [], []
        for b0 in range(0, W, BATCH_B):
            batch = range(b0, b0 + BATCH_B)
            d1 = jnp.concatenate([take(r.mid, pl.ds(w, WIN, stride=W)) for w in batch], axis=0)
            d1b = d1.astype(BF)
            do = dot(d1b, r.wout[...], 1, 1)
            dob = {w: spread(do[(w - b0) * WIN : (w - b0 + 1) * WIN], marks) for w in batch}
            qb = {w: spread(r.qv[i, w].astype(F32), marks) for w in batch}
            dpt = {w: scores(r.vv[i, w], dob[w]) for w in batch}
            dv = [weigh(r.pv[i, w], dob[w]) for w in batch]
            dsb = {}
            for w in batch:
                pf = r.pv[i, w].astype(F32)
                ds = pf * (dpt[w] - jnp.sum(dpt[w] * pf, 0, keepdims=True))
                dsb[w] = ds.astype(BF)
                r.bias[w // NWLON] = r.bias[w // NWLON] + ds
            dk = [weigh(dsb[w], qb[w]) * SCALE for w in batch]
            dq = [mix(dsb[w], r.kv[i, w], bounds) * SCALE for w in batch]
            x = r.xv[i, b0 : b0 + BATCH_B].astype(F32).reshape(BATCH_B * WIN, D)
            n1s.append((norm(x)[0] * gain1 + shift1).astype(BF))
            os.append(r.ov[i, b0 : b0 + BATCH_B].astype(F32).reshape(BATCH_B * WIN, D).astype(BF))
            r.ov[i, b0 : b0 + BATCH_B] = d1.reshape(BATCH_B, WIN, D).astype(BF)
            d1s.append(d1b)
            for part, parts, keep in ((dq, dqs, r.qv), (dk, dks, r.kv), (dv, dvs, r.vv)):
                flat = jnp.concatenate(part, axis=0)
                keep[i, b0 : b0 + BATCH_B] = flat.reshape(BATCH_B, WIN, D).astype(BF)
                parts.append(flat.astype(BF))
        n1 = jnp.concatenate(n1s, axis=0)
        for m, part in enumerate((dqs, dks, dvs)):
            r.dwin[m] = r.dwin[m] + dot(n1, jnp.concatenate(part, axis=0), 0, 0)
        r.dwout[...] = r.dwout[...] + dot(jnp.concatenate(os, axis=0), jnp.concatenate(d1s, axis=0), 0, 0)
        return 0

    lax.fori_loop(0, S * L, back_step, 0)

    for t in range(z.nt):
        rows = slice(t * z.rows, (t + 1) * z.rows)
        for i in range(3):
            r.g1s[t, :, i * D : (i + 1) * D] = r.dwin[i, rows, :].astype(BF)
        r.g1s[t, :, 3 * D : 4 * D] = r.dwout[rows, :].astype(BF)
    tile_start(0)
    tile_sum(1)
    tile_sum(2)

    pads = jnp.zeros((WIN, 128 - WIN), F32)
    for b in range(z.bands):
        for h in range(8):
            at = (b * 8 + h) * WIN
            if h < HEADS:
                r.bbuf[at : at + WIN, :] = jnp.concatenate([r.bias[b, :, h * WIN : (h + 1) * WIN], pads], axis=1)
            else:
                r.bbuf[at : at + WIN, :] = jnp.zeros((WIN, 128), F32)
    tab = jnp.zeros((n8, RELP), F32)
    for j in range(0, WIN, 2):
        both = jnp.concatenate([one_hot(r.idxt, j), one_hot(r.idxt, j + 1)], axis=1)
        pair = jnp.concatenate([r.bbuf[pl.ds(j, n8, stride=WIN), :], r.bbuf[pl.ds(j + 1, n8, stride=WIN), :]], axis=1)
        tab = tab + dot(pair.astype(BF), both, 1, 1)
    for b in range(z.bands):
        r.ts[:, b * RELB : (b + 1) * RELB] = tab[b * 8 : (b + 1) * 8, :RELB].astype(BF)
    for j in range(1, z.nl):
        tab_copy(j).start()

    def norm_step(i, _):
        x = r.xv[i].astype(F32).reshape(TOK, D)
        xh, rs = norm(x)
        dn = 0.0
        for m, kept in enumerate((r.qv, r.kv, r.vv)):
            dn = dn + dot(kept[i].astype(F32).reshape(TOK, D).astype(BF), r.win[m], 1, 1)
        dx, a, b = norm_back(xh, rs, dn, gain1)
        r.xv[i] = (r.ov[i].astype(F32).reshape(TOK, D) + dx).reshape(W, WIN, D).astype(BF)
        store_x(i).start()
        r.dgs[0:1, :] = r.dgs[0:1, :] + a
        r.dgs[1:2, :] = r.dgs[1:2, :] + b
        return 0

    lax.fori_loop(0, S * L, norm_step, 0)

    for t in range(z.nt):
        r.g4s[t] = lane_pad(r.dgs[:, t * z.rows : (t + 1) * z.rows], 128).astype(BF)
    tile_start(3)
    tile_sum(0)
    two = lev_sum(1)
    r.oci[...] = two[:, 0 : 3 * D]
    r.oco[...] = two[:, 3 * D : 4 * D]
    r.oew[...] = two[:, 4 * D :]
    r.orw[...] = unfold_rows(lev_sum(2))
    tile_sum(3)
    total = r.ts[...].astype(F32)
    for j in range(1, z.nl):
        tab_copy(j).wait_recv()
        total = total + r.tr[j - 1].astype(F32)
    r.otab[...] = total[:HEADS]
    one = lev_sum(0)
    r.owi[...] = one[:, 0 : 3 * D]
    r.owo[...] = one[:, 3 * D : 4 * D]
    vec = lev_sum(3)
    for i, ref in enumerate((r.o0, r.o1, r.o2, r.o3, r.o4, r.o5)):
        ref[...] = vec[i : i + 1, 0 : z.rows]
    for i in range(4):
        for j in range(1, z.nt):
            weight_copy(i, j).wait_send()
            tile_copy(i, j).wait_send()
        for j in range(1, z.nl):
            lev_copy(i, j).wait_send()
    for j in range(1, z.nl):
        tab_copy(j).wait_send()
        for i in range(S * L):
            stream_copy(i, j).wait_send()
        for i in range(S * NCH):
            back_copy(i, j).wait_send()
    for i in range(S * L):
        store_x(i).wait()
    for i in range(S * NCH):
        store_out(i).wait()


def dma(*shape):
    return pltpu.SemaphoreType.DMA(shape)


def body(mesh, inputs, out_grad, lowest_level, bias_index, first_gain, first_shift, window_in, window_out, earth_bias,
         second_gain, second_shift, column_in, column_out, third_gain, third_shift, expand_weight, reduce_weight):
    z = Sizes(mesh, inputs, out_grad, expand_weight)
    S, L, LV, W, C, CB, NCH, A, FF, nt, nl = z.S, z.L, z.LV, z.W, z.C, z.CB, z.NCH, HEADS * WIN, z.FF, z.nt, z.nl
    lanes = 4 * D + FF
    tab_lanes = z.bands * RELB
    g = out_grad.transpose(0, 1, 3, 2, 4).reshape(S, LV, z.cells * W, D)
    row = lambda a: a.reshape(1, z.rows)
    ins = dict(x=inputs, g=g, lowest=lowest_level, idx=bias_index, tab=earth_bias.T, wi=window_in, wo=window_out,
               ci=column_in, co=column_out, ew=expand_weight, rw=reduce_weight, v0=row(first_gain), v1=row(first_shift),
               v2=row(second_gain), v3=row(second_shift), v4=row(third_gain), v5=row(third_shift))
    outs = dict(out=(g.shape, BF), dx=(inputs.shape, BF), owi=((z.rows, 3 * D), F32), owo=((z.rows, D), F32),
                oci=((z.rows, 3 * D), F32), oco=((z.rows, D), F32), oew=((z.rows, FF), F32), orw=((z.frows, D), F32),
                otab=((HEADS, tab_lanes), F32), **{f"o{i}": ((1, z.rows), F32) for i in range(6)})
    tokens = pltpu.VMEM((S * L, W, WIN, D), BF)
    slabs = ((z.rpad + 8, 3 * D), (z.rows, D), (z.rows, lanes), z.fshape)
    sums = ((z.rows, 4 * D), (z.rows, lanes), z.fshape, (8, 128))
    scratch = dict(xv=tokens, qv=tokens, kv=tokens, vv=tokens, ov=tokens, pv=pltpu.VMEM((S * L, W, WIN, A), BF),
                   gv=pltpu.VMEM((S * NCH, LV, C, D), BF), xs=pltpu.VMEM((S * L, nl, NCH, CB, 128), BF),
                   x1r=pltpu.VMEM((S, LV, NCH, CB, 128), BF), ys=pltpu.VMEM((S * NCH, LV, CB, 128), BF),
                   dxr=pltpu.VMEM((S, L, nl, NCH, CB, 128), BF), mid=pltpu.VMEM((2, W * WIN, 128), F32),
                   bias=pltpu.VMEM((z.bands, WIN, A), F32), bbuf=pltpu.VMEM((z.bands * 8 * WIN, 128), F32),
                   idxt=pltpu.VMEM((128, 128), jnp.int32), key=pltpu.VMEM((LV * 8, HEADS * LV * 8), F32),
                   low=pltpu.VMEM((S, W // 8, z.cells, HEADS * LV * 8), F32),
                   wide=pltpu.VMEM((D, lanes), F32), widef=pltpu.VMEM((FF, D), F32), gs=pltpu.VMEM((8, D), F32),
                   win=pltpu.VMEM((3, D, D), BF), wout=pltpu.VMEM((D, D), BF), cin=pltpu.VMEM((3, D, D), BF),
                   cout=pltpu.VMEM((D, D), BF), ewf=pltpu.VMEM((D, FF), BF), rwf=pltpu.VMEM((FF, D), BF),
                   dwin=pltpu.VMEM((3, D, D), F32), dwout=pltpu.VMEM((D, D), F32), dcin=pltpu.VMEM((3, D, D), F32),
                   dcout=pltpu.VMEM((D, D), F32), dew=pltpu.VMEM((D, FF), F32), drw=pltpu.VMEM((FF, D), F32), dgs=pltpu.VMEM((8, D), F32),
                   ts=pltpu.VMEM((8, tab_lanes), BF), tr=pltpu.VMEM((nl - 1, 8, tab_lanes), BF))
    for i, sh in enumerate(slabs):
        scratch.update({f"w{i + 1}s": pltpu.VMEM(sh, BF), f"w{i + 1}r": pltpu.VMEM((nt,) + sh, BF)})
    for i, sh in enumerate(sums):
        scratch.update({f"g{i + 1}s": pltpu.VMEM((nt,) + sh, BF), f"g{i + 1}r": pltpu.VMEM((nt - 1,) + sh, BF),
                        f"h{i + 1}s": pltpu.VMEM(sh, BF), f"h{i + 1}r": pltpu.VMEM((nl - 1,) + sh, BF)})
    scratch.update(x_sem=dma(S * L), dx_sem=dma(S * L), g_sem=dma(S * NCH), out_sem=dma(S * NCH), w_send=dma(4, nt - 1), w_recv=dma(4, nt - 1),
                   s_send=dma(S * L, nl - 1), s_recv=dma(S * L, nl - 1), s_own=dma(S * L),
                   b_send=dma(S * NCH, nl - 1), b_recv=dma(S * NCH, nl - 1), b_own=dma(S * NCH),
                   g_send=dma(4, nt - 1), g_recv=dma(4, nt - 1), h_send=dma(4, nl - 1), h_recv=dma(4, nl - 1),
                   t_send=dma(nl - 1), t_recv=dma(nl - 1))
    hbm = ("x", "g", "out", "dx")
    place = lambda name: pl.BlockSpec(memory_space=pl.ANY if name in hbm else pltpu.VMEM)
    done = dict(zip(outs, pl.pallas_call(
        functools.partial(layer_kernel, z, tuple(ins) + tuple(outs) + tuple(scratch)),
        in_specs=[place(name) for name in ins],
        out_specs=[place(name) for name in outs],
        out_shape=[jax.ShapeDtypeStruct(*o) for o in outs.values()],
        scratch_shapes=list(scratch.values()),
        compiler_params=pltpu.CompilerParams(vmem_limit_bytes=VMEM_LIMIT, collective_id=0, has_side_effects=True),
        name="layer",
    )(*ins.values())))
    output = done["out"].reshape(S, LV, z.cells, W, D).transpose(0, 1, 3, 2, 4)
    v = [done[f"o{i}"].reshape(z.rows) for i in range(6)]
    return (output, done["dx"], v[0], v[1], done["owi"], done["owo"], done["otab"].T, v[2], v[3],
            done["oci"], done["oco"], v[4], v[5], done["oew"], done["orw"])


def solution(mesh):
    t, t2 = P("tile"), P("tile", None)
    level_tokens = P(None, "lev", "tile", None, None)
    column_tokens = P(None, None, "tile", "lev", None)
    placed = (level_tokens, column_tokens, P(None, "tile", "lev"), P(), t, t, t2, t2, t2, t, t, t2, t2, t, t, t2, t2)
    outs = (column_tokens, level_tokens, t, t, t2, t2, t2, t, t, t2, t2, t, t, t2, t2)
    return jax.shard_map(functools.partial(body, mesh), mesh=mesh, in_specs=placed, out_specs=outs, check_vma=False)
```

```python
import functools

import jax
import jax.numpy as jnp
from jax import lax
from jax.experimental import pallas as pl
from jax.experimental.pallas import tpu as pltpu
from jax.sharding import PartitionSpec as P

HEADS = 6
HEAD_DIM = 32
D = HEADS * HEAD_DIM
WIN = 72
RELB = 828
RELP = 832
NWLON = 2
EPSILON = 1e-05
SCALE = HEAD_DIM ** (-0.5)
LOG2E = 1.4426950408889634
MASKED = -1e30
F32 = jnp.float32
BF = jnp.bfloat16
MESH = pl.DeviceIdType.MESH
VMEM_LIMIT = 60 << 20
BATCH_F, BATCH_C, BATCH_B = 8, 12, 8


def dot(a, b, ca=1, cb=0):
    return lax.dot_general(a, b, (((ca,), (cb,)), ((), ())), preferred_element_type=F32)


def lane_heads():
    lane = lax.broadcasted_iota(jnp.int32, (1, 128), 1)
    return [(lane // HEAD_DIM == h).astype(F32) for h in range(4)], [lane < HEAD_DIM * (h + 1) for h in range(3)]


def spread(v, marks, factor=None):
    n = v.shape[0]
    low, high = v[:, :128], v[:, 128:]
    tops = [m if factor is None else m * factor for m in marks]
    if n == 64:
        low, high = low.astype(BF), high.astype(BF)
        tops = [m.astype(BF) for m in tops]
        first = jnp.concatenate([low * m for m in tops], axis=0)
        return first, jnp.concatenate([high * m[:, :64] for m in tops[:2]], axis=0)
    parts = [low * m for m in tops]
    cut = 256 - 3 * n
    first = jnp.concatenate(parts[:3] + [parts[3][:cut]], axis=0).astype(BF)
    head3 = jnp.concatenate([parts[3][cut:], jnp.zeros((n - cut, 64), F32)], axis=1)
    blank = jnp.zeros((n, 128), F32)
    rest = [jnp.concatenate([blank, high * m[:, :64]], axis=1) for m in tops[:2]]
    return first, jnp.concatenate([head3] + rest, axis=0).astype(BF)


def scores(k, spread_q):
    first, rest = spread_q
    right = k[:, 128:] if rest.shape[1] == 64 else k
    return jnp.concatenate([dot(k[:, :128], first, 1, 1), dot(right, rest, 1, 1)], axis=1)


def weigh(p, spread_v):
    first, rest = spread_v
    low, high = dot(p[:, :256], first), dot(p[:, 256:], rest)
    if rest.shape[1] == 64:
        return jnp.concatenate([low, high], axis=1)
    return jnp.concatenate([low + high[:, :128], high[:, 128:]], axis=1)


def mix(p, v, bounds):
    n = v.shape[0]
    first = dot(p[:, :256], v[:, :128], 0, 0)
    if n == 64:
        rest = dot(p[:, 256:], v[:, 128:], 0, 0)
        head3, tail = first[3 * n :], rest
    else:
        rest = dot(p[:, 256:], v, 0, 0)
        cut = 4 * n - 256
        head3, tail = jnp.concatenate([first[3 * n :], rest[:cut, :128]], axis=0), rest[cut:, 128:]
    low = jnp.where(bounds[0], first[:n], jnp.where(bounds[1], first[n : 2 * n], jnp.where(bounds[2], first[2 * n : 3 * n], head3)))
    high = jnp.where(bounds[0][:, :64], tail[:n], tail[n:])
    return jnp.concatenate([low, high], axis=1)


def norm(x):
    mean = jnp.sum(x, -1, keepdims=True) * (1.0 / D)
    c = x - mean
    var = jnp.sum(c * c, -1, keepdims=True) * (1.0 / D)
    r = lax.rsqrt(var + EPSILON)
    return c * r, r


def norm_back(xh, r, dn, gain):
    t = dn * gain
    a = jnp.sum(t, -1, keepdims=True) * (1.0 / D)
    b = jnp.sum(t * xh, -1, keepdims=True) * (1.0 / D)
    return r * (t - a - xh * b), jnp.sum(dn * xh, 0, keepdims=True), jnp.sum(dn, 0, keepdims=True)


def softmax2(st):
    e = jnp.exp2(st - jnp.max(st, 0, keepdims=True))
    return e * (1.0 / jnp.sum(e, 0, keepdims=True))


def put(ref, rows, v):
    n = v.shape[0]
    ref[0, rows, :] = v[:, :128]
    ref[1, rows, :] = jnp.concatenate([v[:, 128:], jnp.zeros((n, 256 - D), F32)], axis=1)


def take(ref, rows):
    return jnp.concatenate([ref[0, rows, :], ref[1, rows, :][:, : D - 128]], axis=1)


def fold(ref, at, v):
    c = v.shape[0]
    ref[at + (slice(0, c),)] = v[:, :128].astype(BF)
    tail = jnp.concatenate([v[: c // 2, 128:], v[c // 2 :, 128:]], axis=1)
    ref[at + (slice(c, c + c // 2),)] = tail.astype(BF)


def unfold(block):
    c = block.shape[0] * 2 // 3
    wide = block.astype(F32)
    tail = wide[c:]
    return jnp.concatenate([wide[:c], jnp.concatenate([tail[:, :64], tail[:, 64:]], axis=0)], axis=1)


def one_hot(idx_ref, j):
    entry = lax.broadcasted_iota(jnp.int32, (RELP, 128), 0)
    return (entry == idx_ref[j : j + 1, :]).astype(F32).astype(BF)


def barrier(axes):
    sem = pltpu.get_barrier_semaphore()
    count = 0
    for axis, size in axes:
        me = lax.axis_index(axis)
        for j in range(1, size):
            pl.semaphore_signal(sem, inc=1, device_id={axis: lax.rem(me + j, size)}, device_id_type=MESH)
            count += 1
    pl.semaphore_wait(sem, count)


def to_peer(axis, size, j, src, dst, send, recv):
    me = lax.axis_index(axis)
    return pltpu.make_async_remote_copy(
        src_ref=src, dst_ref=dst, send_sem=send, recv_sem=recv,
        device_id={axis: lax.rem(me + j, size)}, device_id_type=MESH,
    )


def rows_to_lanes(m, n):
    return jnp.concatenate([m[i : i + n] for i in range(0, m.shape[0], n)], axis=1)


class Sizes:
    def __init__(self, mesh, inputs, out_grad, expand):
        self.nl = mesh.shape["lev"]
        self.nt = mesh.shape["tile"]
        self.S, self.L, self.W = inputs.shape[:3]
        self.LV = out_grad.shape[1]
        self.cells = out_grad.shape[3]
        self.bands = self.W // NWLON
        self.rows = D // self.nt
        self.rpad = -(-self.rows // 8) * 8
        self.FF = expand.shape[1]
        self.frows = self.FF // self.nt
        self.T = 6 if self.cells % 6 == 0 else 3
        self.NCH = self.cells // self.T
        self.C = self.T * self.W
        self.CB = self.C * 3 // 2


def lane_pad(m, width, value=0.0):
    if m.shape[1] == width:
        return m
    return jnp.concatenate([m, jnp.full((m.shape[0], width - m.shape[1]), value, F32)], axis=1)


class Sems:
    pass


def layer_kernel(z, names, *refs):
    r = Sems()
    for name, ref in zip(names, refs):
        setattr(r, name, ref)
    me_l, me_t = lax.axis_index("lev"), lax.axis_index("tile")
    S, L, LV, W, C, NCH = z.S, z.L, z.LV, z.W, z.C, z.NCH
    TOK = W * WIN
    marks, bounds = lane_heads()

    def load_x(i):
        return pltpu.make_async_copy(r.x.at[i // L, lax.rem(i, L)], r.xv.at[i], r.x_sem.at[i])

    def store_x(i):
        return pltpu.make_async_copy(r.xv.at[i], r.dx.at[i // L, lax.rem(i, L)], r.dx_sem.at[i])

    def load_g(i):
        rows = pl.ds(pl.multiple_of(lax.rem(i, NCH) * C, 16), C)
        return pltpu.make_async_copy(r.g.at[i // NCH, :, rows, :], r.gv.at[i], r.g_sem.at[i])

    def store_out(i):
        rows = pl.ds(pl.multiple_of(lax.rem(i, NCH) * C, 16), C)
        return pltpu.make_async_copy(r.gv.at[i], r.out.at[i // NCH, :, rows, :], r.out_sem.at[i])

    core, twin = lax.rem(me_l, 2), me_l + 1 - 2 * lax.rem(me_l, 2)

    def to_twin(src, dst, send, recv):
        return pltpu.make_async_remote_copy(src_ref=src, dst_ref=dst, send_sem=send, recv_sem=recv,
                                            device_id={"lev": twin}, device_id_type=MESH)

    def half(ref, which):
        width = ref.shape[-1] // 2
        return ref.at[:, :, pl.ds(pl.multiple_of(which * width, 128), width)]

    weights = ((r.w1s, r.w1r), (r.w2s, r.w2r))

    def weight_copy(i, j):
        src, dst = weights[i]
        return to_peer("tile", z.nt, j, half(src, core).at[0], half(dst, core).at[me_t], r.w_send.at[i, j - 1], r.w_recv.at[i, j - 1])

    def weight_pass(i):
        part = half(weights[i][1], core)
        return to_twin(part, part, r.wt_send.at[i], r.wt_recv.at[i])

    def weight_start(i):
        for j in range(1, z.nt):
            weight_copy(i, j).start()
        src, dst = weights[i]
        width = src.shape[-1] // 2
        own = pl.ds(pl.multiple_of(core * width, 128), width)
        dst[pl.ds(me_t, 1), :, own] = src[:, :, own]

    def weight_hand(i):
        for j in range(1, z.nt):
            weight_copy(i, j).wait_recv()
        weight_pass(i).start()

    def stream_copy(i, j):
        return to_peer("lev", z.nl, j, r.xs.at[i, lax.rem(me_l + j, z.nl)], r.x1r.at[i // L, me_l * L + lax.rem(i, L)],
                       r.s_send.at[i, j - 1], r.s_recv.at[i, j - 1])

    def stream_own(i):
        return pltpu.make_async_copy(r.xs.at[i, me_l], r.x1r.at[i // L, me_l * L + lax.rem(i, L)], r.s_own.at[i])

    def back_copy(i, j):
        return to_peer("lev", z.nl, j, r.ys.at[i, pl.ds(lax.rem(me_l + j, z.nl) * L, L)],
                       r.dxr.at[i // NCH, :, me_l, lax.rem(i, NCH)], r.b_send.at[i, j - 1], r.b_recv.at[i, j - 1])

    def back_own(i):
        return pltpu.make_async_copy(r.ys.at[i, pl.ds(me_l * L, L)], r.dxr.at[i // NCH, :, me_l, lax.rem(i, NCH)], r.b_own.at[i])

    grads = ((r.g1s, r.g1t, r.g1h, r.g1r, r.h1s, r.h1r, r.k1), (r.g2s, r.g2t, r.g2h, r.g2r, r.h2s, r.h2r, r.k2))

    def core_copy(i):
        return to_twin(half(grads[i][0], 1 - core), grads[i][1], r.gt_send.at[i], r.gt_recv.at[i])

    def tile_copy(i, j):
        src, dst = grads[i][2], grads[i][3]
        return to_peer("tile", z.nt, j, src.at[lax.rem(me_t + j, z.nt)], dst.at[j - 1], r.g_send.at[i, j - 1], r.g_recv.at[i, j - 1])

    def chip_copy(i, j):
        return to_peer("lev", z.nl, 2 * j, grads[i][4], grads[i][5].at[j - 1], r.h_send.at[i, j - 1], r.h_recv.at[i, j - 1])

    def join_copy(i):
        part = half(grads[i][6], core)
        return to_twin(part, part, r.k_send.at[i], r.k_recv.at[i])

    def sum_cores(i):
        core_copy(i).wait_recv()
        gs, gt, gh = grads[i][:3]
        width = gt.shape[-1]
        mine = gs[:, :, pl.ds(pl.multiple_of(core * width, 128), width)]
        gh[...] = (mine.astype(F32) + gt[...].astype(F32)).astype(BF)
        for j in range(1, z.nt):
            tile_copy(i, j).start()

    def sum_tiles(i):
        gh, gr, hs = grads[i][2:5]
        total = gh[pl.ds(me_t, 1)][0].astype(F32)
        for j in range(1, z.nt):
            tile_copy(i, j).wait_recv()
            total = total + gr[j - 1].astype(F32)
        hs[...] = total.astype(BF)
        for j in range(1, z.nl // 2):
            chip_copy(i, j).start()

    def sum_chips(i):
        hs, hr, k = grads[i][4:]
        total = hs[...].astype(F32)
        for j in range(1, z.nl // 2):
            chip_copy(i, j).wait_recv()
            total = total + hr[j - 1].astype(F32)
        width = hs.shape[-1]
        k[:, :, pl.ds(pl.multiple_of(core * width, 128), width)] = total.astype(BF)[None]
        join_copy(i).start()

    def tab_copy(j):
        return to_peer("lev", z.nl, j, r.ts, r.tr.at[j - 1], r.t_send.at[j - 1], r.t_recv.at[j - 1])

    def norm_tile_copy(j):
        return to_peer("tile", z.nt, j, r.g3s.at[lax.rem(me_t + j, z.nt)], r.g3r.at[j - 1], r.n_send.at[j - 1], r.n_recv.at[j - 1])

    def norm_lev_copy(j):
        return to_peer("lev", z.nl, j, r.h3s, r.h3r.at[j - 1], r.m_send.at[j - 1], r.m_recv.at[j - 1])

    for i in range(S * L):
        load_x(i).start()
    for i in range(S * NCH):
        load_g(i).start()
    r.w1s[...] = jnp.zeros(r.w1s.shape, BF)
    r.w1s[0, 0 : z.rows, 0 : 3 * D] = r.wi[...]
    r.w1s[0, 0 : z.rows, 3 * D : 4 * D] = r.wo[...]
    for i, vec in enumerate((r.v0, r.v1, r.v2, r.v3, r.v4, r.v5)):
        r.w1s[0, z.rpad + i : z.rpad + i + 1, 0 : z.rows] = vec[...]
    r.w2s[0, :, 0 : 3 * D] = r.ci[...]
    r.w2s[0, :, 3 * D : 4 * D] = r.co[...]
    r.w2s[0, :, 4 * D : 4 * D + z.FF] = r.ew[...]
    r.w2s[0, :, 4 * D + z.FF :] = rows_to_lanes(r.rw[...].astype(F32), z.rows).astype(BF)
    barrier((("lev", z.nl), ("tile", z.nt)))
    weight_start(0)
    for ref in (r.dcin, r.dcout, r.dew, r.drw, r.dwin, r.dwout, r.dgs):
        ref[...] = jnp.zeros(ref.shape, F32)
    entries = lane_pad(r.idx[...].astype(F32), 128, -1.0)
    entries = jnp.concatenate([entries, jnp.full((128 - WIN, 128), -1.0, F32)], axis=0)
    r.idxt[...] = jnp.transpose(entries).astype(jnp.int32)
    cells8 = lax.broadcasted_iota(jnp.int32, (LV * 8, HEADS * LV * 8), 0)
    lane8 = lax.broadcasted_iota(jnp.int32, (LV * 8, HEADS * LV * 8), 1)
    r.key[...] = jnp.where(cells8 % 8 == lane8 % 8, (cells8 // 8).astype(F32), -1.0)
    wrow = lax.broadcasted_iota(jnp.int32, (W, HEADS * LV * 8), 0)
    wlane = lax.broadcasted_iota(jnp.int32, (W, HEADS * LV * 8), 1)
    for part in range(W // 8):
        pick = (wrow == wlane % 8 + 8 * part).astype(F32).astype(BF)
        for s in range(S):
            r.low[s, part] = dot(r.lowest[s].astype(F32).astype(BF), pick, 0, 0)
    table = r.tab[...].astype(F32)
    pads = jnp.zeros((8 - HEADS, RELP), F32)
    table = jnp.concatenate(
        [jnp.concatenate([lane_pad(table[:, b * RELB : (b + 1) * RELB], RELP), pads], axis=0) for b in range(z.bands)], axis=0
    ).astype(BF)
    n8 = z.bands * 8
    for j in range(0, WIN, 2):
        both = jnp.concatenate([one_hot(r.idxt, j), one_hot(r.idxt, j + 1)], axis=1)
        vals = dot(table, both) * LOG2E
        r.bbuf[pl.ds(j, n8, stride=WIN), :] = vals[:, :128]
        r.bbuf[pl.ds(j + 1, n8, stride=WIN), :] = vals[:, 128:]
    for b in range(z.bands):
        r.bias[b] = jnp.concatenate(
            [r.bbuf[(b * 8 + h) * WIN : (b * 8 + h + 1) * WIN, :][:, :WIN] for h in range(HEADS)], axis=1
        )
    weight_hand(0)
    weight_start(1)
    weight_pass(0).wait_recv()
    for t in range(z.nt):
        r.wide[t * z.rows : (t + 1) * z.rows, 0 : 4 * D] = r.w1r[t, 0 : z.rows, :].astype(F32)
    for i in range(3):
        r.win[i] = r.wide[:, i * D : (i + 1) * D].astype(BF)
    r.wout[...] = r.wide[:, 3 * D : 4 * D].astype(BF)
    r.gs[...] = jnp.concatenate([r.w1r[t, z.rpad : z.rpad + 8, :].astype(F32)[:, : z.rows] for t in range(z.nt)], axis=1)
    gain1, shift1, g2, s2, g3, s3 = (r.gs[i : i + 1, :] for i in range(6))

    def window_step(i, _):
        load_x(i).wait()
        x = r.xv[i].astype(F32).reshape(TOK, D)
        xh, _ = norm(x)
        n1 = (xh * gain1 + shift1).astype(BF)
        q, k, v = (dot(n1, r.win[m]) for m in range(3))
        mixed = []
        for b0 in range(0, W, BATCH_F):
            batch = range(b0, b0 + BATCH_F)
            cut = {w: slice(w * WIN, (w + 1) * WIN) for w in batch}
            kb = {w: k[cut[w]].astype(BF) for w in batch}
            vb = {w: v[cut[w]].astype(BF) for w in batch}
            for w in batch:
                r.qv[i, w] = q[cut[w]].astype(BF)
                r.kv[i, w] = kb[w]
                r.vv[i, w] = vb[w]
            sq = {w: spread(q[cut[w]], marks, SCALE * LOG2E) for w in batch}
            st = {w: scores(kb[w], sq[w]) + r.bias[w // NWLON] for w in batch}
            pb = {w: softmax2(st[w]).astype(BF) for w in batch}
            for w in batch:
                r.pv[i, w] = pb[w]
            mixed += [mix(pb[w], vb[w], bounds) for w in batch]
        o = jnp.concatenate(mixed, axis=0).astype(BF)
        r.ov[i] = o.astype(F32).reshape(W, WIN, D).astype(BF)
        x1 = x + dot(o, r.wout[...])
        for w in range(W):
            put(r.mid, pl.ds(w, WIN, stride=W), x1[w * WIN : (w + 1) * WIN])
        for d in range(z.nl):
            for c in range(NCH):
                at = (d * NCH + c) * C
                fold(r.xs, (i, d, c), take(r.mid, slice(at, at + C)))
        for j in range(1, z.nl):
            stream_copy(i, j).start()
        stream_own(i).start()

        @pl.when(i == S * L - 1)
        def _():
            weight_hand(1)

        return 0

    lax.fori_loop(0, S * L, window_step, 0)

    weight_pass(1).wait_recv()
    for t in range(z.nt):
        r.wide[t * z.rows : (t + 1) * z.rows, :] = r.w2r[t].astype(F32)
        for i in range(z.FF // D):
            at = t * z.frows + i * z.rows
            r.widef[at : at + z.rows, :] = r.w2r[t].astype(F32)[:, 4 * D + z.FF + i * D : 4 * D + z.FF + (i + 1) * D]
    for i in range(3):
        r.cin[i] = r.wide[:, i * D : (i + 1) * D].astype(BF)
    r.cout[...] = r.wide[:, 3 * D : 4 * D].astype(BF)
    r.ewf[...] = r.wide[:, 4 * D : 4 * D + z.FF].astype(BF)
    r.rwf[...] = r.widef[...].astype(BF)
    r.bias[...] = jnp.zeros(r.bias.shape, F32)

    groups, R, GR = C // 8, LV * C, LV * 8
    halves = W // 8

    def cols(m, j):
        return m.reshape(LV, C, D)[:, j * 8 : (j + 1) * 8, :].reshape(GR, D)

    def join(parts):
        return jnp.concatenate([p.reshape(LV, 8, D) for p in parts], axis=1).reshape(R, D)

    def column_step(i, _):
        s, ch = i // NCH, lax.rem(i, NCH)

        @pl.when(ch == 0)
        def _():
            for l in range(L):
                stream_own(s * L + l).wait()
                for j in range(1, z.nl):
                    stream_copy(s * L + l, j).wait_recv()

        x1 = jnp.concatenate([unfold(r.x1r[s, m, ch]) for m in range(LV)], axis=0)
        xh2, r2 = norm(x1)
        n2 = (xh2 * g2 + s2).astype(BF)
        q, k, v = (dot(n2, r.cin[m]) for m in range(3))
        key = r.key[...]
        mixed = []
        qb, kb, vb, pb = {}, {}, {}, {}
        for b0 in range(0, groups, BATCH_C):
            batch = range(b0, min(b0 + BATCH_C, groups))
            for j in batch:
                kb[j], vb[j] = cols(k, j).astype(BF), cols(v, j).astype(BF)
                qb[j] = spread(cols(q, j), marks, SCALE * LOG2E)
            st = {j: scores(kb[j], qb[j]) for j in batch}
            for j in batch:
                low = r.low[s, j % halves, pl.ds(ch * z.T + j // halves, 1), :]
                pb[j] = softmax2(jnp.where(key >= low, st[j], MASKED)).astype(BF)
            mixed += [mix(pb[j], vb[j], bounds) for j in batch]
        o2 = join(mixed).astype(BF)
        x2 = x1 + dot(o2, r.cout[...])
        xh3, r3 = norm(x2)
        n3 = (xh3 * g3 + s3).astype(BF)
        load_g(i).wait()
        gb = r.gv[i].astype(F32).reshape(R, D).astype(BF)
        u = dot(n3, r.ewf[...] * 0.5).astype(BF)
        dh = dot(gb, r.rwf[...] * 0.5, 1, 1).astype(BF)
        c = 0.7978845608028654
        a = BF(2 * c) + BF(8 * c * 0.044715) * (u * u)
        t = jnp.tanh(u * a)
        up = BF(1.0) + t
        hid = u * up
        du = dh * (up + hid * (BF(1.0) - t) * (BF(3.0) * a - BF(4.0 * c)))
        dn3 = dot(du, r.ewf[...], 1, 1)
        dx, a3, b3 = norm_back(xh3, r3, dn3, g3)
        dx2 = gb.astype(F32) + dx
        dx2b = dx2.astype(BF)
        r.gv[i] = (x2 + dot(hid, r.rwf[...])).reshape(LV, C, D).astype(BF)
        store_out(i).start()
        r.drw[...] = r.drw[...] + dot(hid, gb, 0, 0)
        r.dew[...] = r.dew[...] + dot(n3, du, 0, 0)
        r.dcout[...] = r.dcout[...] + dot(o2, dx2b, 0, 0)
        do = dot(dx2b, r.cout[...], 1, 1)
        dq, dk, dv = [], [], []
        for b0 in range(0, groups, BATCH_C):
            batch = range(b0, min(b0 + BATCH_C, groups))
            dob = {j: spread(cols(do, j), marks) for j in batch}
            dpt = {j: scores(vb[j], dob[j]) for j in batch}
            dv += [weigh(pb[j], dob[j]) for j in batch]
            dsb = {}
            for j in batch:
                pf = pb[j].astype(F32)
                dsb[j] = (pf * (dpt[j] - jnp.sum(dpt[j] * pf, 0, keepdims=True))).astype(BF)
            dk += [weigh(dsb[j], qb[j]) * (1.0 / LOG2E) for j in batch]
            dq += [mix(dsb[j], kb[j], bounds) * SCALE for j in batch]
        dn2 = 0.0
        packs = [join(part).astype(BF) for part in (dq, dk, dv)]
        for m, pack in enumerate(packs):
            dn2 = dn2 + dot(pack, r.cin[m], 1, 1)
        dx, a2, b2 = norm_back(xh2, r2, dn2, g2)
        for m, pack in enumerate(packs):
            r.dcin[m] = r.dcin[m] + dot(n2, pack, 0, 0)
        dx1 = dx2 + dx
        for m in range(LV):
            fold(r.ys, (i, m), dx1[m * C : (m + 1) * C])
        for m, part in enumerate((a2, b2, a3, b3)):
            r.dgs[m + 2 : m + 3, :] = r.dgs[m + 2 : m + 3, :] + part
        for j in range(1, z.nl):
            back_copy(i, j).start()
        back_own(i).start()
        return 0

    lax.fori_loop(0, S * NCH, column_step, 0)

    for t in range(z.nt):
        rows = slice(t * z.rows, (t + 1) * z.rows)
        for i in range(3):
            r.g2s[t, :, i * D : (i + 1) * D] = r.dcin[i, rows, :].astype(BF)
        r.g2s[t, :, 3 * D : 4 * D] = r.dcout[rows, :].astype(BF)
        r.g2s[t, :, 4 * D : 4 * D + z.FF] = r.dew[rows, :].astype(BF)
        r.g2s[t, :, 4 * D + z.FF :] = rows_to_lanes(r.drw[t * z.frows : (t + 1) * z.frows, :], z.rows).astype(BF)
    core_copy(1).start()

    def back_step(i, _):
        s, l = i // L, lax.rem(i, L)

        @pl.when(l == 0)
        def _():
            for c in range(NCH):
                back_own(s * NCH + c).wait()
                for j in range(1, z.nl):
                    back_copy(s * NCH + c, j).wait_recv()

        @pl.when(i == 1)
        def _():
            sum_cores(1)

        for d in range(z.nl):
            for c in range(NCH):
                at = (d * NCH + c) * C
                put(r.mid, slice(at, at + C), unfold(r.dxr[s, l, d, c]))
        n1s, dqs, dks, dvs, d1s, os = [], [], [], [], [], []
        for b0 in range(0, W, BATCH_B):
            batch = range(b0, b0 + BATCH_B)
            d1 = jnp.concatenate([take(r.mid, pl.ds(w, WIN, stride=W)) for w in batch], axis=0)
            d1b = d1.astype(BF)
            do = dot(d1b, r.wout[...], 1, 1)
            dob = {w: spread(do[(w - b0) * WIN : (w - b0 + 1) * WIN], marks) for w in batch}
            qb = {w: spread(r.qv[i, w].astype(F32), marks) for w in batch}
            dpt = {w: scores(r.vv[i, w], dob[w]) for w in batch}
            dv = [weigh(r.pv[i, w], dob[w]) for w in batch]
            dsb = {}
            for w in batch:
                pf = r.pv[i, w].astype(F32)
                ds = pf * (dpt[w] - jnp.sum(dpt[w] * pf, 0, keepdims=True))
                dsb[w] = ds.astype(BF)
                r.bias[w // NWLON] = r.bias[w // NWLON] + ds
            dk = [weigh(dsb[w], qb[w]) * SCALE for w in batch]
            dq = [mix(dsb[w], r.kv[i, w], bounds) * SCALE for w in batch]
            x = r.xv[i, b0 : b0 + BATCH_B].astype(F32).reshape(BATCH_B * WIN, D)
            n1s.append((norm(x)[0] * gain1 + shift1).astype(BF))
            os.append(r.ov[i, b0 : b0 + BATCH_B].astype(F32).reshape(BATCH_B * WIN, D).astype(BF))
            r.ov[i, b0 : b0 + BATCH_B] = d1.reshape(BATCH_B, WIN, D).astype(BF)
            d1s.append(d1b)
            for part, parts, keep in ((dq, dqs, r.qv), (dk, dks, r.kv), (dv, dvs, r.vv)):
                flat = jnp.concatenate(part, axis=0)
                keep[i, b0 : b0 + BATCH_B] = flat.reshape(BATCH_B, WIN, D).astype(BF)
                parts.append(flat.astype(BF))
        n1 = jnp.concatenate(n1s, axis=0)
        for m, part in enumerate((dqs, dks, dvs)):
            r.dwin[m] = r.dwin[m] + dot(n1, jnp.concatenate(part, axis=0), 0, 0)
        r.dwout[...] = r.dwout[...] + dot(jnp.concatenate(os, axis=0), jnp.concatenate(d1s, axis=0), 0, 0)
        return 0

    lax.fori_loop(0, S * L, back_step, 0)

    for t in range(z.nt):
        rows = slice(t * z.rows, (t + 1) * z.rows)
        for i in range(3):
            r.g1s[t, :, i * D : (i + 1) * D] = r.dwin[i, rows, :].astype(BF)
        r.g1s[t, :, 3 * D : 4 * D] = r.dwout[rows, :].astype(BF)
    core_copy(0).start()
    sum_tiles(1)

    pads = jnp.zeros((WIN, 128 - WIN), F32)
    for b in range(z.bands):
        for h in range(8):
            at = (b * 8 + h) * WIN
            if h < HEADS:
                r.bbuf[at : at + WIN, :] = jnp.concatenate([r.bias[b, :, h * WIN : (h + 1) * WIN], pads], axis=1)
            else:
                r.bbuf[at : at + WIN, :] = jnp.zeros((WIN, 128), F32)
    tab = jnp.zeros((n8, RELP), F32)
    for j in range(0, WIN, 2):
        both = jnp.concatenate([one_hot(r.idxt, j), one_hot(r.idxt, j + 1)], axis=1)
        pair = jnp.concatenate([r.bbuf[pl.ds(j, n8, stride=WIN), :], r.bbuf[pl.ds(j + 1, n8, stride=WIN), :]], axis=1)
        tab = tab + dot(pair.astype(BF), both, 1, 1)
    for b in range(z.bands):
        r.ts[:, b * RELB : (b + 1) * RELB] = tab[b * 8 : (b + 1) * 8, :RELB].astype(BF)
    for j in range(1, z.nl):
        tab_copy(j).start()
    sum_cores(0)
    sum_chips(1)

    def norm_step(i, _):
        x = r.xv[i].astype(F32).reshape(TOK, D)
        xh, rs = norm(x)
        dn = 0.0
        for m, kept in enumerate((r.qv, r.kv, r.vv)):
            dn = dn + dot(kept[i].astype(F32).reshape(TOK, D).astype(BF), r.win[m], 1, 1)
        dx, a, b = norm_back(xh, rs, dn, gain1)
        r.xv[i] = (r.ov[i].astype(F32).reshape(TOK, D) + dx).reshape(W, WIN, D).astype(BF)
        store_x(i).start()
        r.dgs[0:1, :] = r.dgs[0:1, :] + a
        r.dgs[1:2, :] = r.dgs[1:2, :] + b
        return 0

    lax.fori_loop(0, S * L, norm_step, 0)

    for t in range(z.nt):
        r.g3s[t] = lane_pad(r.dgs[:, t * z.rows : (t + 1) * z.rows], 128).astype(BF)
    for j in range(1, z.nt):
        norm_tile_copy(j).start()
    sum_tiles(0)
    total = r.ts[...].astype(F32)
    for j in range(1, z.nl):
        tab_copy(j).wait_recv()
        total = total + r.tr[j - 1].astype(F32)
    r.otab[...] = total
    vec = r.g3s[pl.ds(me_t, 1)][0].astype(F32)
    for j in range(1, z.nt):
        norm_tile_copy(j).wait_recv()
        vec = vec + r.g3r[j - 1].astype(F32)
    r.h3s[...] = vec.astype(BF)
    for j in range(1, z.nl):
        norm_lev_copy(j).start()
    sum_chips(0)
    join_copy(1).wait_recv()
    r.osum2[...] = r.k2[0].astype(F32)
    vec = r.h3s[...].astype(F32)
    for j in range(1, z.nl):
        norm_lev_copy(j).wait_recv()
        vec = vec + r.h3r[j - 1].astype(F32)
    r.ovec[...] = vec
    join_copy(0).wait_recv()
    r.osum1[...] = r.k1[0].astype(F32)
    for i in range(2):
        weight_pass(i).wait_send()
        core_copy(i).wait_send()
        join_copy(i).wait_send()
        for j in range(1, z.nt):
            weight_copy(i, j).wait_send()
            tile_copy(i, j).wait_send()
        for j in range(1, z.nl // 2):
            chip_copy(i, j).wait_send()
    for j in range(1, z.nt):
        norm_tile_copy(j).wait_send()
    for j in range(1, z.nl):
        norm_lev_copy(j).wait_send()
    for j in range(1, z.nl):
        tab_copy(j).wait_send()
        for i in range(S * L):
            stream_copy(i, j).wait_send()
        for i in range(S * NCH):
            back_copy(i, j).wait_send()
    for i in range(S * L):
        store_x(i).wait()
    for i in range(S * NCH):
        store_out(i).wait()


def finish_kernel(z, names, pieces, *refs):
    r = Sems()
    for name, ref in zip(names, refs):
        setattr(r, name, ref)
    loads, stores = [], []
    for src, mid, dst in ((r.out0, r.out_mid, r.out), (r.dx0, r.dx_mid, r.dx)):
        n = max(1, src.shape[1] // pieces)
        for s in range(src.shape[0]):
            for p in range(0, src.shape[1], n):
                at = (s, pl.ds(p, n))
                sem = len(stores)
                loads.append(pltpu.make_async_copy(src.at[at], mid.at[at], r.sem.at[0, sem]))
                stores.append(pltpu.make_async_copy(mid.at[at], dst.at[at], r.sem.at[1, sem]))
    parts = ((r.sum1_in, r.sum1), (r.sum2_in, r.sum2), (r.vec_in, r.vec), (r.tab_in, r.tab))
    small = [pltpu.make_async_copy(a, b, r.load_sem.at[i]) for i, (a, b) in enumerate(parts)]
    for c in loads + small:
        c.start()
    for a, b in zip(loads, stores):
        a.wait()
        b.start()
    for c in small:
        c.wait()
    r.owi[...] = r.sum1[:, 0 : 3 * D]
    r.owo[...] = r.sum1[:, 3 * D : 4 * D]
    r.oci[...] = r.sum2[:, 0 : 3 * D]
    r.oco[...] = r.sum2[:, 3 * D : 4 * D]
    r.oew[...] = r.sum2[:, 4 * D : 4 * D + z.FF]
    for i in range(z.FF // D):
        r.orw[i * z.rows : (i + 1) * z.rows, :] = r.sum2[:, 4 * D + z.FF + i * D : 4 * D + z.FF + (i + 1) * D]
    for i, ref in enumerate((r.o0, r.o1, r.o2, r.o3, r.o4, r.o5)):
        ref[...] = r.vec[i : i + 1, 0 : z.rows]
    r.otab[...] = r.tab[0:HEADS, :]
    for c in stores:
        c.wait()


def dma(*shape):
    return pltpu.SemaphoreType.DMA(shape)


def body(mesh, inputs, out_grad, lowest_level, bias_index, first_gain, first_shift, window_in, window_out, earth_bias,
         second_gain, second_shift, column_in, column_out, third_gain, third_shift, expand_weight, reduce_weight):
    z = Sizes(mesh, inputs, out_grad, expand_weight)
    S, L, LV, W, C, CB, NCH, A, FF, nt, nl = z.S, z.L, z.LV, z.W, z.C, z.CB, z.NCH, HEADS * WIN, z.FF, z.nt, z.nl
    lanes = 4 * D + 2 * FF
    tab_lanes = z.bands * RELB
    g = out_grad.transpose(0, 1, 3, 2, 4).reshape(S, LV, z.cells * W, D)
    row = lambda a: a.reshape(1, z.rows)
    ins = dict(x=inputs, g=g, lowest=lowest_level, idx=bias_index, tab=earth_bias.T, wi=window_in, wo=window_out,
               ci=column_in, co=column_out, ew=expand_weight, rw=reduce_weight, v0=row(first_gain), v1=row(first_shift),
               v2=row(second_gain), v3=row(second_shift), v4=row(third_gain), v5=row(third_shift))
    outs = dict(out=(g.shape, BF), dx=(inputs.shape, BF), osum1=((z.rows, 4 * D), F32), osum2=((z.rows, lanes), F32),
                ovec=((8, 128), F32), otab=((8, tab_lanes), F32))
    tokens = pltpu.VMEM((S * L, W, WIN, D), BF)
    slabs = ((z.rpad + 8, 4 * D), (z.rows, lanes))
    sums = ((z.rows, 4 * D), (z.rows, lanes))
    scratch = dict(xv=tokens, qv=tokens, kv=tokens, vv=tokens, ov=tokens, pv=pltpu.VMEM((S * L, W, WIN, A), BF),
                   gv=pltpu.VMEM((S * NCH, LV, C, D), BF), xs=pltpu.VMEM((S * L, nl, NCH, CB, 128), BF),
                   x1r=pltpu.VMEM((S, LV, NCH, CB, 128), BF), ys=pltpu.VMEM((S * NCH, LV, CB, 128), BF),
                   dxr=pltpu.VMEM((S, L, nl, NCH, CB, 128), BF), mid=pltpu.VMEM((2, W * WIN, 128), F32),
                   bias=pltpu.VMEM((z.bands, WIN, A), F32), bbuf=pltpu.VMEM((z.bands * 8 * WIN, 128), F32),
                   idxt=pltpu.VMEM((128, 128), jnp.int32), key=pltpu.VMEM((LV * 8, HEADS * LV * 8), F32),
                   low=pltpu.VMEM((S, W // 8, z.cells, HEADS * LV * 8), F32),
                   wide=pltpu.VMEM((D, lanes), F32), widef=pltpu.VMEM((FF, D), F32), gs=pltpu.VMEM((8, D), F32),
                   win=pltpu.VMEM((3, D, D), BF), wout=pltpu.VMEM((D, D), BF), cin=pltpu.VMEM((3, D, D), BF),
                   cout=pltpu.VMEM((D, D), BF), ewf=pltpu.VMEM((D, FF), BF), rwf=pltpu.VMEM((FF, D), BF),
                   dwin=pltpu.VMEM((3, D, D), F32), dwout=pltpu.VMEM((D, D), F32), dcin=pltpu.VMEM((3, D, D), F32),
                   dcout=pltpu.VMEM((D, D), F32), dew=pltpu.VMEM((D, FF), F32), drw=pltpu.VMEM((FF, D), F32), dgs=pltpu.VMEM((8, D), F32),
                   ts=pltpu.VMEM((8, tab_lanes), BF), tr=pltpu.VMEM((nl - 1, 8, tab_lanes), BF))
    for i, sh in enumerate(slabs):
        scratch.update({f"w{i + 1}s": pltpu.VMEM((1,) + sh, BF), f"w{i + 1}r": pltpu.VMEM((nt,) + sh, BF)})
    for i, (n, m) in enumerate(sums):
        part = (n, m // 2)
        scratch.update({f"g{i + 1}s": pltpu.VMEM((nt, n, m), BF), f"g{i + 1}t": pltpu.VMEM((nt,) + part, BF),
                        f"g{i + 1}h": pltpu.VMEM((nt,) + part, BF), f"g{i + 1}r": pltpu.VMEM((nt - 1,) + part, BF),
                        f"h{i + 1}s": pltpu.VMEM(part, BF), f"h{i + 1}r": pltpu.VMEM((nl // 2 - 1,) + part, BF),
                        f"k{i + 1}": pltpu.VMEM((1, n, m), BF)})
    scratch.update(g3s=pltpu.VMEM((nt, 8, 128), BF), g3r=pltpu.VMEM((nt - 1, 8, 128), BF), h3s=pltpu.VMEM((8, 128), BF),
                   h3r=pltpu.VMEM((nl - 1, 8, 128), BF))
    chips = max(nl // 2 - 1, 1)
    scratch.update(x_sem=dma(S * L), dx_sem=dma(S * L), g_sem=dma(S * NCH), out_sem=dma(S * NCH), w_send=dma(2, nt - 1), w_recv=dma(2, nt - 1),
                   wt_send=dma(2), wt_recv=dma(2), s_send=dma(S * L, nl - 1), s_recv=dma(S * L, nl - 1), s_own=dma(S * L),
                   b_send=dma(S * NCH, nl - 1), b_recv=dma(S * NCH, nl - 1), b_own=dma(S * NCH),
                   gt_send=dma(2), gt_recv=dma(2), g_send=dma(2, nt - 1), g_recv=dma(2, nt - 1), h_send=dma(2, chips), h_recv=dma(2, chips),
                   k_send=dma(2), k_recv=dma(2), t_send=dma(nl - 1), t_recv=dma(nl - 1),
                   n_send=dma(nt - 1), n_recv=dma(nt - 1), m_send=dma(nl - 1), m_recv=dma(nl - 1))
    hbm = ("x", "g", "out", "dx")
    place = lambda name: pl.BlockSpec(memory_space=pl.ANY if name in hbm else pltpu.VMEM)
    done = dict(zip(outs, pl.pallas_call(
        functools.partial(layer_kernel, z, tuple(ins) + tuple(outs) + tuple(scratch)),
        in_specs=[place(name) for name in ins],
        out_specs=[place(name) for name in outs],
        out_shape=[jax.ShapeDtypeStruct(*o) for o in outs.values()],
        scratch_shapes=list(scratch.values()),
        compiler_params=pltpu.CompilerParams(vmem_limit_bytes=VMEM_LIMIT, collective_id=0, has_side_effects=True),
        name="layer",
    )(*ins.values())))
    last_in = dict(out0=done["out"], dx0=done["dx"], sum1_in=done["osum1"], sum2_in=done["osum2"], vec_in=done["ovec"], tab_in=done["otab"])
    last = dict(out=(g.shape, BF), dx=(inputs.shape, BF), owi=((z.rows, 3 * D), F32), owo=((z.rows, D), F32),
                oci=((z.rows, 3 * D), F32), oco=((z.rows, D), F32), oew=((z.rows, FF), F32), orw=((z.frows, D), F32),
                otab=((HEADS, tab_lanes), F32), **{f"o{i}": ((1, z.rows), F32) for i in range(6)})
    pieces = 4
    place = lambda name: pl.BlockSpec(memory_space=pl.ANY if name in last_in or name in ("out", "dx") else pltpu.VMEM)
    held = dict(sum1=done["osum1"], sum2=done["osum2"], vec=done["ovec"], tab=done["otab"])
    end = dict(zip(last, pl.pallas_call(
        functools.partial(finish_kernel, z, tuple(last_in) + tuple(last) + tuple(held) + ("out_mid", "dx_mid", "sem", "load_sem"), pieces),
        in_specs=[place(name) for name in last_in],
        out_specs=[place(name) for name in last],
        out_shape=[jax.ShapeDtypeStruct(*o) for o in last.values()],
        scratch_shapes=[pltpu.VMEM(a.shape, F32) for a in held.values()] + [pltpu.VMEM(g.shape, BF), pltpu.VMEM(inputs.shape, BF), dma(2, 4 * S * pieces), dma(4)],
        compiler_params=pltpu.CompilerParams(vmem_limit_bytes=VMEM_LIMIT),
        name="finish",
    )(*last_in.values())))
    output = end["out"].reshape(S, LV, z.cells, W, D).transpose(0, 1, 3, 2, 4)
    v = [end[f"o{i}"].reshape(z.rows) for i in range(6)]
    return (output, end["dx"], v[0], v[1], end["owi"], end["owo"], end["otab"].T, v[2], v[3],
            end["oci"], end["oco"], v[4], v[5], end["oew"], end["orw"])


def solution(mesh):
    t, t2 = P("tile"), P("tile", None)
    level_tokens = P(None, "lev", "tile", None, None)
    column_tokens = P(None, None, "tile", "lev", None)
    placed = (level_tokens, column_tokens, P(None, "tile", "lev"), P(), t, t, t2, t2, t2, t, t, t2, t2, t, t, t2, t2)
    outs = (column_tokens, level_tokens, t, t, t2, t2, t2, t, t, t2, t2, t, t, t2, t2)
    return jax.shard_map(functools.partial(body, mesh), mesh=mesh, in_specs=placed, out_specs=outs, check_vma=False)
```

```python
import functools

import jax
import jax.numpy as jnp
from jax import lax
from jax.experimental import pallas as pl
from jax.experimental.pallas import tpu as pltpu
from jax.sharding import PartitionSpec as P

HEADS = 6
HEAD_DIM = 32
D = HEADS * HEAD_DIM
WIN = 72
RELB = 828
RELP = 832
NWLON = 2
EPSILON = 1e-05
SCALE = HEAD_DIM ** (-0.5)
LOG2E = 1.4426950408889634
MASKED = -1e30
F32 = jnp.float32
BF = jnp.bfloat16
MESH = pl.DeviceIdType.MESH
VMEM_LIMIT = 60 << 20
BATCH_F, BATCH_C, BATCH_B = 8, 12, 8


def dot(a, b, ca=1, cb=0):
    return lax.dot_general(a, b, (((ca,), (cb,)), ((), ())), preferred_element_type=F32)


def lane_heads():
    lane = lax.broadcasted_iota(jnp.int32, (1, 128), 1)
    return [(lane // HEAD_DIM == h).astype(F32) for h in range(4)], [lane < HEAD_DIM * (h + 1) for h in range(3)]


def spread(v, marks, factor=None):
    n = v.shape[0]
    low, high = v[:, :128], v[:, 128:]
    tops = [m if factor is None else m * factor for m in marks]
    if n == 64:
        low, high = low.astype(BF), high.astype(BF)
        tops = [m.astype(BF) for m in tops]
        first = jnp.concatenate([low * m for m in tops], axis=0)
        return first, jnp.concatenate([high * m[:, :64] for m in tops[:2]], axis=0)
    parts = [low * m for m in tops]
    cut = 256 - 3 * n
    first = jnp.concatenate(parts[:3] + [parts[3][:cut]], axis=0).astype(BF)
    head3 = jnp.concatenate([parts[3][cut:], jnp.zeros((n - cut, 64), F32)], axis=1)
    blank = jnp.zeros((n, 128), F32)
    rest = [jnp.concatenate([blank, high * m[:, :64]], axis=1) for m in tops[:2]]
    return first, jnp.concatenate([head3] + rest, axis=0).astype(BF)


def scores(k, spread_q):
    first, rest = spread_q
    right = k[:, 128:] if rest.shape[1] == 64 else k
    return jnp.concatenate([dot(k[:, :128], first, 1, 1), dot(right, rest, 1, 1)], axis=1)


def weigh(p, spread_v):
    first, rest = spread_v
    low, high = dot(p[:, :256], first), dot(p[:, 256:], rest)
    if rest.shape[1] == 64:
        return jnp.concatenate([low, high], axis=1)
    return jnp.concatenate([low + high[:, :128], high[:, 128:]], axis=1)


def mix(p, v, bounds):
    n = v.shape[0]
    first = dot(p[:, :256], v[:, :128], 0, 0)
    if n == 64:
        rest = dot(p[:, 256:], v[:, 128:], 0, 0)
        head3, tail = first[3 * n :], rest
    else:
        rest = dot(p[:, 256:], v, 0, 0)
        cut = 4 * n - 256
        head3, tail = jnp.concatenate([first[3 * n :], rest[:cut, :128]], axis=0), rest[cut:, 128:]
    low = jnp.where(bounds[0], first[:n], jnp.where(bounds[1], first[n : 2 * n], jnp.where(bounds[2], first[2 * n : 3 * n], head3)))
    high = jnp.where(bounds[0][:, :64], tail[:n], tail[n:])
    return jnp.concatenate([low, high], axis=1)


def norm(x):
    mean = jnp.sum(x, -1, keepdims=True) * (1.0 / D)
    c = x - mean
    var = jnp.sum(c * c, -1, keepdims=True) * (1.0 / D)
    r = lax.rsqrt(var + EPSILON)
    return c * r, r


def norm_back(xh, r, dn, gain, sums=True):
    t = dn * gain
    a = jnp.sum(t, -1, keepdims=True) * (1.0 / D)
    b = jnp.sum(t * xh, -1, keepdims=True) * (1.0 / D)
    dx = r * (t - a - xh * b)
    if not sums:
        return dx
    return dx, jnp.sum(dn * xh, 0, keepdims=True), jnp.sum(dn, 0, keepdims=True)


def softmax2(st):
    e = jnp.exp2(st - jnp.max(st, 0, keepdims=True))
    return e * (1.0 / jnp.sum(e, 0, keepdims=True))


def put(ref, rows, v):
    n = v.shape[0]
    ref[0, rows, :] = v[:, :128]
    ref[1, rows, :] = jnp.concatenate([v[:, 128:], jnp.zeros((n, 256 - D), F32)], axis=1)


def take(ref, rows):
    return jnp.concatenate([ref[0, rows, :], ref[1, rows, :][:, : D - 128]], axis=1)


def fold(ref, at, v):
    c = v.shape[0]
    ref[at + (slice(0, c),)] = v[:, :128].astype(BF)
    tail = jnp.concatenate([v[: c // 2, 128:], v[c // 2 :, 128:]], axis=1)
    ref[at + (slice(c, c + c // 2),)] = tail.astype(BF)


def unfold(block):
    c = block.shape[0] * 2 // 3
    wide = block.astype(F32)
    tail = wide[c:]
    return jnp.concatenate([wide[:c], jnp.concatenate([tail[:, :64], tail[:, 64:]], axis=0)], axis=1)


def one_hot(idx_ref, j):
    entry = lax.broadcasted_iota(jnp.int32, (RELP, 128), 0)
    return (entry == idx_ref[j : j + 1, :]).astype(F32).astype(BF)


def announce(axes):
    sem = pltpu.get_barrier_semaphore()
    count = 0
    for axis, size in axes:
        me = lax.axis_index(axis)
        for j in range(1, size):
            pl.semaphore_signal(sem, inc=1, device_id={axis: lax.rem(me + j, size)}, device_id_type=MESH)
            count += 1
    return sem, count


def to_peer(axis, size, j, src, dst, send, recv):
    me = lax.axis_index(axis)
    return pltpu.make_async_remote_copy(
        src_ref=src, dst_ref=dst, send_sem=send, recv_sem=recv,
        device_id={axis: lax.rem(me + j, size)}, device_id_type=MESH,
    )


def rows_to_lanes(m, n):
    return jnp.concatenate([m[i : i + n] for i in range(0, m.shape[0], n)], axis=1)


class Sizes:
    def __init__(self, mesh, inputs, out_grad, expand):
        self.nl = mesh.shape["lev"]
        self.nt = mesh.shape["tile"]
        self.S, self.L, self.W = inputs.shape[:3]
        self.LV = out_grad.shape[1]
        self.cells = out_grad.shape[3]
        self.bands = self.W // NWLON
        self.rows = D // self.nt
        self.rpad = -(-self.rows // 8) * 8
        self.FF = expand.shape[1]
        self.frows = self.FF // self.nt
        self.T = 6 if self.cells % 6 == 0 else 3
        self.NCH = self.cells // self.T
        self.C = self.T * self.W
        self.CB = self.C * 3 // 2


def lane_pad(m, width, value=0.0):
    if m.shape[1] == width:
        return m
    return jnp.concatenate([m, jnp.full((m.shape[0], width - m.shape[1]), value, F32)], axis=1)


def pairs(count, before, step, after):
    def two(i, _):
        for k in range(2):
            before(2 * i + k)
        for k in range(2):
            step(2 * i + k, k)
        for k in range(2):
            after(2 * i + k)
        return 0

    lax.fori_loop(0, count // 2, two, 0)


def singles(count, before, step, after):
    def one(i, _):
        before(i)
        step(i, 0)
        after(i)
        return 0

    lax.fori_loop(0, count, one, 0)


class Sems:
    pass


def layer_kernel(z, names, *refs):
    r = Sems()
    for name, ref in zip(names, refs):
        setattr(r, name, ref)
    me_l, me_t = lax.axis_index("lev"), lax.axis_index("tile")
    S, L, LV, W, C, NCH = z.S, z.L, z.LV, z.W, z.C, z.NCH
    TOK = W * WIN
    TABH = r.th.shape[-1]
    marks, bounds = lane_heads()

    def load_x(i):
        return pltpu.make_async_copy(r.x.at[i // L, lax.rem(i, L)], r.xv.at[i], r.x_sem.at[i])

    def store_x(i):
        return pltpu.make_async_copy(r.xv.at[i], r.dx.at[i // L, lax.rem(i, L)], r.dx_sem.at[i])

    def load_g(i):
        rows = pl.ds(pl.multiple_of(lax.rem(i, NCH) * C, 16), C)
        return pltpu.make_async_copy(r.g.at[i // NCH, :, rows, :], r.gv.at[i], r.g_sem.at[i])

    def store_out(i):
        rows = pl.ds(pl.multiple_of(lax.rem(i, NCH) * C, 16), C)
        return pltpu.make_async_copy(r.gv.at[i], r.out.at[i // NCH, :, rows, :], r.out_sem.at[i])

    core, twin = lax.rem(me_l, 2), me_l + 1 - 2 * lax.rem(me_l, 2)

    def to_twin(src, dst, send, recv):
        return pltpu.make_async_remote_copy(src_ref=src, dst_ref=dst, send_sem=send, recv_sem=recv,
                                            device_id={"lev": twin}, device_id_type=MESH)

    def half(ref, which):
        width = ref.shape[-1] // 2
        return ref.at[:, :, pl.ds(pl.multiple_of(which * width, 128), width)]

    weights = ((r.w1s, r.w1r), (r.w2s, r.w2r))

    def weight_copy(i, j):
        src, dst = weights[i]
        return to_peer("tile", z.nt, j, half(src, core).at[0], half(dst, core).at[me_t], r.w_send.at[i, j - 1], r.w_recv.at[i, j - 1])

    def weight_pass(i):
        part = half(weights[i][1], core)
        return to_twin(part, part, r.wt_send.at[i], r.wt_recv.at[i])

    def weight_start(i):
        for j in range(1, z.nt):
            weight_copy(i, j).start()
        src, dst = weights[i]
        width = src.shape[-1] // 2
        own = pl.ds(pl.multiple_of(core * width, 128), width)
        dst[pl.ds(me_t, 1), :, own] = src[:, :, own]

    def weight_hand(i):
        for j in range(1, z.nt):
            weight_copy(i, j).wait_recv()
        weight_pass(i).start()

    def stream_copy(i, c, j):
        return to_peer("lev", z.nl, j, r.xs.at[i, lax.rem(me_l + j, z.nl), c], r.x1r.at[i // L, me_l * L + lax.rem(i, L), c],
                       r.s_send.at[i * NCH + c, j - 1], r.s_recv.at[i * NCH + c, j - 1])

    def stream_own(i, c):
        return pltpu.make_async_copy(r.xs.at[i, me_l, c], r.x1r.at[i // L, me_l * L + lax.rem(i, L), c], r.s_own.at[i * NCH + c])

    def back_copy(i, j):
        return to_peer("lev", z.nl, j, r.ys.at[i, pl.ds(lax.rem(me_l + j, z.nl) * L, L)],
                       r.dxr.at[i // NCH, :, me_l, lax.rem(i, NCH)], r.b_send.at[i, j - 1], r.b_recv.at[i, j - 1])

    def back_own(i):
        return pltpu.make_async_copy(r.ys.at[i, pl.ds(me_l * L, L)], r.dxr.at[i // NCH, :, me_l, lax.rem(i, NCH)], r.b_own.at[i])

    grads = ((r.g1s, r.g1t, r.g1h, r.g1r, r.h1s, r.h1r), (r.g2s, r.g2t, r.g2h, r.g2r, r.h2s, r.h2r))

    def core_copy(i):
        return to_twin(half(grads[i][0], 1 - core), grads[i][1], r.gt_send.at[i], r.gt_recv.at[i])

    def tile_copy(i, j):
        src, dst = grads[i][2], grads[i][3]
        return to_peer("tile", z.nt, j, src.at[lax.rem(me_t + j, z.nt)], dst.at[j - 1], r.g_send.at[i, j - 1], r.g_recv.at[i, j - 1])

    def lev_copy(i, j):
        return to_peer("lev", z.nl, j, grads[i][4], grads[i][5].at[j - 1], r.h_send.at[i, j - 1], r.h_recv.at[i, j - 1])

    def sum_cores(i):
        core_copy(i).wait_recv()
        gs, gt, gh = grads[i][:3]
        width = gt.shape[-1]
        mine = gs[:, :, pl.ds(pl.multiple_of(core * width, 128), width)]
        gh[...] = (mine.astype(F32) + gt[...].astype(F32)).astype(BF)
        for j in range(1, z.nt):
            tile_copy(i, j).start()

    def sum_tiles(i):
        gh, gr, hs = grads[i][2:5]
        total = gh[pl.ds(me_t, 1)][0].astype(F32)
        for j in range(1, z.nt):
            tile_copy(i, j).wait_recv()
            total = total + gr[j - 1].astype(F32)
        hs[...] = total.astype(BF)
        for j in range(1, z.nl):
            lev_copy(i, j).start()

    def sum_halves(own, got, out):
        mine, other = own[...].astype(F32), 0.0
        for j in range(1, z.nl):
            if j % 2 == 0:
                mine = mine + got[j - 1].astype(F32)
            else:
                other = other + got[j - 1].astype(F32)
        width = own.shape[-1]
        first = core == 0
        out[:, 0:width] = jnp.where(first, mine, other)
        out[:, width : 2 * width] = jnp.where(first, other, mine)

    def sum_lev(i, out):
        for j in range(1, z.nl):
            lev_copy(i, j).wait_recv()
        sum_halves(grads[i][4], grads[i][5], out)

    def tab_core_copy():
        part = r.ts.at[:, pl.ds(pl.multiple_of((1 - core) * TABH, 128), TABH)]
        return to_twin(part, r.tt, r.tt_send.at[0], r.tt_recv.at[0])

    def tab_cores():
        tab_core_copy().wait_recv()
        mine = r.ts[:, pl.ds(pl.multiple_of(core * TABH, 128), TABH)]
        r.th[...] = (mine.astype(F32) + r.tt[...].astype(F32)).astype(BF)
        for j in range(1, z.nl):
            tab_copy(j).start()

    def tab_copy(j):
        return to_peer("lev", z.nl, j, r.th, r.tr.at[j - 1], r.t_send.at[j - 1], r.t_recv.at[j - 1])

    def norm_tile_copy(j):
        return to_peer("tile", z.nt, j, r.g3s.at[lax.rem(me_t + j, z.nt)], r.g3r.at[j - 1], r.n_send.at[j - 1], r.n_recv.at[j - 1])

    def norm_lev_copy(j):
        return to_peer("lev", z.nl, j, r.h3s, r.h3r.at[j - 1], r.m_send.at[j - 1], r.m_recv.at[j - 1])

    sem, count = announce((("lev", z.nl), ("tile", z.nt)))
    for i in range(S * L):
        load_x(i).start()
    for i in range(S * NCH):
        load_g(i).start()
    r.w1s[...] = jnp.zeros(r.w1s.shape, BF)
    r.w1s[0, 0 : z.rows, 0 : 3 * D] = r.wi[...]
    r.w1s[0, 0 : z.rows, 3 * D : 4 * D] = r.wo[...]
    for i, vec in enumerate((r.v0, r.v1, r.v2, r.v3, r.v4, r.v5)):
        r.w1s[0, z.rpad + i : z.rpad + i + 1, 0 : z.rows] = vec[...]
    r.w2s[0, :, 0 : 3 * D] = r.ci[...]
    r.w2s[0, :, 3 * D : 4 * D] = r.co[...]
    r.w2s[0, :, 4 * D : 4 * D + z.FF] = r.ew[...]
    r.w2s[0, :, 4 * D + z.FF :] = rows_to_lanes(r.rw[...].astype(F32), z.rows).astype(BF)
    entries = lane_pad(r.idx[...].astype(F32), 128, -1.0)
    entries = jnp.concatenate([entries, jnp.full((128 - WIN, 128), -1.0, F32)], axis=0)
    r.idxt[...] = jnp.transpose(entries).astype(jnp.int32)
    cells8 = lax.broadcasted_iota(jnp.int32, (LV * 8, HEADS * LV * 8), 0)
    lane8 = lax.broadcasted_iota(jnp.int32, (LV * 8, HEADS * LV * 8), 1)
    r.key[...] = jnp.where(cells8 % 8 == lane8 % 8, (cells8 // 8).astype(F32), -1.0)
    wrow = lax.broadcasted_iota(jnp.int32, (W, HEADS * LV * 8), 0)
    wlane = lax.broadcasted_iota(jnp.int32, (W, HEADS * LV * 8), 1)
    for part in range(W // 8):
        pick = (wrow == wlane % 8 + 8 * part).astype(F32).astype(BF)
        for s in range(S):
            r.low[s, part] = dot(r.lowest[s].astype(F32).astype(BF), pick, 0, 0)
    r.ts[...] = jnp.zeros(r.ts.shape, BF)
    pl.semaphore_wait(sem, count)
    weight_start(0)
    table = r.tab[...].astype(F32)
    pads = jnp.zeros((8 - HEADS, RELP), F32)
    table = jnp.concatenate(
        [jnp.concatenate([lane_pad(table[:, b * RELB : (b + 1) * RELB], RELP), pads], axis=0) for b in range(z.bands)], axis=0
    ).astype(BF)
    n8 = z.bands * 8
    for j in range(0, WIN, 2):
        both = jnp.concatenate([one_hot(r.idxt, j), one_hot(r.idxt, j + 1)], axis=1)
        vals = dot(table, both) * LOG2E
        r.bbuf[pl.ds(j, n8, stride=WIN), :] = vals[:, :128]
        r.bbuf[pl.ds(j + 1, n8, stride=WIN), :] = vals[:, 128:]
    weight_hand(0)
    weight_start(1)
    for b in range(z.bands):
        r.bias[b] = jnp.concatenate(
            [r.bbuf[(b * 8 + h) * WIN : (b * 8 + h + 1) * WIN, :][:, :WIN] for h in range(HEADS)], axis=1
        )
    for ref in (r.dcin, r.dcout, r.dew, r.drw, r.dwin, r.dwout, r.dgs, r.dsum):
        ref[...] = jnp.zeros(ref.shape, F32)
    weight_pass(0).wait_recv()
    for t in range(z.nt):
        r.wide[t * z.rows : (t + 1) * z.rows, 0 : 4 * D] = r.w1r[t, 0 : z.rows, :].astype(F32)
    for i in range(3):
        r.win[i] = r.wide[:, i * D : (i + 1) * D].astype(BF)
    r.wout[...] = r.wide[:, 3 * D : 4 * D].astype(BF)
    r.gs[...] = jnp.concatenate([r.w1r[t, z.rpad : z.rpad + 8, :].astype(F32)[:, : z.rows] for t in range(z.nt)], axis=1)
    gain1, shift1, g2, s2, g3, s3 = (r.gs[i : i + 1, :] for i in range(6))

    def window_step(i, slot):
        x = r.xv[i].astype(F32).reshape(TOK, D)
        xh, _ = norm(x)
        n1 = (xh * gain1 + shift1).astype(BF)
        q, k, v = (dot(n1, r.win[m]) for m in range(3))
        mixed = []
        for b0 in range(0, W, BATCH_F):
            batch = range(b0, b0 + BATCH_F)
            cut = {w: slice(w * WIN, (w + 1) * WIN) for w in batch}
            kb = {w: k[cut[w]].astype(BF) for w in batch}
            vb = {w: v[cut[w]].astype(BF) for w in batch}
            for w in batch:
                r.qv[i, w] = q[cut[w]].astype(BF)
                r.kv[i, w] = kb[w]
                r.vv[i, w] = vb[w]
            sq = {w: spread(q[cut[w]], marks, SCALE * LOG2E) for w in batch}
            st = {w: scores(kb[w], sq[w]) + r.bias[w // NWLON] for w in batch}
            pb = {w: softmax2(st[w]).astype(BF) for w in batch}
            for w in batch:
                r.pv[i, w] = pb[w]
            mixed += [mix(pb[w], vb[w], bounds) for w in batch]
        o = jnp.concatenate(mixed, axis=0).astype(BF)
        r.ov[i] = o.astype(F32).reshape(W, WIN, D).astype(BF)
        x1 = x + dot(o, r.wout[...])
        for w in range(W):
            put(r.mid.at[slot], pl.ds(w, WIN, stride=W), x1[w * WIN : (w + 1) * WIN])
        for d in range(z.nl):
            for c in range(NCH):
                at = (d * NCH + c) * C
                fold(r.xs, (i, d, c), take(r.mid.at[slot], slice(at, at + C)))

    def window_before(i):
        load_x(i).wait()

        @pl.when(i == S * L - 1)
        def _():
            weight_hand(1)

    def window_after(i):
        for c in range(NCH):
            for j in range(1, z.nl):
                stream_copy(i, c, j).start()
            stream_own(i, c).start()

    singles(S * L, window_before, window_step, window_after)

    weight_pass(1).wait_recv()
    for t in range(z.nt):
        r.wide[t * z.rows : (t + 1) * z.rows, :] = r.w2r[t].astype(F32)
        for i in range(z.FF // D):
            at = t * z.frows + i * z.rows
            r.widef[at : at + z.rows, :] = r.w2r[t].astype(F32)[:, 4 * D + z.FF + i * D : 4 * D + z.FF + (i + 1) * D]
    for i in range(3):
        r.cin[i] = r.wide[:, i * D : (i + 1) * D].astype(BF)
    r.cout[...] = r.wide[:, 3 * D : 4 * D].astype(BF)
    r.ewf[...] = r.wide[:, 4 * D : 4 * D + z.FF].astype(BF)
    r.rwf[...] = r.widef[...].astype(BF)
    r.bias[...] = jnp.zeros(r.bias.shape, F32)

    groups, R, GR = C // 8, LV * C, LV * 8
    halves = W // 8

    def cols(m, j):
        return m.reshape(LV, C, D)[:, j * 8 : (j + 1) * 8, :].reshape(GR, D)

    def join(parts):
        return jnp.concatenate([p.reshape(LV, 8, D) for p in parts], axis=1).reshape(R, D)

    def column_step(i, slot):
        s, ch = i // NCH, lax.rem(i, NCH)

        x1 = jnp.concatenate([unfold(r.x1r[s, m, ch]) for m in range(LV)], axis=0)
        xh2, r2 = norm(x1)
        n2 = (xh2 * g2 + s2).astype(BF)
        q, k, v = (dot(n2, r.cin[m]) for m in range(3))
        key = r.key[...]
        mixed = []
        qb, kb, vb, pb = {}, {}, {}, {}
        for b0 in range(0, groups, BATCH_C):
            batch = range(b0, min(b0 + BATCH_C, groups))
            for j in batch:
                kb[j], vb[j] = cols(k, j).astype(BF), cols(v, j).astype(BF)
                qb[j] = spread(cols(q, j), marks, SCALE * LOG2E)
            st = {j: scores(kb[j], qb[j]) for j in batch}
            for j in batch:
                low = r.low[s, j % halves, pl.ds(ch * z.T + j // halves, 1), :]
                pb[j] = softmax2(jnp.where(key >= low, st[j], MASKED)).astype(BF)
            mixed += [mix(pb[j], vb[j], bounds) for j in batch]
        o2 = join(mixed).astype(BF)
        x2 = x1 + dot(o2, r.cout[...])
        xh3, r3 = norm(x2)
        n3 = (xh3 * g3 + s3).astype(BF)
        gb = r.gv[i].astype(F32).reshape(R, D).astype(BF)
        u = dot(n3, r.ewf[...] * 0.5).astype(BF)
        dh = dot(gb, r.rwf[...] * 0.5, 1, 1).astype(BF)
        c = 0.7978845608028654
        a = BF(2 * c) + BF(8 * c * 0.044715) * (u * u)
        t = jnp.tanh(u * a)
        up = BF(1.0) + t
        hid = u * up
        du = dh * (up + hid * (BF(1.0) - t) * (BF(3.0) * a - BF(4.0 * c)))
        dn3 = dot(du, r.ewf[...], 1, 1)
        dx, a3, b3 = norm_back(xh3, r3, dn3, g3)
        dx2 = gb.astype(F32) + dx
        dx2b = dx2.astype(BF)
        r.gv[i] = (x2 + dot(hid, r.rwf[...])).reshape(LV, C, D).astype(BF)
        r.drw[...] = r.drw[...] + dot(hid, gb, 0, 0)
        r.dew[...] = r.dew[...] + dot(n3, du, 0, 0)
        r.dcout[...] = r.dcout[...] + dot(o2, dx2b, 0, 0)
        do = dot(dx2b, r.cout[...], 1, 1)
        dq, dk, dv = [], [], []
        for b0 in range(0, groups, BATCH_C):
            batch = range(b0, min(b0 + BATCH_C, groups))
            dob = {j: spread(cols(do, j), marks) for j in batch}
            dpt = {j: scores(vb[j], dob[j]) for j in batch}
            dv += [weigh(pb[j], dob[j]) for j in batch]
            dsb = {}
            for j in batch:
                pf = pb[j].astype(F32)
                dsb[j] = (pf * (dpt[j] - jnp.sum(dpt[j] * pf, 0, keepdims=True))).astype(BF)
            dk += [weigh(dsb[j], qb[j]) * (1.0 / LOG2E) for j in batch]
            dq += [mix(dsb[j], kb[j], bounds) * SCALE for j in batch]
        dn2 = 0.0
        packs = [join(part).astype(BF) for part in (dq, dk, dv)]
        for m, pack in enumerate(packs):
            dn2 = dn2 + dot(pack, r.cin[m], 1, 1)
        dx, a2, b2 = norm_back(xh2, r2, dn2, g2)
        for m, pack in enumerate(packs):
            r.dcin[m] = r.dcin[m] + dot(n2, pack, 0, 0)
        dx1 = dx2 + dx
        for m in range(LV):
            fold(r.ys, (i, m), dx1[m * C : (m + 1) * C])
        for m, part in enumerate((a2, b2, a3, b3)):
            r.dgs[m + 2 : m + 3, :] = r.dgs[m + 2 : m + 3, :] + part

    def column_before(i):
        s, ch = i // NCH, lax.rem(i, NCH)
        load_g(i).wait()
        for l in range(L):
            stream_own(s * L + l, ch).wait()
            for j in range(1, z.nl):
                stream_copy(s * L + l, ch, j).wait_recv()

    def column_after(i):
        store_out(i).start()
        for j in range(1, z.nl):
            back_copy(i, j).start()
        back_own(i).start()

    pairs(S * NCH, column_before, column_step, column_after)

    for t in range(z.nt):
        rows = slice(t * z.rows, (t + 1) * z.rows)
        for i in range(3):
            r.g2s[t, :, i * D : (i + 1) * D] = r.dcin[i, rows, :].astype(BF)
        r.g2s[t, :, 3 * D : 4 * D] = r.dcout[rows, :].astype(BF)
        r.g2s[t, :, 4 * D : 4 * D + z.FF] = r.dew[rows, :].astype(BF)
        r.g2s[t, :, 4 * D + z.FF :] = rows_to_lanes(r.drw[t * z.frows : (t + 1) * z.frows, :], z.rows).astype(BF)
    core_copy(1).start()
    for t in range(z.nt):
        r.g3s[t] = lane_pad(r.dgs[:, t * z.rows : (t + 1) * z.rows], 128).astype(BF)
    for j in range(1, z.nt):
        norm_tile_copy(j).start()

    def back_step(i, slot):
        s, l = i // L, lax.rem(i, L)

        for d in range(z.nl):
            for c in range(NCH):
                at = (d * NCH + c) * C
                put(r.mid.at[slot], slice(at, at + C), unfold(r.dxr[s, l, d, c]))
        xhs, dqs, dks, dvs, d1s, os = [], [], [], [], [], []
        for b0 in range(0, W, BATCH_B):
            batch = range(b0, b0 + BATCH_B)
            d1 = jnp.concatenate([take(r.mid.at[slot], pl.ds(w, WIN, stride=W)) for w in batch], axis=0)
            d1b = d1.astype(BF)
            do = dot(d1b, r.wout[...], 1, 1)
            dob = {w: spread(do[(w - b0) * WIN : (w - b0 + 1) * WIN], marks) for w in batch}
            qb = {w: spread(r.qv[i, w].astype(F32), marks) for w in batch}
            dpt = {w: scores(r.vv[i, w], dob[w]) for w in batch}
            dv = [weigh(r.pv[i, w], dob[w]) for w in batch]
            dsb = {}
            for w in batch:
                pf = r.pv[i, w].astype(F32)
                ds = pf * (dpt[w] - jnp.sum(dpt[w] * pf, 0, keepdims=True))
                dsb[w] = ds.astype(BF)
                r.bias[w // NWLON] = r.bias[w // NWLON] + ds
            dk = [weigh(dsb[w], qb[w]) * SCALE for w in batch]
            dq = [mix(dsb[w], r.kv[i, w], bounds) * SCALE for w in batch]
            x = r.xv[i, b0 : b0 + BATCH_B].astype(F32).reshape(BATCH_B * WIN, D)
            xhs.append(norm(x)[0].astype(BF))
            os.append(r.ov[i, b0 : b0 + BATCH_B].astype(F32).reshape(BATCH_B * WIN, D).astype(BF))
            r.ov[i, b0 : b0 + BATCH_B] = d1.reshape(BATCH_B, WIN, D).astype(BF)
            d1s.append(d1b)
            for m, (part, parts, keep) in enumerate(((dq, dqs, r.qv), (dk, dks, r.kv), (dv, dvs, r.vv))):
                flat = jnp.concatenate(part, axis=0)
                r.dsum[m : m + 1, :] = r.dsum[m : m + 1, :] + jnp.sum(flat, 0, keepdims=True)
                keep[i, b0 : b0 + BATCH_B] = flat.reshape(BATCH_B, WIN, D).astype(BF)
                parts.append(flat.astype(BF))
        xh = jnp.concatenate(xhs, axis=0)
        for m, part in enumerate((dqs, dks, dvs)):
            r.dwin[m] = r.dwin[m] + dot(xh, jnp.concatenate(part, axis=0), 0, 0)
        r.dwout[...] = r.dwout[...] + dot(jnp.concatenate(os, axis=0), jnp.concatenate(d1s, axis=0), 0, 0)

    def back_before(i):
        s, l = i // L, lax.rem(i, L)

        @pl.when(l == 0)
        def _():
            for c in range(NCH):
                back_own(s * NCH + c).wait()
                for j in range(1, z.nl):
                    back_copy(s * NCH + c, j).wait_recv()

        @pl.when(i == S * L // 2)
        def _():
            sum_cores(1)
            vec = r.g3s[pl.ds(me_t, 1)][0].astype(F32)
            for j in range(1, z.nt):
                norm_tile_copy(j).wait_recv()
                vec = vec + r.g3r[j - 1].astype(F32)
            r.h3s[...] = vec.astype(BF)
            for j in range(1, z.nl):
                norm_lev_copy(j).start()

    def nothing(i):
        pass

    pairs(S * L, back_before, back_step, nothing)

    tall = jnp.concatenate([gain1, shift1, jnp.zeros((126, D), F32)], axis=0)
    tall = jnp.transpose(lane_pad(tall, 256))[:D]
    to_gain, to_shift = 0.0, 0.0
    for i in range(3):
        w, m, c = r.win[i].astype(F32), r.dwin[i], r.dsum[i : i + 1, :]
        to_gain = to_gain + jnp.sum(w * m, 1, keepdims=True)
        to_shift = to_shift + jnp.sum(w * c, 1, keepdims=True)
        r.dwin[i] = tall[:, 0:1] * m + tall[:, 1:2] * c
    lane = lax.broadcasted_iota(jnp.int32, (D, 128), 1)
    flat = jnp.concatenate([jnp.where(lane == 0, to_gain, jnp.where(lane == 1, to_shift, 0.0)), jnp.zeros((256 - D, 128), F32)], axis=0)
    flat = jnp.transpose(flat)
    for t in range(z.nt):
        rows = slice(t * z.rows, (t + 1) * z.rows)
        for i in range(3):
            r.g1s[t, 0 : z.rows, i * D : (i + 1) * D] = r.dwin[i, rows, :].astype(BF)
        r.g1s[t, 0 : z.rows, 3 * D : 4 * D] = r.dwout[rows, :].astype(BF)
        r.g1s[t, z.rpad : z.rpad + 8, :] = lane_pad(flat[0:8, rows], 4 * D).astype(BF)
    core_copy(0).start()
    sum_tiles(1)
    vec = r.h3s[...].astype(F32)
    for j in range(1, z.nl):
        norm_lev_copy(j).wait_recv()
        vec = vec + r.h3r[j - 1].astype(F32)
    r.ovec[...] = vec

    pads = jnp.zeros((WIN, 128 - WIN), F32)
    for b in range(z.bands):
        for h in range(8):
            at = (b * 8 + h) * WIN
            if h < HEADS:
                r.bbuf[at : at + WIN, :] = jnp.concatenate([r.bias[b, :, h * WIN : (h + 1) * WIN], pads], axis=1)
            else:
                r.bbuf[at : at + WIN, :] = jnp.zeros((WIN, 128), F32)
    tab = jnp.zeros((n8, RELP), F32)
    for j in range(0, WIN, 2):
        if j == WIN // 2:
            sum_cores(0)
        both = jnp.concatenate([one_hot(r.idxt, j), one_hot(r.idxt, j + 1)], axis=1)
        pair = jnp.concatenate([r.bbuf[pl.ds(j, n8, stride=WIN), :], r.bbuf[pl.ds(j + 1, n8, stride=WIN), :]], axis=1)
        tab = tab + dot(pair.astype(BF), both, 1, 1)
    for b in range(z.bands):
        r.ts[:, b * RELB : (b + 1) * RELB] = tab[b * 8 : (b + 1) * 8, :RELB].astype(BF)
    tab_core_copy().start()

    def norm_step(i, slot):
        x = r.xv[i].astype(F32).reshape(TOK, D)
        xh, rs = norm(x)
        dn = 0.0
        for m, kept in enumerate((r.qv, r.kv, r.vv)):
            dn = dn + dot(kept[i].astype(F32).reshape(TOK, D).astype(BF), r.win[m], 1, 1)
        dx = norm_back(xh, rs, dn, gain1, False)
        r.xv[i] = (r.ov[i].astype(F32).reshape(TOK, D) + dx).reshape(W, WIN, D).astype(BF)

    def norm_before(i):
        @pl.when(i == 1)
        def _():
            tab_cores()

        @pl.when(i == S * L - 1)
        def _():
            sum_tiles(0)

    def norm_after(i):
        store_x(i).start()

    singles(S * L, norm_before, norm_step, norm_after)

    sum_lev(1, r.osum2)
    for j in range(1, z.nl):
        tab_copy(j).wait_recv()
    sum_halves(r.th, r.tr, r.otab)
    sum_lev(0, r.osum1)
    tab_core_copy().wait_send()
    for i in range(2):
        weight_pass(i).wait_send()
        core_copy(i).wait_send()
        for j in range(1, z.nt):
            weight_copy(i, j).wait_send()
            tile_copy(i, j).wait_send()
        for j in range(1, z.nl):
            lev_copy(i, j).wait_send()
    for j in range(1, z.nt):
        norm_tile_copy(j).wait_send()
    for j in range(1, z.nl):
        norm_lev_copy(j).wait_send()
    for j in range(1, z.nl):
        tab_copy(j).wait_send()
        for i in range(S * L):
            for c in range(NCH):
                stream_copy(i, c, j).wait_send()
        for i in range(S * NCH):
            back_copy(i, j).wait_send()
    for i in range(S * L):
        store_x(i).wait()
    for i in range(S * NCH):
        store_out(i).wait()


def finish_kernel(z, names, pieces, *refs):
    r = Sems()
    for name, ref in zip(names, refs):
        setattr(r, name, ref)
    loads, stores = [], []
    for src, mid, dst in ((r.out0, r.out_mid, r.out), (r.dx0, r.dx_mid, r.dx)):
        n = max(1, src.shape[1] // pieces)
        for s in range(src.shape[0]):
            for p in range(0, src.shape[1], n):
                at = (s, pl.ds(p, n))
                sem = len(stores)
                loads.append(pltpu.make_async_copy(src.at[at], mid.at[at], r.sem.at[0, sem]))
                stores.append(pltpu.make_async_copy(mid.at[at], dst.at[at], r.sem.at[1, sem]))
    parts = ((r.sum1_in, r.sum1), (r.sum2_in, r.sum2), (r.vec_in, r.vec), (r.tab_in, r.tab))
    small = [pltpu.make_async_copy(a, b, r.load_sem.at[i]) for i, (a, b) in enumerate(parts)]
    for c in loads + small:
        c.start()
    for a, b in zip(loads, stores):
        a.wait()
        b.start()
    for c in small:
        c.wait()
    r.owi[...] = r.sum1[0 : z.rows, 0 : 3 * D]
    r.owo[...] = r.sum1[0 : z.rows, 3 * D : 4 * D]
    r.oci[...] = r.sum2[:, 0 : 3 * D]
    r.oco[...] = r.sum2[:, 3 * D : 4 * D]
    r.oew[...] = r.sum2[:, 4 * D : 4 * D + z.FF]
    for i in range(z.FF // D):
        r.orw[i * z.rows : (i + 1) * z.rows, :] = r.sum2[:, 4 * D + z.FF + i * D : 4 * D + z.FF + (i + 1) * D]
    for i, ref in enumerate((r.o0, r.o1, r.o2, r.o3, r.o4, r.o5)):
        ref[...] = r.vec[i : i + 1, 0 : z.rows] if i > 1 else r.sum1[z.rpad + i : z.rpad + i + 1, 0 : z.rows]
    r.otab[...] = r.tab[0:HEADS, 0 : r.otab.shape[1]]
    for c in stores:
        c.wait()


def dma(*shape):
    return pltpu.SemaphoreType.DMA(shape)


def body(mesh, inputs, out_grad, lowest_level, bias_index, first_gain, first_shift, window_in, window_out, earth_bias,
         second_gain, second_shift, column_in, column_out, third_gain, third_shift, expand_weight, reduce_weight):
    z = Sizes(mesh, inputs, out_grad, expand_weight)
    S, L, LV, W, C, CB, NCH, A, FF, nt, nl = z.S, z.L, z.LV, z.W, z.C, z.CB, z.NCH, HEADS * WIN, z.FF, z.nt, z.nl
    lanes = 4 * D + 2 * FF
    tab_lanes = z.bands * RELB
    tab_half = -(-tab_lanes // 256) * 128
    g = out_grad.transpose(0, 1, 3, 2, 4).reshape(S, LV, z.cells * W, D)
    row = lambda a: a.reshape(1, z.rows)
    ins = dict(x=inputs, g=g, lowest=lowest_level, idx=bias_index, tab=earth_bias.T, wi=window_in, wo=window_out,
               ci=column_in, co=column_out, ew=expand_weight, rw=reduce_weight, v0=row(first_gain), v1=row(first_shift),
               v2=row(second_gain), v3=row(second_shift), v4=row(third_gain), v5=row(third_shift))
    outs = dict(out=(g.shape, BF), dx=(inputs.shape, BF), osum1=((z.rpad + 8, 4 * D), F32), osum2=((z.rows, lanes), F32),
                ovec=((8, 128), F32), otab=((8, 2 * tab_half), F32))
    tokens = pltpu.VMEM((S * L, W, WIN, D), BF)
    slabs = ((z.rpad + 8, 4 * D), (z.rows, lanes))
    sums = ((z.rpad + 8, 4 * D), (z.rows, lanes))
    scratch = dict(xv=tokens, qv=tokens, kv=tokens, vv=tokens, ov=tokens, pv=pltpu.VMEM((S * L, W, WIN, A), BF),
                   gv=pltpu.VMEM((S * NCH, LV, C, D), BF), xs=pltpu.VMEM((S * L, nl, NCH, CB, 128), BF),
                   x1r=pltpu.VMEM((S, LV, NCH, CB, 128), BF), ys=pltpu.VMEM((S * NCH, LV, CB, 128), BF),
                   dxr=pltpu.VMEM((S, L, nl, NCH, CB, 128), BF), mid=pltpu.VMEM((2, 2, W * WIN, 128), F32),
                   bias=pltpu.VMEM((z.bands, WIN, A), F32), bbuf=pltpu.VMEM((z.bands * 8 * WIN, 128), F32),
                   idxt=pltpu.VMEM((128, 128), jnp.int32), key=pltpu.VMEM((LV * 8, HEADS * LV * 8), F32),
                   low=pltpu.VMEM((S, W // 8, z.cells, HEADS * LV * 8), F32),
                   wide=pltpu.VMEM((D, lanes), F32), widef=pltpu.VMEM((FF, D), F32), gs=pltpu.VMEM((8, D), F32),
                   win=pltpu.VMEM((3, D, D), BF), wout=pltpu.VMEM((D, D), BF), cin=pltpu.VMEM((3, D, D), BF),
                   cout=pltpu.VMEM((D, D), BF), ewf=pltpu.VMEM((D, FF), BF), rwf=pltpu.VMEM((FF, D), BF),
                   dwin=pltpu.VMEM((3, D, D), F32), dwout=pltpu.VMEM((D, D), F32), dcin=pltpu.VMEM((3, D, D), F32),
                   dcout=pltpu.VMEM((D, D), F32), dew=pltpu.VMEM((D, FF), F32), drw=pltpu.VMEM((FF, D), F32), dgs=pltpu.VMEM((8, D), F32), dsum=pltpu.VMEM((8, D), F32),
                   ts=pltpu.VMEM((8, 2 * tab_half), BF), tt=pltpu.VMEM((8, tab_half), BF), th=pltpu.VMEM((8, tab_half), BF),
                   tr=pltpu.VMEM((nl - 1, 8, tab_half), BF))
    for i, sh in enumerate(slabs):
        scratch.update({f"w{i + 1}s": pltpu.VMEM((1,) + sh, BF), f"w{i + 1}r": pltpu.VMEM((nt,) + sh, BF)})
    for i, (n, m) in enumerate(sums):
        part = (n, m // 2)
        scratch.update({f"g{i + 1}s": pltpu.VMEM((nt, n, m), BF), f"g{i + 1}t": pltpu.VMEM((nt,) + part, BF),
                        f"g{i + 1}h": pltpu.VMEM((nt,) + part, BF), f"g{i + 1}r": pltpu.VMEM((nt - 1,) + part, BF),
                        f"h{i + 1}s": pltpu.VMEM(part, BF), f"h{i + 1}r": pltpu.VMEM((nl - 1,) + part, BF)})
    scratch.update(g3s=pltpu.VMEM((nt, 8, 128), BF), g3r=pltpu.VMEM((nt - 1, 8, 128), BF), h3s=pltpu.VMEM((8, 128), BF),
                   h3r=pltpu.VMEM((nl - 1, 8, 128), BF))
    scratch.update(x_sem=dma(S * L), dx_sem=dma(S * L), g_sem=dma(S * NCH), out_sem=dma(S * NCH), w_send=dma(2, nt - 1), w_recv=dma(2, nt - 1),
                   wt_send=dma(2), wt_recv=dma(2), s_send=dma(S * L * NCH, nl - 1), s_recv=dma(S * L * NCH, nl - 1), s_own=dma(S * L * NCH),
                   b_send=dma(S * NCH, nl - 1), b_recv=dma(S * NCH, nl - 1), b_own=dma(S * NCH),
                   gt_send=dma(2), gt_recv=dma(2), g_send=dma(2, nt - 1), g_recv=dma(2, nt - 1), h_send=dma(2, nl - 1), h_recv=dma(2, nl - 1),
                   tt_send=dma(1), tt_recv=dma(1), t_send=dma(nl - 1), t_recv=dma(nl - 1),
                   n_send=dma(nt - 1), n_recv=dma(nt - 1), m_send=dma(nl - 1), m_recv=dma(nl - 1))
    hbm = ("x", "g", "out", "dx")
    place = lambda name: pl.BlockSpec(memory_space=pl.ANY if name in hbm else pltpu.VMEM)
    done = dict(zip(outs, pl.pallas_call(
        functools.partial(layer_kernel, z, tuple(ins) + tuple(outs) + tuple(scratch)),
        in_specs=[place(name) for name in ins],
        out_specs=[place(name) for name in outs],
        out_shape=[jax.ShapeDtypeStruct(*o) for o in outs.values()],
        scratch_shapes=list(scratch.values()),
        compiler_params=pltpu.CompilerParams(vmem_limit_bytes=VMEM_LIMIT, collective_id=0, has_side_effects=True),
        name="layer",
    )(*ins.values())))
    last_in = dict(out0=done["out"], dx0=done["dx"], sum1_in=done["osum1"], sum2_in=done["osum2"], vec_in=done["ovec"], tab_in=done["otab"])
    last = dict(out=(g.shape, BF), dx=(inputs.shape, BF), owi=((z.rows, 3 * D), F32), owo=((z.rows, D), F32),
                oci=((z.rows, 3 * D), F32), oco=((z.rows, D), F32), oew=((z.rows, FF), F32), orw=((z.frows, D), F32),
                otab=((HEADS, tab_lanes), F32), **{f"o{i}": ((1, z.rows), F32) for i in range(6)})
    pieces = 1
    place = lambda name: pl.BlockSpec(memory_space=pl.ANY if name in last_in or name in ("out", "dx") else pltpu.VMEM)
    held = dict(sum1=done["osum1"], sum2=done["osum2"], vec=done["ovec"], tab=done["otab"])
    end = dict(zip(last, pl.pallas_call(
        functools.partial(finish_kernel, z, tuple(last_in) + tuple(last) + tuple(held) + ("out_mid", "dx_mid", "sem", "load_sem"), pieces),
        in_specs=[place(name) for name in last_in],
        out_specs=[place(name) for name in last],
        out_shape=[jax.ShapeDtypeStruct(*o) for o in last.values()],
        scratch_shapes=[pltpu.VMEM(a.shape, F32) for a in held.values()] + [pltpu.VMEM(g.shape, BF), pltpu.VMEM(inputs.shape, BF), dma(2, 4 * S * pieces), dma(4)],
        compiler_params=pltpu.CompilerParams(vmem_limit_bytes=VMEM_LIMIT),
        name="finish",
    )(*last_in.values())))
    output = end["out"].reshape(S, LV, z.cells, W, D).transpose(0, 1, 3, 2, 4)
    v = [end[f"o{i}"].reshape(z.rows) for i in range(6)]
    return (output, end["dx"], v[0], v[1], end["owi"], end["owo"], end["otab"].T, v[2], v[3],
            end["oci"], end["oco"], v[4], v[5], end["oew"], end["orw"])


def solution(mesh):
    t, t2 = P("tile"), P("tile", None)
    level_tokens = P(None, "lev", "tile", None, None)
    column_tokens = P(None, None, "tile", "lev", None)
    placed = (level_tokens, column_tokens, P(None, "tile", "lev"), P(), t, t, t2, t2, t2, t, t, t2, t2, t, t, t2, t2)
    outs = (column_tokens, level_tokens, t, t, t2, t2, t2, t, t, t2, t2, t, t, t2, t2)
    return jax.shard_map(functools.partial(body, mesh), mesh=mesh, in_specs=placed, out_specs=outs, check_vma=False)
```

```python
import functools

import jax
import jax.numpy as jnp
from jax import lax
from jax.experimental import pallas as pl
from jax.experimental.pallas import tpu as pltpu
from jax.sharding import PartitionSpec as P

HEADS = 6
HEAD_DIM = 32
D = HEADS * HEAD_DIM
WIN = 72
RELB = 828
RELP = 832
NWLON = 2
EPSILON = 1e-05
SCALE = HEAD_DIM ** (-0.5)
LOG2E = 1.4426950408889634
MASKED = -1e30
F32 = jnp.float32
BF = jnp.bfloat16
MESH = pl.DeviceIdType.MESH
VMEM_LIMIT = 60 << 20
BATCH_F, BATCH_C, BATCH_B = 8, 12, 8


def dot(a, b, ca=1, cb=0):
    return lax.dot_general(a, b, (((ca,), (cb,)), ((), ())), preferred_element_type=F32)


def lane_heads():
    lane = lax.broadcasted_iota(jnp.int32, (1, 128), 1)
    return [(lane // HEAD_DIM == h).astype(F32) for h in range(4)], [lane < HEAD_DIM * (h + 1) for h in range(3)]


def spread(v, marks, factor=None):
    n = v.shape[0]
    low, high = v[:, :128], v[:, 128:]
    tops = [m if factor is None else m * factor for m in marks]
    if n == 64:
        low, high = low.astype(BF), high.astype(BF)
        tops = [m.astype(BF) for m in tops]
        first = jnp.concatenate([low * m for m in tops], axis=0)
        return first, jnp.concatenate([high * m[:, :64] for m in tops[:2]], axis=0)
    parts = [low * m for m in tops]
    cut = 256 - 3 * n
    first = jnp.concatenate(parts[:3] + [parts[3][:cut]], axis=0).astype(BF)
    head3 = jnp.concatenate([parts[3][cut:], jnp.zeros((n - cut, 64), F32)], axis=1)
    blank = jnp.zeros((n, 128), F32)
    rest = [jnp.concatenate([blank, high * m[:, :64]], axis=1) for m in tops[:2]]
    return first, jnp.concatenate([head3] + rest, axis=0).astype(BF)


def scores(k, spread_q):
    first, rest = spread_q
    right = k[:, 128:] if rest.shape[1] == 64 else k
    return jnp.concatenate([dot(k[:, :128], first, 1, 1), dot(right, rest, 1, 1)], axis=1)


def weigh(p, spread_v):
    first, rest = spread_v
    low, high = dot(p[:, :256], first), dot(p[:, 256:], rest)
    if rest.shape[1] == 64:
        return jnp.concatenate([low, high], axis=1)
    return jnp.concatenate([low + high[:, :128], high[:, 128:]], axis=1)


def mix(p, v, bounds):
    n = v.shape[0]
    first = dot(p[:, :256], v[:, :128], 0, 0)
    if n == 64:
        rest = dot(p[:, 256:], v[:, 128:], 0, 0)
        head3, tail = first[3 * n :], rest
    else:
        rest = dot(p[:, 256:], v, 0, 0)
        cut = 4 * n - 256
        head3, tail = jnp.concatenate([first[3 * n :], rest[:cut, :128]], axis=0), rest[cut:, 128:]
    low = jnp.where(bounds[0], first[:n], jnp.where(bounds[1], first[n : 2 * n], jnp.where(bounds[2], first[2 * n : 3 * n], head3)))
    high = jnp.where(bounds[0][:, :64], tail[:n], tail[n:])
    return jnp.concatenate([low, high], axis=1)


def norm(x):
    mean = jnp.sum(x, -1, keepdims=True) * (1.0 / D)
    c = x - mean
    var = jnp.sum(c * c, -1, keepdims=True) * (1.0 / D)
    r = lax.rsqrt(var + EPSILON)
    return c * r, r


def norm_back(xh, r, dn, gain, sums=True):
    t = dn * gain
    a = jnp.sum(t, -1, keepdims=True) * (1.0 / D)
    b = jnp.sum(t * xh, -1, keepdims=True) * (1.0 / D)
    dx = r * (t - a - xh * b)
    if not sums:
        return dx
    return dx, jnp.sum(dn * xh, 0, keepdims=True), jnp.sum(dn, 0, keepdims=True)


def softmax2(st):
    e = jnp.exp2(st - jnp.max(st, 0, keepdims=True))
    return e * (1.0 / jnp.sum(e, 0, keepdims=True))


def moved(rows, by):
    if isinstance(rows, slice):
        return slice(rows.start + by, rows.stop + by)
    return pl.ds(rows.start + by, rows.size, stride=rows.stride)


def put(ref, base, tall, rows, v):
    n = v.shape[0]
    ref[moved(rows, base), :] = v[:, :128]
    ref[moved(rows, base + tall), :] = jnp.concatenate([v[:, 128:], jnp.zeros((n, 256 - D), F32)], axis=1)


def take(ref, base, tall, rows):
    return jnp.concatenate([ref[moved(rows, base), :], ref[moved(rows, base + tall), :][:, : D - 128]], axis=1)


def fold(ref, at, v):
    c = v.shape[0]
    ref[at + (slice(0, c),)] = v[:, :128].astype(BF)
    tail = jnp.concatenate([v[: c // 2, 128:], v[c // 2 :, 128:]], axis=1)
    ref[at + (slice(c, c + c // 2),)] = tail.astype(BF)


def unfold(block):
    c = block.shape[0] * 2 // 3
    wide = block.astype(F32)
    tail = wide[c:]
    return jnp.concatenate([wide[:c], jnp.concatenate([tail[:, :64], tail[:, 64:]], axis=0)], axis=1)


def one_hot(idx_ref, j):
    entry = lax.broadcasted_iota(jnp.int32, (RELP, 128), 0)
    return (entry == idx_ref[j : j + 1, :]).astype(F32).astype(BF)


def announce(axes):
    sem = pltpu.get_barrier_semaphore()
    count = 0
    for axis, size in axes:
        me = lax.axis_index(axis)
        for j in range(1, size):
            pl.semaphore_signal(sem, inc=1, device_id={axis: lax.rem(me + j, size)}, device_id_type=MESH)
            count += 1
    return sem, count


def to_peer(axis, size, j, src, dst, send, recv):
    me = lax.axis_index(axis)
    return pltpu.make_async_remote_copy(
        src_ref=src, dst_ref=dst, send_sem=send, recv_sem=recv,
        device_id={axis: lax.rem(me + j, size)}, device_id_type=MESH,
    )


def rows_to_lanes(m, n):
    return jnp.concatenate([m[i : i + n] for i in range(0, m.shape[0], n)], axis=1)


class Sizes:
    def __init__(self, mesh, inputs, out_grad, expand):
        self.nl = mesh.shape["lev"]
        self.nt = mesh.shape["tile"]
        self.S, self.L, self.W = inputs.shape[:3]
        self.LV = out_grad.shape[1]
        self.cells = out_grad.shape[3]
        self.bands = self.W // NWLON
        self.rows = D // self.nt
        self.rpad = -(-self.rows // 8) * 8
        self.FF = expand.shape[1]
        self.frows = self.FF // self.nt
        self.T = 6 if self.cells % 6 == 0 else 3
        self.NCH = self.cells // self.T
        self.C = self.T * self.W
        self.CB = self.C * 3 // 2


def lane_pad(m, width, value=0.0):
    if m.shape[1] == width:
        return m
    return jnp.concatenate([m, jnp.full((m.shape[0], width - m.shape[1]), value, F32)], axis=1)


def pairs(count, before, step, after):
    def two(i, _):
        for k in range(2):
            before(2 * i + k)
        for k in range(2):
            step(2 * i + k, k)
        for k in range(2):
            after(2 * i + k)
        return 0

    lax.fori_loop(0, count // 2, two, 0)


def singles(count, before, step, after):
    def one(i, _):
        before(i)
        step(i, 0)
        after(i)
        return 0

    lax.fori_loop(0, count, one, 0)


class Sems:
    pass


def layer_kernel(z, names, *refs):
    r = Sems()
    for name, ref in zip(names, refs):
        setattr(r, name, ref)
    me_l, me_t = lax.axis_index("lev"), lax.axis_index("tile")
    S, L, LV, W, C, NCH = z.S, z.L, z.LV, z.W, z.C, z.NCH
    TOK = W * WIN
    TABH = r.th.shape[-1]
    marks, bounds = lane_heads()

    def load_x(i):
        return pltpu.make_async_copy(r.x.at[i // L, lax.rem(i, L)], r.xv.at[i], r.x_sem.at[i])

    def store_x(i):
        return pltpu.make_async_copy(r.xv.at[i], r.dx.at[i // L, lax.rem(i, L)], r.dx_sem.at[i])

    def load_g(i):
        rows = pl.ds(pl.multiple_of(lax.rem(i, NCH) * C, 16), C)
        return pltpu.make_async_copy(r.g.at[i // NCH, :, rows, :], r.gv.at[i], r.g_sem.at[i])

    def store_out(i):
        rows = pl.ds(pl.multiple_of(lax.rem(i, NCH) * C, 16), C)
        return pltpu.make_async_copy(r.gv.at[i], r.out.at[i // NCH, :, rows, :], r.out_sem.at[i])

    core, twin = lax.rem(me_l, 2), me_l + 1 - 2 * lax.rem(me_l, 2)

    def to_twin(src, dst, send, recv):
        return pltpu.make_async_remote_copy(src_ref=src, dst_ref=dst, send_sem=send, recv_sem=recv,
                                            device_id={"lev": twin}, device_id_type=MESH)

    def half(ref, which):
        width = ref.shape[-1] // 2
        return ref.at[:, :, pl.ds(pl.multiple_of(which * width, 128), width)]

    weights = ((r.w1s, r.w1r), (r.w2s, r.w2r))

    def weight_copy(i, j):
        src, dst = weights[i]
        return to_peer("tile", z.nt, j, half(src, core).at[0], half(dst, core).at[me_t], r.w_send.at[i, j - 1], r.w_recv.at[i, j - 1])

    def weight_pass(i):
        part = half(weights[i][1], core)
        return to_twin(part, part, r.wt_send.at[i], r.wt_recv.at[i])

    def weight_start(i):
        for j in range(1, z.nt):
            weight_copy(i, j).start()
        src, dst = weights[i]
        width = src.shape[-1] // 2
        own = pl.ds(pl.multiple_of(core * width, 128), width)
        dst[pl.ds(me_t, 1), :, own] = src[:, :, own]

    def weight_hand(i):
        for j in range(1, z.nt):
            weight_copy(i, j).wait_recv()
        weight_pass(i).start()

    def stream_copy(i, c, j):
        return to_peer("lev", z.nl, j, r.xs.at[i, lax.rem(me_l + j, z.nl), c], r.x1r.at[i // L, me_l * L + lax.rem(i, L), c],
                       r.s_send.at[i * NCH + c, j - 1], r.s_recv.at[i * NCH + c, j - 1])

    def stream_own(i, c):
        return pltpu.make_async_copy(r.xs.at[i, me_l, c], r.x1r.at[i // L, me_l * L + lax.rem(i, L), c], r.s_own.at[i * NCH + c])

    def back_copy(i, j):
        return to_peer("lev", z.nl, j, r.ys.at[i, pl.ds(lax.rem(me_l + j, z.nl) * L, L)],
                       r.dxr.at[i // NCH, :, me_l, lax.rem(i, NCH)], r.b_send.at[i, j - 1], r.b_recv.at[i, j - 1])

    def back_own(i):
        return pltpu.make_async_copy(r.ys.at[i, pl.ds(me_l * L, L)], r.dxr.at[i // NCH, :, me_l, lax.rem(i, NCH)], r.b_own.at[i])

    grads = ((r.g1s, r.g1t, r.g1h, r.g1r, r.h1s, r.h1r), (r.g2s, r.g2t, r.g2h, r.g2r, r.h2s, r.h2r))

    def core_copy(i):
        return to_twin(half(grads[i][0], 1 - core), grads[i][1], r.gt_send.at[i], r.gt_recv.at[i])

    def tile_copy(i, j):
        src, dst = grads[i][2], grads[i][3]
        return to_peer("tile", z.nt, j, src.at[lax.rem(me_t + j, z.nt)], dst.at[j - 1], r.g_send.at[i, j - 1], r.g_recv.at[i, j - 1])

    def lev_copy(i, j):
        return to_peer("lev", z.nl, j, grads[i][4], grads[i][5].at[j - 1], r.h_send.at[i, j - 1], r.h_recv.at[i, j - 1])

    def sum_cores(i):
        core_copy(i).wait_recv()
        gs, gt, gh = grads[i][:3]
        width = gt.shape[-1]
        mine = gs[:, :, pl.ds(pl.multiple_of(core * width, 128), width)]
        gh[...] = (mine.astype(F32) + gt[...].astype(F32)).astype(BF)
        for j in range(1, z.nt):
            tile_copy(i, j).start()

    def sum_tiles(i):
        gh, gr, hs = grads[i][2:5]
        total = gh[pl.ds(me_t, 1)][0].astype(F32)
        for j in range(1, z.nt):
            tile_copy(i, j).wait_recv()
            total = total + gr[j - 1].astype(F32)
        hs[...] = total.astype(BF)
        for j in range(1, z.nl):
            lev_copy(i, j).start()

    def sum_halves(own, got, out):
        mine, other = own[...].astype(F32), 0.0
        for j in range(1, z.nl):
            if j % 2 == 0:
                mine = mine + got[j - 1].astype(F32)
            else:
                other = other + got[j - 1].astype(F32)
        width = own.shape[-1]
        first = core == 0
        out[:, 0:width] = jnp.where(first, mine, other)
        out[:, width : 2 * width] = jnp.where(first, other, mine)

    def sum_lev(i, out):
        for j in range(1, z.nl):
            lev_copy(i, j).wait_recv()
        sum_halves(grads[i][4], grads[i][5], out)

    def leave(i):
        src, dst = ((r.sum1, r.osum1), (r.sum2, r.osum2), (r.vecv, r.ovec), (r.tabv, r.otab))[i]
        return pltpu.make_async_copy(src, dst, r.o_sem.at[i])

    def tab_core_copy():
        part = r.ts.at[:, pl.ds(pl.multiple_of((1 - core) * TABH, 128), TABH)]
        return to_twin(part, r.tt, r.tt_send.at[0], r.tt_recv.at[0])

    def tab_cores():
        tab_core_copy().wait_recv()
        mine = r.ts[:, pl.ds(pl.multiple_of(core * TABH, 128), TABH)]
        r.th[...] = (mine.astype(F32) + r.tt[...].astype(F32)).astype(BF)
        for j in range(1, z.nl):
            tab_copy(j).start()

    def tab_copy(j):
        return to_peer("lev", z.nl, j, r.th, r.tr.at[j - 1], r.t_send.at[j - 1], r.t_recv.at[j - 1])

    def norm_tile_copy(j):
        return to_peer("tile", z.nt, j, r.g3s.at[lax.rem(me_t + j, z.nt)], r.g3r.at[j - 1], r.n_send.at[j - 1], r.n_recv.at[j - 1])

    def norm_lev_copy(j):
        return to_peer("lev", z.nl, j, r.h3s, r.h3r.at[j - 1], r.m_send.at[j - 1], r.m_recv.at[j - 1])

    sem, count = announce((("lev", z.nl), ("tile", z.nt)))
    for i in range(S * L):
        load_x(i).start()
    for i in range(S * NCH):
        load_g(i).start()
    r.w1s[...] = jnp.zeros(r.w1s.shape, BF)
    r.w1s[0, 0 : z.rows, 0 : 3 * D] = r.wi[...]
    r.w1s[0, 0 : z.rows, 3 * D : 4 * D] = r.wo[...]
    for i, vec in enumerate((r.v0, r.v1, r.v2, r.v3, r.v4, r.v5)):
        r.w1s[0, z.rpad + i : z.rpad + i + 1, 0 : z.rows] = vec[...]
    r.w2s[0, :, 0 : 3 * D] = r.ci[...]
    r.w2s[0, :, 3 * D : 4 * D] = r.co[...]
    r.w2s[0, :, 4 * D : 4 * D + z.FF] = r.ew[...]
    r.w2s[0, :, 4 * D + z.FF :] = rows_to_lanes(r.rw[...].astype(F32), z.rows).astype(BF)
    entries = lane_pad(r.idx[...].astype(F32), 128, -1.0)
    entries = jnp.concatenate([entries, jnp.full((128 - WIN, 128), -1.0, F32)], axis=0)
    r.idxt[...] = jnp.transpose(entries).astype(jnp.int32)
    cells8 = lax.broadcasted_iota(jnp.int32, (LV * 8, HEADS * LV * 8), 0)
    lane8 = lax.broadcasted_iota(jnp.int32, (LV * 8, HEADS * LV * 8), 1)
    r.key[...] = jnp.where(cells8 % 8 == lane8 % 8, (cells8 // 8).astype(F32), -1.0)
    wrow = lax.broadcasted_iota(jnp.int32, (W, HEADS * LV * 8), 0)
    wlane = lax.broadcasted_iota(jnp.int32, (W, HEADS * LV * 8), 1)
    for part in range(W // 8):
        pick = (wrow == wlane % 8 + 8 * part).astype(F32).astype(BF)
        for s in range(S):
            r.low[s, part] = dot(r.lowest[s].astype(F32).astype(BF), pick, 0, 0)
    r.ts[...] = jnp.zeros(r.ts.shape, BF)
    pl.semaphore_wait(sem, count)
    weight_start(0)
    table = r.tab[...].astype(F32)
    pads = jnp.zeros((8 - HEADS, RELP), F32)
    table = jnp.concatenate(
        [jnp.concatenate([lane_pad(table[:, b * RELB : (b + 1) * RELB], RELP), pads], axis=0) for b in range(z.bands)], axis=0
    ).astype(BF)
    n8 = z.bands * 8
    for j in range(0, WIN, 2):
        both = jnp.concatenate([one_hot(r.idxt, j), one_hot(r.idxt, j + 1)], axis=1)
        vals = dot(table, both) * LOG2E
        r.bbuf[pl.ds(j, n8, stride=WIN), :] = vals[:, :128]
        r.bbuf[pl.ds(j + 1, n8, stride=WIN), :] = vals[:, 128:]
    def normalize(i, _):
        load_x(i).wait()
        r.xhv[i] = norm(r.xv[i].astype(F32).reshape(TOK, D))[0].reshape(W, WIN, D).astype(BF)
        return 0

    lax.fori_loop(0, S * L // 2, normalize, 0)
    weight_hand(0)
    weight_start(1)
    lax.fori_loop(S * L // 2, S * L, normalize, 0)
    for b in range(z.bands):
        r.bias[b] = jnp.concatenate(
            [r.bbuf[(b * 8 + h) * WIN : (b * 8 + h + 1) * WIN, :][:, :WIN] for h in range(HEADS)], axis=1
        )
    for ref in (r.dcin, r.dcout, r.dew, r.drw, r.dwin, r.dwout, r.dgs, r.dsum):
        ref[...] = jnp.zeros(ref.shape, F32)
    weight_pass(0).wait_recv()
    for t in range(z.nt):
        r.wide[t * z.rows : (t + 1) * z.rows, 0 : 4 * D] = r.w1r[t, 0 : z.rows, :].astype(F32)
    for i in range(3):
        r.win[i] = r.wide[:, i * D : (i + 1) * D].astype(BF)
    r.wout[...] = r.wide[:, 3 * D : 4 * D].astype(BF)
    r.gs[...] = jnp.concatenate([r.w1r[t, z.rpad : z.rpad + 8, :].astype(F32)[:, : z.rows] for t in range(z.nt)], axis=1)
    gain1, shift1, g2, s2, g3, s3 = (r.gs[i : i + 1, :] for i in range(6))

    def window_step(i, slot):
        n1 = (r.xhv[i].astype(F32).reshape(TOK, D) * gain1 + shift1).astype(BF)
        q, k, v = (dot(n1, r.win[m]) for m in range(3))
        mixed = []
        for b0 in range(0, W, BATCH_F):
            batch = range(b0, b0 + BATCH_F)
            cut = {w: slice(w * WIN, (w + 1) * WIN) for w in batch}
            kb = {w: k[cut[w]].astype(BF) for w in batch}
            vb = {w: v[cut[w]].astype(BF) for w in batch}
            for w in batch:
                r.qv[i, w] = q[cut[w]].astype(BF)
                r.kv[i, w] = kb[w]
                r.vv[i, w] = vb[w]
            sq = {w: spread(q[cut[w]], marks, SCALE * LOG2E) for w in batch}
            st = {w: scores(kb[w], sq[w]) + r.bias[w // NWLON] for w in batch}
            pb = {w: softmax2(st[w]).astype(BF) for w in batch}
            for w in batch:
                r.pv[i, w] = pb[w]
            mixed += [mix(pb[w], vb[w], bounds) for w in batch]
        o = jnp.concatenate(mixed, axis=0).astype(BF)
        r.ov[i] = o.astype(F32).reshape(W, WIN, D).astype(BF)
        x1 = r.xv[i].astype(F32).reshape(TOK, D) + dot(o, r.wout[...])
        for w in range(W):
            put(r.bbuf, 2 * TOK * slot, TOK, pl.ds(w, WIN, stride=W), x1[w * WIN : (w + 1) * WIN])
        for d in range(z.nl):
            for c in range(NCH):
                at = (d * NCH + c) * C
                fold(r.xs, (i, d, c), take(r.bbuf, 2 * TOK * slot, TOK, slice(at, at + C)))

    def window_before(i):
        @pl.when(i == S * L - 1)
        def _():
            weight_hand(1)

    def window_after(i):
        for c in range(NCH):
            for j in range(1, z.nl):
                stream_copy(i, c, j).start()
            stream_own(i, c).start()

    singles(S * L, window_before, window_step, window_after)

    weight_pass(1).wait_recv()
    for t in range(z.nt):
        r.wide[t * z.rows : (t + 1) * z.rows, :] = r.w2r[t].astype(F32)
        for i in range(z.FF // D):
            at = t * z.frows + i * z.rows
            r.widef[at : at + z.rows, :] = r.w2r[t].astype(F32)[:, 4 * D + z.FF + i * D : 4 * D + z.FF + (i + 1) * D]
    for i in range(3):
        r.cin[i] = r.wide[:, i * D : (i + 1) * D].astype(BF)
    r.cout[...] = r.wide[:, 3 * D : 4 * D].astype(BF)
    r.ewf[...] = r.wide[:, 4 * D : 4 * D + z.FF].astype(BF)
    r.rwf[...] = r.widef[...].astype(BF)
    r.bias[...] = jnp.zeros(r.bias.shape, F32)

    groups, R, GR = C // 8, LV * C, LV * 8
    halves = W // 8

    def cols(m, j):
        return m.reshape(LV, C, D)[:, j * 8 : (j + 1) * 8, :].reshape(GR, D)

    def join(parts):
        return jnp.concatenate([p.reshape(LV, 8, D) for p in parts], axis=1).reshape(R, D)

    def column_step(i, slot):
        s, ch = i // NCH, lax.rem(i, NCH)

        x1 = jnp.concatenate([unfold(r.x1r[s, m, ch]) for m in range(LV)], axis=0)
        xh2, r2 = norm(x1)
        n2 = (xh2 * g2 + s2).astype(BF)
        q, k, v = (dot(n2, r.cin[m]) for m in range(3))
        key = r.key[...]
        mixed = []
        qb, kb, vb, pb = {}, {}, {}, {}
        for b0 in range(0, groups, BATCH_C):
            batch = range(b0, min(b0 + BATCH_C, groups))
            for j in batch:
                kb[j], vb[j] = cols(k, j).astype(BF), cols(v, j).astype(BF)
                qb[j] = spread(cols(q, j), marks, SCALE * LOG2E)
            st = {j: scores(kb[j], qb[j]) for j in batch}
            for j in batch:
                low = r.low[s, j % halves, pl.ds(ch * z.T + j // halves, 1), :]
                pb[j] = softmax2(jnp.where(key >= low, st[j], MASKED)).astype(BF)
            mixed += [mix(pb[j], vb[j], bounds) for j in batch]
        o2 = join(mixed).astype(BF)
        x2 = x1 + dot(o2, r.cout[...])
        xh3, r3 = norm(x2)
        n3 = (xh3 * g3 + s3).astype(BF)
        gb = r.gv[i].astype(F32).reshape(R, D).astype(BF)
        u = dot(n3, r.ewf[...] * 0.5).astype(BF)
        dh = dot(gb, r.rwf[...] * 0.5, 1, 1).astype(BF)
        c = 0.7978845608028654
        a = BF(2 * c) + BF(8 * c * 0.044715) * (u * u)
        t = jnp.tanh(u * a)
        up = BF(1.0) + t
        hid = u * up
        du = dh * (up + hid * (BF(1.0) - t) * (BF(3.0) * a - BF(4.0 * c)))
        dn3 = dot(du, r.ewf[...], 1, 1)
        dx, a3, b3 = norm_back(xh3, r3, dn3, g3)
        dx2 = gb.astype(F32) + dx
        dx2b = dx2.astype(BF)
        r.gv[i] = (x2 + dot(hid, r.rwf[...])).reshape(LV, C, D).astype(BF)
        r.drw[...] = r.drw[...] + dot(hid, gb, 0, 0)
        r.dew[...] = r.dew[...] + dot(n3, du, 0, 0)
        r.dcout[...] = r.dcout[...] + dot(o2, dx2b, 0, 0)
        do = dot(dx2b, r.cout[...], 1, 1)
        dq, dk, dv = [], [], []
        for b0 in range(0, groups, BATCH_C):
            batch = range(b0, min(b0 + BATCH_C, groups))
            dob = {j: spread(cols(do, j), marks) for j in batch}
            dpt = {j: scores(vb[j], dob[j]) for j in batch}
            dv += [weigh(pb[j], dob[j]) for j in batch]
            dsb = {}
            for j in batch:
                pf = pb[j].astype(F32)
                dsb[j] = (pf * (dpt[j] - jnp.sum(dpt[j] * pf, 0, keepdims=True))).astype(BF)
            dk += [weigh(dsb[j], qb[j]) * (1.0 / LOG2E) for j in batch]
            dq += [mix(dsb[j], kb[j], bounds) * SCALE for j in batch]
        dn2 = 0.0
        packs = [join(part).astype(BF) for part in (dq, dk, dv)]
        for m, pack in enumerate(packs):
            dn2 = dn2 + dot(pack, r.cin[m], 1, 1)
        dx, a2, b2 = norm_back(xh2, r2, dn2, g2)
        for m, pack in enumerate(packs):
            r.dcin[m] = r.dcin[m] + dot(n2, pack, 0, 0)
        dx1 = dx2 + dx
        for m in range(LV):
            fold(r.ys, (i, m), dx1[m * C : (m + 1) * C])
        for m, part in enumerate((a2, b2, a3, b3)):
            r.dgs[m + 2 : m + 3, :] = r.dgs[m + 2 : m + 3, :] + part

    def column_before(i):
        s, ch = i // NCH, lax.rem(i, NCH)
        load_g(i).wait()
        for l in range(L):
            stream_own(s * L + l, ch).wait()
            for j in range(1, z.nl):
                stream_copy(s * L + l, ch, j).wait_recv()

    def column_after(i):
        store_out(i).start()
        for j in range(1, z.nl):
            back_copy(i, j).start()
        back_own(i).start()

    pairs(S * NCH, column_before, column_step, column_after)

    for t in range(z.nt):
        rows = slice(t * z.rows, (t + 1) * z.rows)
        for i in range(3):
            r.g2s[t, :, i * D : (i + 1) * D] = r.dcin[i, rows, :].astype(BF)
        r.g2s[t, :, 3 * D : 4 * D] = r.dcout[rows, :].astype(BF)
        r.g2s[t, :, 4 * D : 4 * D + z.FF] = r.dew[rows, :].astype(BF)
        r.g2s[t, :, 4 * D + z.FF :] = rows_to_lanes(r.drw[t * z.frows : (t + 1) * z.frows, :], z.rows).astype(BF)
    core_copy(1).start()
    for t in range(z.nt):
        r.g3s[t] = lane_pad(r.dgs[:, t * z.rows : (t + 1) * z.rows], 128).astype(BF)
    for j in range(1, z.nt):
        norm_tile_copy(j).start()

    def back_step(i, slot):
        s, l = i // L, lax.rem(i, L)

        for d in range(z.nl):
            for c in range(NCH):
                at = (d * NCH + c) * C
                put(r.bbuf, 2 * TOK * slot, TOK, slice(at, at + C), unfold(r.dxr[s, l, d, c]))
        xhs, dqs, dks, dvs, d1s, os = [], [], [], [], [], []
        for b0 in range(0, W, BATCH_B):
            batch = range(b0, b0 + BATCH_B)
            d1 = jnp.concatenate([take(r.bbuf, 2 * TOK * slot, TOK, pl.ds(w, WIN, stride=W)) for w in batch], axis=0)
            d1b = d1.astype(BF)
            do = dot(d1b, r.wout[...], 1, 1)
            dob = {w: spread(do[(w - b0) * WIN : (w - b0 + 1) * WIN], marks) for w in batch}
            qb = {w: spread(r.qv[i, w].astype(F32), marks) for w in batch}
            dpt = {w: scores(r.vv[i, w], dob[w]) for w in batch}
            dv = [weigh(r.pv[i, w], dob[w]) for w in batch]
            dsb = {}
            for w in batch:
                pf = r.pv[i, w].astype(F32)
                ds = pf * (dpt[w] - jnp.sum(dpt[w] * pf, 0, keepdims=True))
                dsb[w] = ds.astype(BF)
                r.bias[w // NWLON] = r.bias[w // NWLON] + ds
            dk = [weigh(dsb[w], qb[w]) * SCALE for w in batch]
            dq = [mix(dsb[w], r.kv[i, w], bounds) * SCALE for w in batch]
            xhs.append(r.xhv[i, b0 : b0 + BATCH_B].astype(F32).reshape(BATCH_B * WIN, D).astype(BF))
            os.append(r.ov[i, b0 : b0 + BATCH_B].astype(F32).reshape(BATCH_B * WIN, D).astype(BF))
            r.ov[i, b0 : b0 + BATCH_B] = d1.reshape(BATCH_B, WIN, D).astype(BF)
            d1s.append(d1b)
            for m, (part, parts, keep) in enumerate(((dq, dqs, r.qv), (dk, dks, r.kv), (dv, dvs, r.vv))):
                flat = jnp.concatenate(part, axis=0)
                r.dsum[m : m + 1, :] = r.dsum[m : m + 1, :] + jnp.sum(flat, 0, keepdims=True)
                keep[i, b0 : b0 + BATCH_B] = flat.reshape(BATCH_B, WIN, D).astype(BF)
                parts.append(flat.astype(BF))
        xh = jnp.concatenate(xhs, axis=0)
        for m, part in enumerate((dqs, dks, dvs)):
            r.dwin[m] = r.dwin[m] + dot(xh, jnp.concatenate(part, axis=0), 0, 0)
        r.dwout[...] = r.dwout[...] + dot(jnp.concatenate(os, axis=0), jnp.concatenate(d1s, axis=0), 0, 0)

    def back_before(i):
        s, l = i // L, lax.rem(i, L)

        @pl.when(l == 0)
        def _():
            for c in range(NCH):
                back_own(s * NCH + c).wait()
                for j in range(1, z.nl):
                    back_copy(s * NCH + c, j).wait_recv()

        @pl.when(i == S * L // 2)
        def _():
            sum_cores(1)
            vec = r.g3s[pl.ds(me_t, 1)][0].astype(F32)
            for j in range(1, z.nt):
                norm_tile_copy(j).wait_recv()
                vec = vec + r.g3r[j - 1].astype(F32)
            r.h3s[...] = vec.astype(BF)
            for j in range(1, z.nl):
                norm_lev_copy(j).start()

    def nothing(i):
        pass

    pairs(S * L, back_before, back_step, nothing)

    tall = jnp.concatenate([gain1, shift1, jnp.zeros((126, D), F32)], axis=0)
    tall = jnp.transpose(lane_pad(tall, 256))[:D]
    to_gain, to_shift = 0.0, 0.0
    for i in range(3):
        w, m, c = r.win[i].astype(F32), r.dwin[i], r.dsum[i : i + 1, :]
        to_gain = to_gain + jnp.sum(w * m, 1, keepdims=True)
        to_shift = to_shift + jnp.sum(w * c, 1, keepdims=True)
        r.dwin[i] = tall[:, 0:1] * m + tall[:, 1:2] * c
    lane = lax.broadcasted_iota(jnp.int32, (D, 128), 1)
    flat = jnp.concatenate([jnp.where(lane == 0, to_gain, jnp.where(lane == 1, to_shift, 0.0)), jnp.zeros((256 - D, 128), F32)], axis=0)
    flat = jnp.transpose(flat)
    for t in range(z.nt):
        rows = slice(t * z.rows, (t + 1) * z.rows)
        for i in range(3):
            r.g1s[t, 0 : z.rows, i * D : (i + 1) * D] = r.dwin[i, rows, :].astype(BF)
        r.g1s[t, 0 : z.rows, 3 * D : 4 * D] = r.dwout[rows, :].astype(BF)
        r.g1s[t, z.rpad : z.rpad + 8, :] = lane_pad(flat[0:8, rows], 4 * D).astype(BF)
    core_copy(0).start()
    vec = r.h3s[...].astype(F32)
    for j in range(1, z.nl):
        norm_lev_copy(j).wait_recv()
        vec = vec + r.h3r[j - 1].astype(F32)
    r.vecv[...] = vec
    leave(2).start()

    pads = jnp.zeros((WIN, 128 - WIN), F32)
    for b in range(z.bands):
        for h in range(8):
            at = (b * 8 + h) * WIN
            if h < HEADS:
                r.bbuf[at : at + WIN, :] = jnp.concatenate([r.bias[b, :, h * WIN : (h + 1) * WIN], pads], axis=1)
            else:
                r.bbuf[at : at + WIN, :] = jnp.zeros((WIN, 128), F32)
    tab = jnp.zeros((n8, RELP), F32)
    for j in range(0, WIN, 2):
        if j == WIN // 3:
            sum_cores(0)
        if j == 2 * WIN // 3:
            sum_tiles(1)
        both = jnp.concatenate([one_hot(r.idxt, j), one_hot(r.idxt, j + 1)], axis=1)
        pair = jnp.concatenate([r.bbuf[pl.ds(j, n8, stride=WIN), :], r.bbuf[pl.ds(j + 1, n8, stride=WIN), :]], axis=1)
        tab = tab + dot(pair.astype(BF), both, 1, 1)
    for b in range(z.bands):
        r.ts[:, b * RELB : (b + 1) * RELB] = tab[b * 8 : (b + 1) * 8, :RELB].astype(BF)
    tab_core_copy().start()

    def norm_step(i, slot):
        x = r.xv[i].astype(F32).reshape(TOK, D)
        xh, rs = norm(x)
        dn = 0.0
        for m, kept in enumerate((r.qv, r.kv, r.vv)):
            dn = dn + dot(kept[i].astype(F32).reshape(TOK, D).astype(BF), r.win[m], 1, 1)
        dx = norm_back(xh, rs, dn, gain1, False)
        r.xv[i] = (r.ov[i].astype(F32).reshape(TOK, D) + dx).reshape(W, WIN, D).astype(BF)

    def norm_before(i):
        @pl.when(i == 1)
        def _():
            tab_cores()

        @pl.when(i == S * L - 1)
        def _():
            sum_tiles(0)

    def norm_after(i):
        store_x(i).start()

    singles(S * L, norm_before, norm_step, norm_after)

    sum_lev(1, r.sum2)
    leave(1).start()
    for j in range(1, z.nl):
        tab_copy(j).wait_recv()
    sum_halves(r.th, r.tr, r.tabv)
    leave(3).start()
    sum_lev(0, r.sum1)
    leave(0).start()
    tab_core_copy().wait_send()
    for i in range(2):
        weight_pass(i).wait_send()
        core_copy(i).wait_send()
        for j in range(1, z.nt):
            weight_copy(i, j).wait_send()
            tile_copy(i, j).wait_send()
        for j in range(1, z.nl):
            lev_copy(i, j).wait_send()
    for j in range(1, z.nt):
        norm_tile_copy(j).wait_send()
    for j in range(1, z.nl):
        norm_lev_copy(j).wait_send()
    for j in range(1, z.nl):
        tab_copy(j).wait_send()
        for i in range(S * L):
            for c in range(NCH):
                stream_copy(i, c, j).wait_send()
        for i in range(S * NCH):
            back_copy(i, j).wait_send()
    for i in range(S * L):
        store_x(i).wait()
    for i in range(S * NCH):
        store_out(i).wait()
    for i in range(4):
        leave(i).wait()


def finish_kernel(z, names, pieces, *refs):
    r = Sems()
    for name, ref in zip(names, refs):
        setattr(r, name, ref)
    loads, stores = [], []
    for src, mid, dst in ((r.out0, r.out_mid, r.out), (r.dx0, r.dx_mid, r.dx)):
        n = max(1, src.shape[1] // pieces)
        for s in range(src.shape[0]):
            for p in range(0, src.shape[1], n):
                at = (s, pl.ds(p, n))
                sem = len(stores)
                loads.append(pltpu.make_async_copy(src.at[at], mid.at[at], r.sem.at[0, sem]))
                stores.append(pltpu.make_async_copy(mid.at[at], dst.at[at], r.sem.at[1, sem]))
    parts = ((r.sum1_in, r.sum1), (r.sum2_in, r.sum2), (r.vec_in, r.vec), (r.tab_in, r.tab))
    small = [pltpu.make_async_copy(a, b, r.load_sem.at[i]) for i, (a, b) in enumerate(parts)]
    for c in loads + small:
        c.start()
    for a, b in zip(loads, stores):
        a.wait()
        b.start()
    for c in small:
        c.wait()
    small_names = ("owi", "owo", "oci", "oco", "oew", "orw", "otab", "o0", "o1", "o2", "o3", "o4", "o5")
    held = {name: getattr(r, name + "_held") for name in small_names}
    held["owi"][...] = r.sum1[0 : z.rows, 0 : 3 * D]
    held["owo"][...] = r.sum1[0 : z.rows, 3 * D : 4 * D]
    held["oci"][...] = r.sum2[:, 0 : 3 * D]
    held["oco"][...] = r.sum2[:, 3 * D : 4 * D]
    held["oew"][...] = r.sum2[:, 4 * D : 4 * D + z.FF]
    for i in range(z.FF // D):
        held["orw"][i * z.rows : (i + 1) * z.rows, :] = r.sum2[:, 4 * D + z.FF + i * D : 4 * D + z.FF + (i + 1) * D]
    for i in range(6):
        held[f"o{i}"][...] = r.vec[i : i + 1, 0 : z.rows] if i > 1 else r.sum1[z.rpad + i : z.rpad + i + 1, 0 : z.rows]
    held["otab"][...] = r.tab[0:HEADS, 0 : held["otab"].shape[1]]
    outs = [pltpu.make_async_copy(held[name], getattr(r, name), r.small_sem.at[i]) for i, name in enumerate(small_names)]
    for c in outs:
        c.start()
    for c in outs:
        c.wait()
    for c in stores:
        c.wait()


def dma(*shape):
    return pltpu.SemaphoreType.DMA(shape)


def body(mesh, inputs, out_grad, lowest_level, bias_index, first_gain, first_shift, window_in, window_out, earth_bias,
         second_gain, second_shift, column_in, column_out, third_gain, third_shift, expand_weight, reduce_weight):
    z = Sizes(mesh, inputs, out_grad, expand_weight)
    S, L, LV, W, C, CB, NCH, A, FF, nt, nl = z.S, z.L, z.LV, z.W, z.C, z.CB, z.NCH, HEADS * WIN, z.FF, z.nt, z.nl
    lanes = 4 * D + 2 * FF
    tab_lanes = z.bands * RELB
    tab_half = -(-tab_lanes // 256) * 128
    g = out_grad.transpose(0, 1, 3, 2, 4).reshape(S, LV, z.cells * W, D)
    row = lambda a: a.reshape(1, z.rows)
    ins = dict(x=inputs, g=g, lowest=lowest_level, idx=bias_index, tab=earth_bias.T, wi=window_in, wo=window_out,
               ci=column_in, co=column_out, ew=expand_weight, rw=reduce_weight, v0=row(first_gain), v1=row(first_shift),
               v2=row(second_gain), v3=row(second_shift), v4=row(third_gain), v5=row(third_shift))
    outs = dict(out=(g.shape, BF), dx=(inputs.shape, BF), osum1=((z.rpad + 8, 4 * D), F32), osum2=((z.rows, lanes), F32),
                ovec=((8, 128), F32), otab=((8, 2 * tab_half), F32))
    tokens = pltpu.VMEM((S * L, W, WIN, D), BF)
    slabs = ((z.rpad + 8, 4 * D), (z.rows, lanes))
    sums = ((z.rpad + 8, 4 * D), (z.rows, lanes))
    scratch = dict(xv=tokens, xhv=tokens, qv=tokens, kv=tokens, vv=tokens, ov=tokens, pv=pltpu.VMEM((S * L, W, WIN, A), BF),
                   gv=pltpu.VMEM((S * NCH, LV, C, D), BF), xs=pltpu.VMEM((S * L, nl, NCH, CB, 128), BF),
                   x1r=pltpu.VMEM((S, LV, NCH, CB, 128), BF), ys=pltpu.VMEM((S * NCH, LV, CB, 128), BF),
                   dxr=pltpu.VMEM((S, L, nl, NCH, CB, 128), BF),                    bias=pltpu.VMEM((z.bands, WIN, A), F32), bbuf=pltpu.VMEM((max(z.bands * 8 * WIN, 4 * W * WIN), 128), F32),
                   idxt=pltpu.VMEM((128, 128), jnp.int32), key=pltpu.VMEM((LV * 8, HEADS * LV * 8), F32),
                   low=pltpu.VMEM((S, W // 8, z.cells, HEADS * LV * 8), F32),
                   wide=pltpu.VMEM((D, lanes), F32), widef=pltpu.VMEM((FF, D), F32), gs=pltpu.VMEM((8, D), F32),
                   win=pltpu.VMEM((3, D, D), BF), wout=pltpu.VMEM((D, D), BF), cin=pltpu.VMEM((3, D, D), BF),
                   cout=pltpu.VMEM((D, D), BF), ewf=pltpu.VMEM((D, FF), BF), rwf=pltpu.VMEM((FF, D), BF),
                   dwin=pltpu.VMEM((3, D, D), F32), dwout=pltpu.VMEM((D, D), F32), dcin=pltpu.VMEM((3, D, D), F32),
                   dcout=pltpu.VMEM((D, D), F32), dew=pltpu.VMEM((D, FF), F32), drw=pltpu.VMEM((FF, D), F32), dgs=pltpu.VMEM((8, D), F32), dsum=pltpu.VMEM((8, D), F32),
                   ts=pltpu.VMEM((8, 2 * tab_half), BF), tt=pltpu.VMEM((8, tab_half), BF), th=pltpu.VMEM((8, tab_half), BF),
                   tr=pltpu.VMEM((nl - 1, 8, tab_half), BF))
    for i, sh in enumerate(slabs):
        scratch.update({f"w{i + 1}s": pltpu.VMEM((1,) + sh, BF), f"w{i + 1}r": pltpu.VMEM((nt,) + sh, BF)})
    for i, (n, m) in enumerate(sums):
        part = (n, m // 2)
        scratch.update({f"g{i + 1}s": pltpu.VMEM((nt, n, m), BF), f"g{i + 1}t": pltpu.VMEM((nt,) + part, BF),
                        f"g{i + 1}h": pltpu.VMEM((nt,) + part, BF), f"g{i + 1}r": pltpu.VMEM((nt - 1,) + part, BF),
                        f"h{i + 1}s": pltpu.VMEM(part, BF), f"h{i + 1}r": pltpu.VMEM((nl - 1,) + part, BF)})
    scratch.update(g3s=pltpu.VMEM((nt, 8, 128), BF), g3r=pltpu.VMEM((nt - 1, 8, 128), BF), h3s=pltpu.VMEM((8, 128), BF),
                   h3r=pltpu.VMEM((nl - 1, 8, 128), BF))
    scratch.update(x_sem=dma(S * L), dx_sem=dma(S * L), g_sem=dma(S * NCH), out_sem=dma(S * NCH), w_send=dma(2, nt - 1), w_recv=dma(2, nt - 1),
                   wt_send=dma(2), wt_recv=dma(2), s_send=dma(S * L * NCH, nl - 1), s_recv=dma(S * L * NCH, nl - 1), s_own=dma(S * L * NCH),
                   b_send=dma(S * NCH, nl - 1), b_recv=dma(S * NCH, nl - 1), b_own=dma(S * NCH),
                   gt_send=dma(2), gt_recv=dma(2), g_send=dma(2, nt - 1), g_recv=dma(2, nt - 1), h_send=dma(2, nl - 1), h_recv=dma(2, nl - 1),
                   tt_send=dma(1), tt_recv=dma(1), t_send=dma(nl - 1), t_recv=dma(nl - 1),
                   n_send=dma(nt - 1), n_recv=dma(nt - 1), m_send=dma(nl - 1), m_recv=dma(nl - 1))
    for name, out in (("sum1", "osum1"), ("sum2", "osum2"), ("vecv", "ovec"), ("tabv", "otab")):
        scratch[name] = pltpu.VMEM(*outs[out])
    scratch["o_sem"] = dma(4)
    hbm = ("x", "g") + tuple(outs)
    place = lambda name: pl.BlockSpec(memory_space=pl.ANY if name in hbm else pltpu.VMEM)
    done = dict(zip(outs, pl.pallas_call(
        functools.partial(layer_kernel, z, tuple(ins) + tuple(outs) + tuple(scratch)),
        in_specs=[place(name) for name in ins],
        out_specs=[place(name) for name in outs],
        out_shape=[jax.ShapeDtypeStruct(*o) for o in outs.values()],
        scratch_shapes=list(scratch.values()),
        compiler_params=pltpu.CompilerParams(vmem_limit_bytes=VMEM_LIMIT, collective_id=0, has_side_effects=True),
        name="layer",
    )(*ins.values())))
    last_in = dict(out0=done["out"], dx0=done["dx"], sum1_in=done["osum1"], sum2_in=done["osum2"], vec_in=done["ovec"], tab_in=done["otab"])
    last = dict(out=(g.shape, BF), dx=(inputs.shape, BF), owi=((z.rows, 3 * D), F32), owo=((z.rows, D), F32),
                oci=((z.rows, 3 * D), F32), oco=((z.rows, D), F32), oew=((z.rows, FF), F32), orw=((z.frows, D), F32),
                otab=((HEADS, tab_lanes), F32), **{f"o{i}": ((1, z.rows), F32) for i in range(6)})
    pieces = 1
    place = lambda name: pl.BlockSpec(memory_space=pl.ANY)
    small_out = [n for n in last if n not in ("out", "dx")]
    held = dict(sum1=done["osum1"], sum2=done["osum2"], vec=done["ovec"], tab=done["otab"])
    end = dict(zip(last, pl.pallas_call(
        functools.partial(finish_kernel, z, tuple(last_in) + tuple(last) + tuple(held) + tuple(n + "_held" for n in small_out) + ("out_mid", "dx_mid", "sem", "load_sem", "small_sem"), pieces),
        in_specs=[place(name) for name in last_in],
        out_specs=[place(name) for name in last],
        out_shape=[jax.ShapeDtypeStruct(*o) for o in last.values()],
        scratch_shapes=[pltpu.VMEM(a.shape, F32) for a in held.values()] + [pltpu.VMEM(*last[n]) for n in small_out]
        + [pltpu.VMEM(g.shape, BF), pltpu.VMEM(inputs.shape, BF), dma(2, 4 * S * pieces), dma(4), dma(len(small_out))],
        compiler_params=pltpu.CompilerParams(vmem_limit_bytes=VMEM_LIMIT),
        name="finish",
    )(*last_in.values())))
    output = end["out"].reshape(S, LV, z.cells, W, D).transpose(0, 1, 3, 2, 4)
    v = [end[f"o{i}"].reshape(z.rows) for i in range(6)]
    return (output, end["dx"], v[0], v[1], end["owi"], end["owo"], end["otab"].T, v[2], v[3],
            end["oci"], end["oco"], v[4], v[5], end["oew"], end["orw"])


def solution(mesh):
    t, t2 = P("tile"), P("tile", None)
    level_tokens = P(None, "lev", "tile", None, None)
    column_tokens = P(None, None, "tile", "lev", None)
    placed = (level_tokens, column_tokens, P(None, "tile", "lev"), P(), t, t, t2, t2, t2, t, t, t2, t2, t, t, t2, t2)
    outs = (column_tokens, level_tokens, t, t, t2, t2, t2, t, t, t2, t2, t, t, t2, t2)
    return jax.shard_map(functools.partial(body, mesh), mesh=mesh, in_specs=placed, out_specs=outs, check_vma=False)
```

```python
import functools

import jax
import jax.numpy as jnp
from jax import lax
from jax.experimental import pallas as pl
from jax.experimental.pallas import tpu as pltpu
from jax.sharding import PartitionSpec as P

HEADS = 6
HEAD_DIM = 32
D = HEADS * HEAD_DIM
WIN = 72
RELB = 828
RELP = 832
NWLON = 2
EPSILON = 1e-05
SCALE = HEAD_DIM ** (-0.5)
LOG2E = 1.4426950408889634
MASKED = -1e30
F32 = jnp.float32
BF = jnp.bfloat16
MESH = pl.DeviceIdType.MESH
VMEM_LIMIT = 60 << 20
BATCH_F, BATCH_C, BATCH_B = 16, 12, 8


def dot(a, b, ca=1, cb=0):
    return lax.dot_general(a, b, (((ca,), (cb,)), ((), ())), preferred_element_type=F32)


def lane_heads():
    lane = lax.broadcasted_iota(jnp.int32, (1, 128), 1)
    return [(lane // HEAD_DIM == h).astype(F32) for h in range(4)], [lane < HEAD_DIM * (h + 1) for h in range(3)]


def spread(v, marks, factor=None):
    n = v.shape[0]
    low, high = v[:, :128], v[:, 128:]
    tops = [m if factor is None else m * factor for m in marks]
    if n == 64:
        low, high = low.astype(BF), high.astype(BF)
        tops = [m.astype(BF) for m in tops]
        first = jnp.concatenate([low * m for m in tops], axis=0)
        return first, jnp.concatenate([high * m[:, :64] for m in tops[:2]], axis=0)
    parts = [low * m for m in tops]
    cut = 256 - 3 * n
    first = jnp.concatenate(parts[:3] + [parts[3][:cut]], axis=0).astype(BF)
    head3 = jnp.concatenate([parts[3][cut:], jnp.zeros((n - cut, 64), F32)], axis=1)
    blank = jnp.zeros((n, 128), F32)
    rest = [jnp.concatenate([blank, high * m[:, :64]], axis=1) for m in tops[:2]]
    return first, jnp.concatenate([head3] + rest, axis=0).astype(BF)


def scores(k, spread_q):
    first, rest = spread_q
    right = k[:, 128:] if rest.shape[1] == 64 else k
    return jnp.concatenate([dot(k[:, :128], first, 1, 1), dot(right, rest, 1, 1)], axis=1)


def weigh(p, spread_v):
    first, rest = spread_v
    low, high = dot(p[:, :256], first), dot(p[:, 256:], rest)
    if rest.shape[1] == 64:
        return jnp.concatenate([low, high], axis=1)
    return jnp.concatenate([low + high[:, :128], high[:, 128:]], axis=1)


def mix(p, v, bounds):
    n = v.shape[0]
    first = dot(p[:, :256], v[:, :128], 0, 0)
    if n == 64:
        rest = dot(p[:, 256:], v[:, 128:], 0, 0)
        head3, tail = first[3 * n :], rest
    else:
        rest = dot(p[:, 256:], v, 0, 0)
        cut = 4 * n - 256
        head3, tail = jnp.concatenate([first[3 * n :], rest[:cut, :128]], axis=0), rest[cut:, 128:]
    low = jnp.where(bounds[0], first[:n], jnp.where(bounds[1], first[n : 2 * n], jnp.where(bounds[2], first[2 * n : 3 * n], head3)))
    high = jnp.where(bounds[0][:, :64], tail[:n], tail[n:])
    return jnp.concatenate([low, high], axis=1)


def norm(x):
    mean = jnp.sum(x, -1, keepdims=True) * (1.0 / D)
    c = x - mean
    var = jnp.sum(c * c, -1, keepdims=True) * (1.0 / D)
    r = lax.rsqrt(var + EPSILON)
    return c * r, r


def norm_back(xh, r, dn, gain, sums=True):
    t = dn * gain
    a = jnp.sum(t, -1, keepdims=True) * (1.0 / D)
    b = jnp.sum(t * xh, -1, keepdims=True) * (1.0 / D)
    dx = r * (t - a - xh * b)
    if not sums:
        return dx
    return dx, jnp.sum(dn * xh, 0, keepdims=True), jnp.sum(dn, 0, keepdims=True)


def softmax2(st):
    e = jnp.exp2(st - jnp.max(st, 0, keepdims=True))
    return e * (1.0 / jnp.sum(e, 0, keepdims=True))


def moved(rows, by):
    if isinstance(rows, slice):
        return slice(rows.start + by, rows.stop + by)
    return pl.ds(rows.start + by, rows.size, stride=rows.stride)


def put(ref, base, tall, rows, v):
    n = v.shape[0]
    ref[moved(rows, base), :] = v[:, :128]
    ref[moved(rows, base + tall), :] = jnp.concatenate([v[:, 128:], jnp.zeros((n, 256 - D), F32)], axis=1)


def take(ref, base, tall, rows):
    return jnp.concatenate([ref[moved(rows, base), :], ref[moved(rows, base + tall), :][:, : D - 128]], axis=1)


def fold(ref, at, v):
    c = v.shape[0]
    ref[at + (slice(0, c),)] = v[:, :128].astype(BF)
    tail = jnp.concatenate([v[: c // 2, 128:], v[c // 2 :, 128:]], axis=1)
    ref[at + (slice(c, c + c // 2),)] = tail.astype(BF)


def unfold(block):
    c = block.shape[0] * 2 // 3
    wide = block.astype(F32)
    tail = wide[c:]
    return jnp.concatenate([wide[:c], jnp.concatenate([tail[:, :64], tail[:, 64:]], axis=0)], axis=1)


def one_hot(idx_ref, j):
    entry = lax.broadcasted_iota(jnp.int32, (RELP, 128), 0)
    return (entry == idx_ref[j : j + 1, :]).astype(F32).astype(BF)


def announce(axes):
    sem = pltpu.get_barrier_semaphore()
    count = 0
    for axis, size in axes:
        me = lax.axis_index(axis)
        for j in range(1, size):
            pl.semaphore_signal(sem, inc=1, device_id={axis: lax.rem(me + j, size)}, device_id_type=MESH)
            count += 1
    return sem, count


def to_peer(axis, size, j, src, dst, send, recv):
    me = lax.axis_index(axis)
    return pltpu.make_async_remote_copy(
        src_ref=src, dst_ref=dst, send_sem=send, recv_sem=recv,
        device_id={axis: lax.rem(me + j, size)}, device_id_type=MESH,
    )


def rows_to_lanes(m, n):
    return jnp.concatenate([m[i : i + n] for i in range(0, m.shape[0], n)], axis=1)


class Sizes:
    def __init__(self, mesh, inputs, out_grad, expand):
        self.nl = mesh.shape["lev"]
        self.nt = mesh.shape["tile"]
        self.S, self.L, self.W = inputs.shape[:3]
        self.LV = out_grad.shape[1]
        self.cells = out_grad.shape[3]
        self.bands = self.W // NWLON
        self.rows = D // self.nt
        self.rpad = -(-self.rows // 8) * 8
        self.FF = expand.shape[1]
        self.frows = self.FF // self.nt
        self.T = 6 if self.cells % 6 == 0 else 3
        self.NCH = self.cells // self.T
        self.C = self.T * self.W
        self.CB = self.C * 3 // 2


def lane_pad(m, width, value=0.0):
    if m.shape[1] == width:
        return m
    return jnp.concatenate([m, jnp.full((m.shape[0], width - m.shape[1]), value, F32)], axis=1)


def pairs(count, before, step, after):
    def two(i, _):
        for k in range(2):
            before(2 * i + k)
        for k in range(2):
            step(2 * i + k, k)
        for k in range(2):
            after(2 * i + k)
        return 0

    lax.fori_loop(0, count // 2, two, 0)


def singles(count, before, step, after):
    def one(i, _):
        before(i)
        step(i, 0)
        after(i)
        return 0

    lax.fori_loop(0, count, one, 0)


class Sems:
    pass


def layer_kernel(z, names, *refs):
    r = Sems()
    for name, ref in zip(names, refs):
        setattr(r, name, ref)
    me_l, me_t = lax.axis_index("lev"), lax.axis_index("tile")
    S, L, LV, W, C, NCH = z.S, z.L, z.LV, z.W, z.C, z.NCH
    TOK = W * WIN
    TABH = r.th.shape[-1]
    marks, bounds = lane_heads()

    def load_x(i):
        return pltpu.make_async_copy(r.x.at[i // L, lax.rem(i, L)], r.xv.at[i], r.x_sem.at[i])

    def store_x(i):
        return pltpu.make_async_copy(r.xv.at[i], r.dx.at[i // L, lax.rem(i, L)], r.dx_sem.at[i])

    def load_g(i):
        rows = pl.ds(pl.multiple_of(lax.rem(i, NCH) * C, 16), C)
        return pltpu.make_async_copy(r.g.at[i // NCH, :, rows, :], r.gv.at[i], r.g_sem.at[i])

    def store_out(i):
        rows = pl.ds(pl.multiple_of(lax.rem(i, NCH) * C, 16), C)
        return pltpu.make_async_copy(r.gv.at[i], r.out.at[i // NCH, :, rows, :], r.out_sem.at[i])

    core, twin = lax.rem(me_l, 2), me_l + 1 - 2 * lax.rem(me_l, 2)

    def to_twin(src, dst, send, recv):
        return pltpu.make_async_remote_copy(src_ref=src, dst_ref=dst, send_sem=send, recv_sem=recv,
                                            device_id={"lev": twin}, device_id_type=MESH)

    def half(ref, which):
        width = ref.shape[-1] // 2
        return ref.at[:, :, pl.ds(pl.multiple_of(which * width, 128), width)]

    weights = ((r.w1s, r.w1r), (r.w2s, r.w2r))

    def weight_copy(i, j):
        src, dst = weights[i]
        return to_peer("tile", z.nt, j, half(src, core).at[0], half(dst, core).at[me_t], r.w_send.at[i, j - 1], r.w_recv.at[i, j - 1])

    def weight_pass(i):
        part = half(weights[i][1], core)
        return to_twin(part, part, r.wt_send.at[i], r.wt_recv.at[i])

    def weight_start(i):
        for j in range(1, z.nt):
            weight_copy(i, j).start()
        src, dst = weights[i]
        width = src.shape[-1] // 2
        own = pl.ds(pl.multiple_of(core * width, 128), width)
        dst[pl.ds(me_t, 1), :, own] = src[:, :, own]

    def weight_hand(i):
        for j in range(1, z.nt):
            weight_copy(i, j).wait_recv()
        weight_pass(i).start()

    def stream_copy(i, c, j):
        return to_peer("lev", z.nl, j, r.xs.at[i, lax.rem(me_l + j, z.nl), c], r.x1r.at[i // L, me_l * L + lax.rem(i, L), c],
                       r.s_send.at[i * NCH + c, j - 1], r.s_recv.at[i * NCH + c, j - 1])

    def stream_own(i, c):
        return pltpu.make_async_copy(r.xs.at[i, me_l, c], r.x1r.at[i // L, me_l * L + lax.rem(i, L), c], r.s_own.at[i * NCH + c])

    def back_copy(i, j):
        return to_peer("lev", z.nl, j, r.ys.at[i, pl.ds(lax.rem(me_l + j, z.nl) * L, L)],
                       r.dxr.at[i // NCH, :, me_l, lax.rem(i, NCH)], r.b_send.at[i, j - 1], r.b_recv.at[i, j - 1])

    def back_own(i):
        return pltpu.make_async_copy(r.ys.at[i, pl.ds(me_l * L, L)], r.dxr.at[i // NCH, :, me_l, lax.rem(i, NCH)], r.b_own.at[i])

    grads = ((r.g1s, r.g1t, r.g1h, r.g1r, r.h1s, r.h1r), (r.g2s, r.g2t, r.g2h, r.g2r, r.h2s, r.h2r))

    def core_copy(i):
        return to_twin(half(grads[i][0], 1 - core), grads[i][1], r.gt_send.at[i], r.gt_recv.at[i])

    def tile_copy(i, j):
        src, dst = grads[i][2], grads[i][3]
        return to_peer("tile", z.nt, j, src.at[lax.rem(me_t + j, z.nt)], dst.at[j - 1], r.g_send.at[i, j - 1], r.g_recv.at[i, j - 1])

    def lev_copy(i, j):
        return to_peer("lev", z.nl, j, grads[i][4], grads[i][5].at[j - 1], r.h_send.at[i, j - 1], r.h_recv.at[i, j - 1])

    def sum_cores(i):
        core_copy(i).wait_recv()
        gs, gt, gh = grads[i][:3]
        width = gt.shape[-1]
        mine = gs[:, :, pl.ds(pl.multiple_of(core * width, 128), width)]
        gh[...] = (mine.astype(F32) + gt[...].astype(F32)).astype(BF)
        for j in range(1, z.nt):
            tile_copy(i, j).start()

    def sum_tiles(i):
        gh, gr, hs = grads[i][2:5]
        total = gh[pl.ds(me_t, 1)][0].astype(F32)
        for j in range(1, z.nt):
            tile_copy(i, j).wait_recv()
            total = total + gr[j - 1].astype(F32)
        hs[...] = total.astype(BF)
        for j in range(1, z.nl):
            lev_copy(i, j).start()

    def sum_halves(own, got, out):
        mine, other = own[...].astype(F32), 0.0
        for j in range(1, z.nl):
            if j % 2 == 0:
                mine = mine + got[j - 1].astype(F32)
            else:
                other = other + got[j - 1].astype(F32)
        width = own.shape[-1]
        first = core == 0
        out[:, 0:width] = jnp.where(first, mine, other)
        out[:, width : 2 * width] = jnp.where(first, other, mine)

    def sum_lev(i, out):
        for j in range(1, z.nl):
            lev_copy(i, j).wait_recv()
        sum_halves(grads[i][4], grads[i][5], out)

    def leave(i):
        src, dst = ((r.sum1, r.osum1), (r.sum2, r.osum2), (r.vecv, r.ovec), (r.tabv, r.otab))[i]
        return pltpu.make_async_copy(src, dst, r.o_sem.at[i])

    def tab_core_copy():
        part = r.ts.at[:, pl.ds(pl.multiple_of((1 - core) * TABH, 128), TABH)]
        return to_twin(part, r.tt, r.tt_send.at[0], r.tt_recv.at[0])

    def tab_cores():
        tab_core_copy().wait_recv()
        mine = r.ts[:, pl.ds(pl.multiple_of(core * TABH, 128), TABH)]
        r.th[...] = (mine.astype(F32) + r.tt[...].astype(F32)).astype(BF)
        for j in range(1, z.nl):
            tab_copy(j).start()

    def tab_copy(j):
        return to_peer("lev", z.nl, j, r.th, r.tr.at[j - 1], r.t_send.at[j - 1], r.t_recv.at[j - 1])

    def norm_tile_copy(j):
        return to_peer("tile", z.nt, j, r.g3s.at[lax.rem(me_t + j, z.nt)], r.g3r.at[j - 1], r.n_send.at[j - 1], r.n_recv.at[j - 1])

    def norm_lev_copy(j):
        return to_peer("lev", z.nl, j, r.h3s, r.h3r.at[j - 1], r.m_send.at[j - 1], r.m_recv.at[j - 1])

    sem, count = announce((("lev", z.nl), ("tile", z.nt)))
    for i in range(S * L):
        load_x(i).start()
    for i in range(S * NCH):
        load_g(i).start()
    r.w1s[...] = jnp.zeros(r.w1s.shape, BF)
    r.w1s[0, 0 : z.rows, 0 : 3 * D] = r.wi[...]
    r.w1s[0, 0 : z.rows, 3 * D : 4 * D] = r.wo[...]
    for i, vec in enumerate((r.v0, r.v1, r.v2, r.v3, r.v4, r.v5)):
        r.w1s[0, z.rpad + i : z.rpad + i + 1, 0 : z.rows] = vec[...]
    r.w2s[0, :, 0 : 3 * D] = r.ci[...]
    r.w2s[0, :, 3 * D : 4 * D] = r.co[...]
    r.w2s[0, :, 4 * D : 4 * D + z.FF] = r.ew[...]
    r.w2s[0, :, 4 * D + z.FF :] = rows_to_lanes(r.rw[...].astype(F32), z.rows).astype(BF)
    entries = lane_pad(r.idx[...].astype(F32), 128, -1.0)
    entries = jnp.concatenate([entries, jnp.full((128 - WIN, 128), -1.0, F32)], axis=0)
    r.idxt[...] = jnp.transpose(entries).astype(jnp.int32)
    cells8 = lax.broadcasted_iota(jnp.int32, (LV * 8, HEADS * LV * 8), 0)
    lane8 = lax.broadcasted_iota(jnp.int32, (LV * 8, HEADS * LV * 8), 1)
    r.key[...] = jnp.where(cells8 % 8 == lane8 % 8, (cells8 // 8).astype(F32), -1.0)
    wrow = lax.broadcasted_iota(jnp.int32, (W, HEADS * LV * 8), 0)
    wlane = lax.broadcasted_iota(jnp.int32, (W, HEADS * LV * 8), 1)
    for part in range(W // 8):
        pick = (wrow == wlane % 8 + 8 * part).astype(F32).astype(BF)
        for s in range(S):
            r.low[s, part] = dot(r.lowest[s].astype(F32).astype(BF), pick, 0, 0)
    r.ts[...] = jnp.zeros(r.ts.shape, BF)
    pl.semaphore_wait(sem, count)
    weight_start(0)
    table = r.tab[...].astype(F32)
    pads = jnp.zeros((8 - HEADS, RELP), F32)
    table = jnp.concatenate(
        [jnp.concatenate([lane_pad(table[:, b * RELB : (b + 1) * RELB], RELP), pads], axis=0) for b in range(z.bands)], axis=0
    ).astype(BF)
    n8 = z.bands * 8
    for j in range(0, WIN, 2):
        both = jnp.concatenate([one_hot(r.idxt, j), one_hot(r.idxt, j + 1)], axis=1)
        vals = dot(table, both) * LOG2E
        r.bbuf[pl.ds(j, n8, stride=WIN), :] = vals[:, :128]
        r.bbuf[pl.ds(j + 1, n8, stride=WIN), :] = vals[:, 128:]
    def normalize(i, _):
        load_x(i).wait()
        r.xhv[i] = norm(r.xv[i].astype(F32).reshape(TOK, D))[0].reshape(W, WIN, D).astype(BF)
        return 0

    lax.fori_loop(0, S * L // 2, normalize, 0)
    weight_hand(0)
    weight_start(1)
    lax.fori_loop(S * L // 2, S * L, normalize, 0)
    for b in range(z.bands):
        r.bias[b] = jnp.concatenate(
            [r.bbuf[(b * 8 + h) * WIN : (b * 8 + h + 1) * WIN, :][:, :WIN] for h in range(HEADS)], axis=1
        )
    for ref in (r.dcin, r.dcout, r.dew, r.drw, r.dwin, r.dwout, r.dgs, r.dsum):
        ref[...] = jnp.zeros(ref.shape, F32)
    weight_pass(0).wait_recv()
    for t in range(z.nt):
        r.wide[t * z.rows : (t + 1) * z.rows, 0 : 4 * D] = r.w1r[t, 0 : z.rows, :].astype(F32)
    for i in range(3):
        r.win[i] = r.wide[:, i * D : (i + 1) * D].astype(BF)
    r.wout[...] = r.wide[:, 3 * D : 4 * D].astype(BF)
    r.gs[...] = jnp.concatenate([r.w1r[t, z.rpad : z.rpad + 8, :].astype(F32)[:, : z.rows] for t in range(z.nt)], axis=1)
    gain1, shift1, g2, s2, g3, s3 = (r.gs[i : i + 1, :] for i in range(6))

    def window_step(i, slot):
        n1 = (r.xhv[i].astype(F32).reshape(TOK, D) * gain1 + shift1).astype(BF)
        q, k, v = (dot(n1, r.win[m]) for m in range(3))
        mixed = []
        for b0 in range(0, W, BATCH_F):
            batch = range(b0, b0 + BATCH_F)
            cut = {w: slice(w * WIN, (w + 1) * WIN) for w in batch}
            kb = {w: k[cut[w]].astype(BF) for w in batch}
            vb = {w: v[cut[w]].astype(BF) for w in batch}
            for w in batch:
                r.qv[i, w] = q[cut[w]].astype(BF)
                r.kv[i, w] = kb[w]
                r.vv[i, w] = vb[w]
            sq = {w: spread(q[cut[w]], marks, SCALE * LOG2E) for w in batch}
            st = {w: scores(kb[w], sq[w]) + r.bias[w // NWLON] for w in batch}
            pb = {w: softmax2(st[w]).astype(BF) for w in batch}
            for w in batch:
                r.pv[i, w] = pb[w]
            mixed += [mix(pb[w], vb[w], bounds) for w in batch]
        o = jnp.concatenate(mixed, axis=0).astype(BF)
        r.ov[i] = o.astype(F32).reshape(W, WIN, D).astype(BF)
        x1 = r.xv[i].astype(F32).reshape(TOK, D) + dot(o, r.wout[...])
        for w in range(W):
            put(r.bbuf, 2 * TOK * slot, TOK, pl.ds(w, WIN, stride=W), x1[w * WIN : (w + 1) * WIN])
        for d in range(z.nl):
            for c in range(NCH):
                at = (d * NCH + c) * C
                fold(r.xs, (i, d, c), take(r.bbuf, 2 * TOK * slot, TOK, slice(at, at + C)))

    def window_before(i):
        @pl.when(i == S * L - 1)
        def _():
            weight_hand(1)

    def window_after(i):
        for c in range(NCH):
            for j in range(1, z.nl):
                stream_copy(i, c, j).start()
            stream_own(i, c).start()

    singles(S * L, window_before, window_step, window_after)

    weight_pass(1).wait_recv()
    for t in range(z.nt):
        r.wide[t * z.rows : (t + 1) * z.rows, :] = r.w2r[t].astype(F32)
        for i in range(z.FF // D):
            at = t * z.frows + i * z.rows
            r.widef[at : at + z.rows, :] = r.w2r[t].astype(F32)[:, 4 * D + z.FF + i * D : 4 * D + z.FF + (i + 1) * D]
    for i in range(3):
        r.cin[i] = r.wide[:, i * D : (i + 1) * D].astype(BF)
    r.cout[...] = r.wide[:, 3 * D : 4 * D].astype(BF)
    r.ewf[...] = r.wide[:, 4 * D : 4 * D + z.FF].astype(BF)
    r.rwf[...] = r.widef[...].astype(BF)
    r.bias[...] = jnp.zeros(r.bias.shape, F32)

    groups, R, GR = C // 8, LV * C, LV * 8
    halves = W // 8

    def cols(m, j):
        return m.reshape(LV, C, D)[:, j * 8 : (j + 1) * 8, :].reshape(GR, D)

    def join(parts):
        return jnp.concatenate([p.reshape(LV, 8, D) for p in parts], axis=1).reshape(R, D)

    def column_step(i, slot):
        s, ch = i // NCH, lax.rem(i, NCH)

        x1 = jnp.concatenate([unfold(r.x1r[s, m, ch]) for m in range(LV)], axis=0)
        xh2, r2 = norm(x1)
        n2 = (xh2 * g2 + s2).astype(BF)
        gb = r.gv[i].astype(F32).reshape(R, D).astype(BF)
        dh = dot(gb, r.rwf[...] * 0.5, 1, 1).astype(BF)
        q, k, v = (dot(n2, r.cin[m]) for m in range(3))
        key = r.key[...]
        mixed = []
        qb, kb, vb, pb = {}, {}, {}, {}
        for b0 in range(0, groups, BATCH_C):
            batch = range(b0, min(b0 + BATCH_C, groups))
            for j in batch:
                kb[j], vb[j] = cols(k, j).astype(BF), cols(v, j).astype(BF)
                qb[j] = spread(cols(q, j), marks, SCALE * LOG2E)
            st = {j: scores(kb[j], qb[j]) for j in batch}
            for j in batch:
                low = r.low[s, j % halves, pl.ds(ch * z.T + j // halves, 1), :]
                pb[j] = softmax2(jnp.where(key >= low, st[j], MASKED)).astype(BF)
            mixed += [mix(pb[j], vb[j], bounds) for j in batch]
        o2 = join(mixed).astype(BF)
        x2 = x1 + dot(o2, r.cout[...])
        xh3, r3 = norm(x2)
        n3 = (xh3 * g3 + s3).astype(BF)
        u = dot(n3, r.ewf[...] * 0.5).astype(BF)
        c = 0.7978845608028654
        a = BF(2 * c) + BF(8 * c * 0.044715) * (u * u)
        t = jnp.tanh(u * a)
        up = BF(1.0) + t
        hid = u * up
        du = dh * (up + hid * (BF(1.0) - t) * (BF(3.0) * a - BF(4.0 * c)))
        dn3 = dot(du, r.ewf[...], 1, 1)
        dx, a3, b3 = norm_back(xh3, r3, dn3, g3)
        dx2 = gb.astype(F32) + dx
        dx2b = dx2.astype(BF)
        r.gv[i] = (x2 + dot(hid, r.rwf[...])).reshape(LV, C, D).astype(BF)
        r.drw[...] = r.drw[...] + dot(hid, gb, 0, 0)
        r.dew[...] = r.dew[...] + dot(n3, du, 0, 0)
        r.dcout[...] = r.dcout[...] + dot(o2, dx2b, 0, 0)
        do = dot(dx2b, r.cout[...], 1, 1)
        dq, dk, dv = [], [], []
        for b0 in range(0, groups, BATCH_C):
            batch = range(b0, min(b0 + BATCH_C, groups))
            dob = {j: spread(cols(do, j), marks) for j in batch}
            dpt = {j: scores(vb[j], dob[j]) for j in batch}
            dv += [weigh(pb[j], dob[j]) for j in batch]
            dsb = {}
            for j in batch:
                pf = pb[j].astype(F32)
                dsb[j] = (pf * (dpt[j] - jnp.sum(dpt[j] * pf, 0, keepdims=True))).astype(BF)
            dk += [weigh(dsb[j], qb[j]) * (1.0 / LOG2E) for j in batch]
            dq += [mix(dsb[j], kb[j], bounds) * SCALE for j in batch]
        dn2 = 0.0
        packs = [join(part).astype(BF) for part in (dq, dk, dv)]
        for m, pack in enumerate(packs):
            dn2 = dn2 + dot(pack, r.cin[m], 1, 1)
        dx, a2, b2 = norm_back(xh2, r2, dn2, g2)
        for m, pack in enumerate(packs):
            r.dcin[m] = r.dcin[m] + dot(n2, pack, 0, 0)
        dx1 = dx2 + dx
        for m in range(LV):
            fold(r.ys, (i, m), dx1[m * C : (m + 1) * C])
        for m, part in enumerate((a2, b2, a3, b3)):
            r.dgs[m + 2 : m + 3, :] = r.dgs[m + 2 : m + 3, :] + part

    def column_before(i):
        s, ch = i // NCH, lax.rem(i, NCH)
        load_g(i).wait()
        for l in range(L):
            stream_own(s * L + l, ch).wait()
            for j in range(1, z.nl):
                stream_copy(s * L + l, ch, j).wait_recv()

    def column_after(i):
        store_out(i).start()
        for j in range(1, z.nl):
            back_copy(i, j).start()
        back_own(i).start()

    pairs(S * NCH, column_before, column_step, column_after)

    for t in range(z.nt):
        rows = slice(t * z.rows, (t + 1) * z.rows)
        for i in range(3):
            r.g2s[t, :, i * D : (i + 1) * D] = r.dcin[i, rows, :].astype(BF)
        r.g2s[t, :, 3 * D : 4 * D] = r.dcout[rows, :].astype(BF)
        r.g2s[t, :, 4 * D : 4 * D + z.FF] = r.dew[rows, :].astype(BF)
        r.g2s[t, :, 4 * D + z.FF :] = rows_to_lanes(r.drw[t * z.frows : (t + 1) * z.frows, :], z.rows).astype(BF)
    core_copy(1).start()
    for t in range(z.nt):
        r.g3s[t] = lane_pad(r.dgs[:, t * z.rows : (t + 1) * z.rows], 128).astype(BF)
    for j in range(1, z.nt):
        norm_tile_copy(j).start()

    def back_step(i, slot):
        s, l = i // L, lax.rem(i, L)

        for d in range(z.nl):
            for c in range(NCH):
                at = (d * NCH + c) * C
                put(r.bbuf, 2 * TOK * slot, TOK, slice(at, at + C), unfold(r.dxr[s, l, d, c]))
        xhs, dqs, dks, dvs, d1s, os = [], [], [], [], [], []
        for b0 in range(0, W, BATCH_B):
            batch = range(b0, b0 + BATCH_B)
            d1 = jnp.concatenate([take(r.bbuf, 2 * TOK * slot, TOK, pl.ds(w, WIN, stride=W)) for w in batch], axis=0)
            d1b = d1.astype(BF)
            do = dot(d1b, r.wout[...], 1, 1)
            os.append(r.ov[i, b0 : b0 + BATCH_B].astype(F32).reshape(BATCH_B * WIN, D).astype(BF))
            r.dwout[...] = r.dwout[...] + dot(os[-1], d1b, 0, 0)
            dob = {w: spread(do[(w - b0) * WIN : (w - b0 + 1) * WIN], marks) for w in batch}
            qb = {w: spread(r.qv[i, w].astype(F32), marks) for w in batch}
            dpt = {w: scores(r.vv[i, w], dob[w]) for w in batch}
            dv = [weigh(r.pv[i, w], dob[w]) for w in batch]
            dsb = {}
            for w in batch:
                pf = r.pv[i, w].astype(F32)
                ds = pf * (dpt[w] - jnp.sum(dpt[w] * pf, 0, keepdims=True))
                dsb[w] = ds.astype(BF)
                r.bias[w // NWLON] = r.bias[w // NWLON] + ds
            dk = [weigh(dsb[w], qb[w]) * SCALE for w in batch]
            dq = [mix(dsb[w], r.kv[i, w], bounds) * SCALE for w in batch]
            xhs.append(r.xhv[i, b0 : b0 + BATCH_B].astype(F32).reshape(BATCH_B * WIN, D).astype(BF))
            r.ov[i, b0 : b0 + BATCH_B] = d1.reshape(BATCH_B, WIN, D).astype(BF)
            d1s.append(d1b)
            for m, (part, parts, keep) in enumerate(((dq, dqs, r.qv), (dk, dks, r.kv), (dv, dvs, r.vv))):
                flat = jnp.concatenate(part, axis=0)
                r.dsum[m : m + 1, :] = r.dsum[m : m + 1, :] + jnp.sum(flat, 0, keepdims=True)
                keep[i, b0 : b0 + BATCH_B] = flat.reshape(BATCH_B, WIN, D).astype(BF)
                parts.append(flat.astype(BF))
        xh = jnp.concatenate(xhs, axis=0)
        for m, part in enumerate((dqs, dks, dvs)):
            r.dwin[m] = r.dwin[m] + dot(xh, jnp.concatenate(part, axis=0), 0, 0)

    def back_before(i):
        s, l = i // L, lax.rem(i, L)

        @pl.when(l == 0)
        def _():
            for c in range(NCH):
                back_own(s * NCH + c).wait()
                for j in range(1, z.nl):
                    back_copy(s * NCH + c, j).wait_recv()

        @pl.when(i == S * L // 2)
        def _():
            sum_cores(1)
            vec = r.g3s[pl.ds(me_t, 1)][0].astype(F32)
            for j in range(1, z.nt):
                norm_tile_copy(j).wait_recv()
                vec = vec + r.g3r[j - 1].astype(F32)
            r.h3s[...] = vec.astype(BF)
            for j in range(1, z.nl):
                norm_lev_copy(j).start()

    def nothing(i):
        pass

    pairs(S * L, back_before, back_step, nothing)

    tall = jnp.concatenate([gain1, shift1, jnp.zeros((126, D), F32)], axis=0)
    tall = jnp.transpose(lane_pad(tall, 256))[:D]
    to_gain, to_shift = 0.0, 0.0
    for i in range(3):
        w, m, c = r.win[i].astype(F32), r.dwin[i], r.dsum[i : i + 1, :]
        to_gain = to_gain + jnp.sum(w * m, 1, keepdims=True)
        to_shift = to_shift + jnp.sum(w * c, 1, keepdims=True)
        r.dwin[i] = tall[:, 0:1] * m + tall[:, 1:2] * c
    lane = lax.broadcasted_iota(jnp.int32, (D, 128), 1)
    flat = jnp.concatenate([jnp.where(lane == 0, to_gain, jnp.where(lane == 1, to_shift, 0.0)), jnp.zeros((256 - D, 128), F32)], axis=0)
    flat = jnp.transpose(flat)
    for t in range(z.nt):
        rows = slice(t * z.rows, (t + 1) * z.rows)
        for i in range(3):
            r.g1s[t, 0 : z.rows, i * D : (i + 1) * D] = r.dwin[i, rows, :].astype(BF)
        r.g1s[t, 0 : z.rows, 3 * D : 4 * D] = r.dwout[rows, :].astype(BF)
        r.g1s[t, z.rpad : z.rpad + 8, :] = lane_pad(flat[0:8, rows], 4 * D).astype(BF)
    core_copy(0).start()
    vec = r.h3s[...].astype(F32)
    for j in range(1, z.nl):
        norm_lev_copy(j).wait_recv()
        vec = vec + r.h3r[j - 1].astype(F32)
    r.vecv[...] = vec
    leave(2).start()

    pads = jnp.zeros((WIN, 128 - WIN), F32)
    for b in range(z.bands):
        for h in range(8):
            at = (b * 8 + h) * WIN
            if h < HEADS:
                r.bbuf[at : at + WIN, :] = jnp.concatenate([r.bias[b, :, h * WIN : (h + 1) * WIN], pads], axis=1)
            else:
                r.bbuf[at : at + WIN, :] = jnp.zeros((WIN, 128), F32)
    tab = jnp.zeros((n8, RELP), F32)
    for j in range(0, WIN, 2):
        if j == WIN // 3:
            sum_cores(0)
        if j == 2 * WIN // 3:
            sum_tiles(1)
        both = jnp.concatenate([one_hot(r.idxt, j), one_hot(r.idxt, j + 1)], axis=1)
        pair = jnp.concatenate([r.bbuf[pl.ds(j, n8, stride=WIN), :], r.bbuf[pl.ds(j + 1, n8, stride=WIN), :]], axis=1)
        tab = tab + dot(pair.astype(BF), both, 1, 1)
    for b in range(z.bands):
        r.ts[:, b * RELB : (b + 1) * RELB] = tab[b * 8 : (b + 1) * 8, :RELB].astype(BF)
    tab_core_copy().start()

    def norm_step(i, slot):
        x = r.xv[i].astype(F32).reshape(TOK, D)
        xh, rs = norm(x)
        dn = 0.0
        for m, kept in enumerate((r.qv, r.kv, r.vv)):
            dn = dn + dot(kept[i].astype(F32).reshape(TOK, D).astype(BF), r.win[m], 1, 1)
        dx = norm_back(xh, rs, dn, gain1, False)
        r.xv[i] = (r.ov[i].astype(F32).reshape(TOK, D) + dx).reshape(W, WIN, D).astype(BF)

    def norm_before(i):
        @pl.when(i == 1)
        def _():
            tab_cores()

        @pl.when(i == S * L - 1)
        def _():
            sum_tiles(0)

    def norm_after(i):
        store_x(i).start()

    singles(S * L, norm_before, norm_step, norm_after)

    sum_lev(1, r.sum2)
    leave(1).start()
    for j in range(1, z.nl):
        tab_copy(j).wait_recv()
    sum_halves(r.th, r.tr, r.tabv)
    leave(3).start()
    sum_lev(0, r.sum1)
    leave(0).start()
    tab_core_copy().wait_send()
    for i in range(2):
        weight_pass(i).wait_send()
        core_copy(i).wait_send()
        for j in range(1, z.nt):
            weight_copy(i, j).wait_send()
            tile_copy(i, j).wait_send()
        for j in range(1, z.nl):
            lev_copy(i, j).wait_send()
    for j in range(1, z.nt):
        norm_tile_copy(j).wait_send()
    for j in range(1, z.nl):
        norm_lev_copy(j).wait_send()
    for j in range(1, z.nl):
        tab_copy(j).wait_send()
        for i in range(S * L):
            for c in range(NCH):
                stream_copy(i, c, j).wait_send()
        for i in range(S * NCH):
            back_copy(i, j).wait_send()
    for i in range(S * L):
        store_x(i).wait()
    for i in range(S * NCH):
        store_out(i).wait()
    for i in range(4):
        leave(i).wait()


def finish_kernel(z, names, pieces, *refs):
    r = Sems()
    for name, ref in zip(names, refs):
        setattr(r, name, ref)
    loads, stores = [], []
    for src, mid, dst in ((r.out0, r.out_mid, r.out), (r.dx0, r.dx_mid, r.dx)):
        n = max(1, src.shape[1] // pieces)
        for s in range(src.shape[0]):
            for p in range(0, src.shape[1], n):
                at = (s, pl.ds(p, n))
                sem = len(stores)
                loads.append(pltpu.make_async_copy(src.at[at], mid.at[at], r.sem.at[0, sem]))
                stores.append(pltpu.make_async_copy(mid.at[at], dst.at[at], r.sem.at[1, sem]))
    parts = ((r.sum1_in, r.sum1), (r.sum2_in, r.sum2), (r.vec_in, r.vec), (r.tab_in, r.tab))
    small = [pltpu.make_async_copy(a, b, r.load_sem.at[i]) for i, (a, b) in enumerate(parts)]
    for c in loads + small:
        c.start()
    for a, b in zip(loads, stores):
        a.wait()
        b.start()
    for c in small:
        c.wait()
    small_names = ("owi", "owo", "oci", "oco", "oew", "orw", "otab", "o0", "o1", "o2", "o3", "o4", "o5")
    held = {name: getattr(r, name + "_held") for name in small_names}
    held["owi"][...] = r.sum1[0 : z.rows, 0 : 3 * D]
    held["owo"][...] = r.sum1[0 : z.rows, 3 * D : 4 * D]
    held["oci"][...] = r.sum2[:, 0 : 3 * D]
    held["oco"][...] = r.sum2[:, 3 * D : 4 * D]
    held["oew"][...] = r.sum2[:, 4 * D : 4 * D + z.FF]
    for i in range(z.FF // D):
        held["orw"][i * z.rows : (i + 1) * z.rows, :] = r.sum2[:, 4 * D + z.FF + i * D : 4 * D + z.FF + (i + 1) * D]
    for i in range(6):
        held[f"o{i}"][...] = r.vec[i : i + 1, 0 : z.rows] if i > 1 else r.sum1[z.rpad + i : z.rpad + i + 1, 0 : z.rows]
    held["otab"][...] = r.tab[0:HEADS, 0 : held["otab"].shape[1]]
    outs = [pltpu.make_async_copy(held[name], getattr(r, name), r.small_sem.at[i]) for i, name in enumerate(small_names)]
    for c in outs:
        c.start()
    for c in outs:
        c.wait()
    for c in stores:
        c.wait()


def dma(*shape):
    return pltpu.SemaphoreType.DMA(shape)


def body(mesh, inputs, out_grad, lowest_level, bias_index, first_gain, first_shift, window_in, window_out, earth_bias,
         second_gain, second_shift, column_in, column_out, third_gain, third_shift, expand_weight, reduce_weight):
    z = Sizes(mesh, inputs, out_grad, expand_weight)
    S, L, LV, W, C, CB, NCH, A, FF, nt, nl = z.S, z.L, z.LV, z.W, z.C, z.CB, z.NCH, HEADS * WIN, z.FF, z.nt, z.nl
    lanes = 4 * D + 2 * FF
    tab_lanes = z.bands * RELB
    tab_half = -(-tab_lanes // 256) * 128
    g = out_grad.transpose(0, 1, 3, 2, 4).reshape(S, LV, z.cells * W, D)
    row = lambda a: a.reshape(1, z.rows)
    ins = dict(x=inputs, g=g, lowest=lowest_level, idx=bias_index, tab=earth_bias.T, wi=window_in, wo=window_out,
               ci=column_in, co=column_out, ew=expand_weight, rw=reduce_weight, v0=row(first_gain), v1=row(first_shift),
               v2=row(second_gain), v3=row(second_shift), v4=row(third_gain), v5=row(third_shift))
    outs = dict(out=(g.shape, BF), dx=(inputs.shape, BF), osum1=((z.rpad + 8, 4 * D), F32), osum2=((z.rows, lanes), F32),
                ovec=((8, 128), F32), otab=((8, 2 * tab_half), F32))
    tokens = pltpu.VMEM((S * L, W, WIN, D), BF)
    slabs = ((z.rpad + 8, 4 * D), (z.rows, lanes))
    sums = ((z.rpad + 8, 4 * D), (z.rows, lanes))
    scratch = dict(xv=tokens, xhv=tokens, qv=tokens, kv=tokens, vv=tokens, ov=tokens, pv=pltpu.VMEM((S * L, W, WIN, A), BF),
                   gv=pltpu.VMEM((S * NCH, LV, C, D), BF), xs=pltpu.VMEM((S * L, nl, NCH, CB, 128), BF),
                   x1r=pltpu.VMEM((S, LV, NCH, CB, 128), BF), ys=pltpu.VMEM((S * NCH, LV, CB, 128), BF),
                   dxr=pltpu.VMEM((S, L, nl, NCH, CB, 128), BF),                    bias=pltpu.VMEM((z.bands, WIN, A), F32), bbuf=pltpu.VMEM((max(z.bands * 8 * WIN, 4 * W * WIN), 128), F32),
                   idxt=pltpu.VMEM((128, 128), jnp.int32), key=pltpu.VMEM((LV * 8, HEADS * LV * 8), F32),
                   low=pltpu.VMEM((S, W // 8, z.cells, HEADS * LV * 8), F32),
                   wide=pltpu.VMEM((D, lanes), F32), widef=pltpu.VMEM((FF, D), F32), gs=pltpu.VMEM((8, D), F32),
                   win=pltpu.VMEM((3, D, D), BF), wout=pltpu.VMEM((D, D), BF), cin=pltpu.VMEM((3, D, D), BF),
                   cout=pltpu.VMEM((D, D), BF), ewf=pltpu.VMEM((D, FF), BF), rwf=pltpu.VMEM((FF, D), BF),
                   dwin=pltpu.VMEM((3, D, D), F32), dwout=pltpu.VMEM((D, D), F32), dcin=pltpu.VMEM((3, D, D), F32),
                   dcout=pltpu.VMEM((D, D), F32), dew=pltpu.VMEM((D, FF), F32), drw=pltpu.VMEM((FF, D), F32), dgs=pltpu.VMEM((8, D), F32), dsum=pltpu.VMEM((8, D), F32),
                   ts=pltpu.VMEM((8, 2 * tab_half), BF), tt=pltpu.VMEM((8, tab_half), BF), th=pltpu.VMEM((8, tab_half), BF),
                   tr=pltpu.VMEM((nl - 1, 8, tab_half), BF))
    for i, sh in enumerate(slabs):
        scratch.update({f"w{i + 1}s": pltpu.VMEM((1,) + sh, BF), f"w{i + 1}r": pltpu.VMEM((nt,) + sh, BF)})
    for i, (n, m) in enumerate(sums):
        part = (n, m // 2)
        scratch.update({f"g{i + 1}s": pltpu.VMEM((nt, n, m), BF), f"g{i + 1}t": pltpu.VMEM((nt,) + part, BF),
                        f"g{i + 1}h": pltpu.VMEM((nt,) + part, BF), f"g{i + 1}r": pltpu.VMEM((nt - 1,) + part, BF),
                        f"h{i + 1}s": pltpu.VMEM(part, BF), f"h{i + 1}r": pltpu.VMEM((nl - 1,) + part, BF)})
    scratch.update(g3s=pltpu.VMEM((nt, 8, 128), BF), g3r=pltpu.VMEM((nt - 1, 8, 128), BF), h3s=pltpu.VMEM((8, 128), BF),
                   h3r=pltpu.VMEM((nl - 1, 8, 128), BF))
    scratch.update(x_sem=dma(S * L), dx_sem=dma(S * L), g_sem=dma(S * NCH), out_sem=dma(S * NCH), w_send=dma(2, nt - 1), w_recv=dma(2, nt - 1),
                   wt_send=dma(2), wt_recv=dma(2), s_send=dma(S * L * NCH, nl - 1), s_recv=dma(S * L * NCH, nl - 1), s_own=dma(S * L * NCH),
                   b_send=dma(S * NCH, nl - 1), b_recv=dma(S * NCH, nl - 1), b_own=dma(S * NCH),
                   gt_send=dma(2), gt_recv=dma(2), g_send=dma(2, nt - 1), g_recv=dma(2, nt - 1), h_send=dma(2, nl - 1), h_recv=dma(2, nl - 1),
                   tt_send=dma(1), tt_recv=dma(1), t_send=dma(nl - 1), t_recv=dma(nl - 1),
                   n_send=dma(nt - 1), n_recv=dma(nt - 1), m_send=dma(nl - 1), m_recv=dma(nl - 1))
    for name, out in (("sum1", "osum1"), ("sum2", "osum2"), ("vecv", "ovec"), ("tabv", "otab")):
        scratch[name] = pltpu.VMEM(*outs[out])
    scratch["o_sem"] = dma(4)
    hbm = ("x", "g") + tuple(outs)
    place = lambda name: pl.BlockSpec(memory_space=pl.ANY if name in hbm else pltpu.VMEM)
    done = dict(zip(outs, pl.pallas_call(
        functools.partial(layer_kernel, z, tuple(ins) + tuple(outs) + tuple(scratch)),
        in_specs=[place(name) for name in ins],
        out_specs=[place(name) for name in outs],
        out_shape=[jax.ShapeDtypeStruct(*o) for o in outs.values()],
        scratch_shapes=list(scratch.values()),
        compiler_params=pltpu.CompilerParams(vmem_limit_bytes=VMEM_LIMIT, collective_id=0, has_side_effects=True),
        name="layer",
    )(*ins.values())))
    last_in = dict(out0=done["out"], dx0=done["dx"], sum1_in=done["osum1"], sum2_in=done["osum2"], vec_in=done["ovec"], tab_in=done["otab"])
    last = dict(out=(g.shape, BF), dx=(inputs.shape, BF), owi=((z.rows, 3 * D), F32), owo=((z.rows, D), F32),
                oci=((z.rows, 3 * D), F32), oco=((z.rows, D), F32), oew=((z.rows, FF), F32), orw=((z.frows, D), F32),
                otab=((HEADS, tab_lanes), F32), **{f"o{i}": ((1, z.rows), F32) for i in range(6)})
    pieces = 1
    place = lambda name: pl.BlockSpec(memory_space=pl.ANY)
    small_out = [n for n in last if n not in ("out", "dx")]
    held = dict(sum1=done["osum1"], sum2=done["osum2"], vec=done["ovec"], tab=done["otab"])
    end = dict(zip(last, pl.pallas_call(
        functools.partial(finish_kernel, z, tuple(last_in) + tuple(last) + tuple(held) + tuple(n + "_held" for n in small_out) + ("out_mid", "dx_mid", "sem", "load_sem", "small_sem"), pieces),
        in_specs=[place(name) for name in last_in],
        out_specs=[place(name) for name in last],
        out_shape=[jax.ShapeDtypeStruct(*o) for o in last.values()],
        scratch_shapes=[pltpu.VMEM(a.shape, F32) for a in held.values()] + [pltpu.VMEM(*last[n]) for n in small_out]
        + [pltpu.VMEM(g.shape, BF), pltpu.VMEM(inputs.shape, BF), dma(2, 4 * S * pieces), dma(4), dma(len(small_out))],
        compiler_params=pltpu.CompilerParams(vmem_limit_bytes=VMEM_LIMIT),
        name="finish",
    )(*last_in.values())))
    output = end["out"].reshape(S, LV, z.cells, W, D).transpose(0, 1, 3, 2, 4)
    v = [end[f"o{i}"].reshape(z.rows) for i in range(6)]
    return (output, end["dx"], v[0], v[1], end["owi"], end["owo"], end["otab"].T, v[2], v[3],
            end["oci"], end["oco"], v[4], v[5], end["oew"], end["orw"])


def solution(mesh):
    t, t2 = P("tile"), P("tile", None)
    level_tokens = P(None, "lev", "tile", None, None)
    column_tokens = P(None, None, "tile", "lev", None)
    placed = (level_tokens, column_tokens, P(None, "tile", "lev"), P(), t, t, t2, t2, t2, t, t, t2, t2, t, t, t2, t2)
    outs = (column_tokens, level_tokens, t, t, t2, t2, t2, t, t, t2, t2, t, t, t2, t2)
    return jax.shard_map(functools.partial(body, mesh), mesh=mesh, in_specs=placed, out_specs=outs, check_vma=False)
```

```python
import functools

import jax
import jax.numpy as jnp
from jax import lax
from jax.experimental import pallas as pl
from jax.experimental.pallas import tpu as pltpu
from jax.sharding import PartitionSpec as P

HEADS = 6
HEAD_DIM = 32
D = HEADS * HEAD_DIM
WIN = 72
RELB = 828
RELP = 832
NWLON = 2
EPSILON = 1e-05
SCALE = HEAD_DIM ** (-0.5)
LOG2E = 1.4426950408889634
MASKED = -1e30
F32 = jnp.float32
BF = jnp.bfloat16
MESH = pl.DeviceIdType.MESH
VMEM_LIMIT = 60 << 20
BATCH_F, BATCH_C, BATCH_B = 16, 12, 8


def dot(a, b, ca=1, cb=0):
    return lax.dot_general(a, b, (((ca,), (cb,)), ((), ())), preferred_element_type=F32)


def lane_heads():
    lane = lax.broadcasted_iota(jnp.int32, (1, 128), 1)
    return [(lane // HEAD_DIM == h).astype(F32) for h in range(4)], [lane < HEAD_DIM * (h + 1) for h in range(3)]


def spread(v, marks, factor=None):
    n = v.shape[0]
    low, high = v[:, :128], v[:, 128:]
    tops = [m if factor is None else m * factor for m in marks]
    if n == 64:
        low, high = low.astype(BF), high.astype(BF)
        tops = [m.astype(BF) for m in tops]
        first = jnp.concatenate([low * m for m in tops], axis=0)
        return first, jnp.concatenate([high * m[:, :64] for m in tops[:2]], axis=0)
    parts = [low * m for m in tops]
    cut = 256 - 3 * n
    first = jnp.concatenate(parts[:3] + [parts[3][:cut]], axis=0).astype(BF)
    head3 = jnp.concatenate([parts[3][cut:], jnp.zeros((n - cut, 64), F32)], axis=1)
    blank = jnp.zeros((n, 128), F32)
    rest = [jnp.concatenate([blank, high * m[:, :64]], axis=1) for m in tops[:2]]
    return first, jnp.concatenate([head3] + rest, axis=0).astype(BF)


def scores(k, spread_q):
    first, rest = spread_q
    right = k[:, 128:] if rest.shape[1] == 64 else k
    return jnp.concatenate([dot(k[:, :128], first, 1, 1), dot(right, rest, 1, 1)], axis=1)


def weigh(p, spread_v):
    first, rest = spread_v
    low, high = dot(p[:, :256], first), dot(p[:, 256:], rest)
    if rest.shape[1] == 64:
        return jnp.concatenate([low, high], axis=1)
    return jnp.concatenate([low + high[:, :128], high[:, 128:]], axis=1)


def mix(p, v, bounds):
    n = v.shape[0]
    first = dot(p[:, :256], v[:, :128], 0, 0)
    if n == 64:
        rest = dot(p[:, 256:], v[:, 128:], 0, 0)
        head3, tail = first[3 * n :], rest
    else:
        rest = dot(p[:, 256:], v, 0, 0)
        cut = 4 * n - 256
        head3, tail = jnp.concatenate([first[3 * n :], rest[:cut, :128]], axis=0), rest[cut:, 128:]
    low = jnp.where(bounds[0], first[:n], jnp.where(bounds[1], first[n : 2 * n], jnp.where(bounds[2], first[2 * n : 3 * n], head3)))
    high = jnp.where(bounds[0][:, :64], tail[:n], tail[n:])
    return jnp.concatenate([low, high], axis=1)


def norm(x):
    mean = jnp.sum(x, -1, keepdims=True) * (1.0 / D)
    c = x - mean
    var = jnp.sum(c * c, -1, keepdims=True) * (1.0 / D)
    r = lax.rsqrt(var + EPSILON)
    return c * r, r


def norm_back(xh, r, dn, gain, sums=True):
    t = dn * gain
    a = jnp.sum(t, -1, keepdims=True) * (1.0 / D)
    b = jnp.sum(t * xh, -1, keepdims=True) * (1.0 / D)
    dx = r * (t - a - xh * b)
    if not sums:
        return dx
    return dx, jnp.sum(dn * xh, 0, keepdims=True), jnp.sum(dn, 0, keepdims=True)


def softmax2(st):
    e = jnp.exp2(st - jnp.max(st, 0, keepdims=True))
    return e * (1.0 / jnp.sum(e, 0, keepdims=True))


def moved(rows, by):
    if isinstance(rows, slice):
        return slice(rows.start + by, rows.stop + by)
    return pl.ds(rows.start + by, rows.size, stride=rows.stride)


def put(ref, base, tall, rows, v):
    n = v.shape[0]
    ref[moved(rows, base), :] = v[:, :128]
    ref[moved(rows, base + tall), :] = jnp.concatenate([v[:, 128:], jnp.zeros((n, 256 - D), F32)], axis=1)


def take(ref, base, tall, rows):
    return jnp.concatenate([ref[moved(rows, base), :], ref[moved(rows, base + tall), :][:, : D - 128]], axis=1)


def fold(ref, at, v):
    c = v.shape[0]
    ref[at + (slice(0, c),)] = v[:, :128].astype(BF)
    tail = jnp.concatenate([v[: c // 2, 128:], v[c // 2 :, 128:]], axis=1)
    ref[at + (slice(c, c + c // 2),)] = tail.astype(BF)


def unfold(block):
    c = block.shape[0] * 2 // 3
    wide = block.astype(F32)
    tail = wide[c:]
    return jnp.concatenate([wide[:c], jnp.concatenate([tail[:, :64], tail[:, 64:]], axis=0)], axis=1)


def one_hot(idx_ref, j):
    entry = lax.broadcasted_iota(jnp.int32, (RELP, 128), 0)
    return (entry == idx_ref[j : j + 1, :]).astype(F32).astype(BF)


def announce(axes):
    sem = pltpu.get_barrier_semaphore()
    count = 0
    for axis, size in axes:
        me = lax.axis_index(axis)
        for j in range(1, size):
            pl.semaphore_signal(sem, inc=1, device_id={axis: lax.rem(me + j, size)}, device_id_type=MESH)
            count += 1
    return sem, count


def to_peer(axis, size, j, src, dst, send, recv):
    me = lax.axis_index(axis)
    return pltpu.make_async_remote_copy(
        src_ref=src, dst_ref=dst, send_sem=send, recv_sem=recv,
        device_id={axis: lax.rem(me + j, size)}, device_id_type=MESH,
    )


def rows_to_lanes(m, n):
    return jnp.concatenate([m[i : i + n] for i in range(0, m.shape[0], n)], axis=1)


class Sizes:
    def __init__(self, mesh, inputs, out_grad, expand):
        self.nl = mesh.shape["lev"]
        self.nt = mesh.shape["tile"]
        self.S, self.L, self.W = inputs.shape[:3]
        self.LV = out_grad.shape[1]
        self.cells = out_grad.shape[3]
        self.bands = self.W // NWLON
        self.rows = D // self.nt
        self.rpad = -(-self.rows // 8) * 8
        self.FF = expand.shape[1]
        self.frows = self.FF // self.nt
        self.T = 6 if self.cells % 6 == 0 else 3
        self.NCH = self.cells // self.T
        self.C = self.T * self.W
        self.CB = self.C * 3 // 2


def lane_pad(m, width, value=0.0):
    if m.shape[1] == width:
        return m
    return jnp.concatenate([m, jnp.full((m.shape[0], width - m.shape[1]), value, F32)], axis=1)


def pairs(count, before, step, after):
    def two(i, _):
        for k in range(2):
            before(2 * i + k)
        for k in range(2):
            step(2 * i + k, k)
        for k in range(2):
            after(2 * i + k)
        return 0

    lax.fori_loop(0, count // 2, two, 0)


def singles(count, before, step, after):
    def one(i, _):
        before(i)
        step(i, 0)
        after(i)
        return 0

    lax.fori_loop(0, count, one, 0)


class Sems:
    pass


def layer_kernel(z, names, *refs):
    r = Sems()
    for name, ref in zip(names, refs):
        setattr(r, name, ref)
    me_l, me_t = lax.axis_index("lev"), lax.axis_index("tile")
    S, L, LV, W, C, NCH = z.S, z.L, z.LV, z.W, z.C, z.NCH
    TOK = W * WIN
    TABH = r.th.shape[-1]
    marks, bounds = lane_heads()

    def load_x(i):
        return pltpu.make_async_copy(r.x.at[i // L, lax.rem(i, L)], r.xv.at[i], r.x_sem.at[i])

    def store_x(i):
        return pltpu.make_async_copy(r.xv.at[i], r.dx.at[i // L, lax.rem(i, L)], r.dx_sem.at[i])

    def load_g(i):
        rows = pl.ds(pl.multiple_of(lax.rem(i, NCH) * C, 16), C)
        return pltpu.make_async_copy(r.g.at[i // NCH, :, rows, :], r.gv.at[i], r.g_sem.at[i])

    def store_out(i):
        rows = pl.ds(pl.multiple_of(lax.rem(i, NCH) * C, 16), C)
        return pltpu.make_async_copy(r.gv.at[i], r.out.at[i // NCH, :, rows, :], r.out_sem.at[i])

    core, twin = lax.rem(me_l, 2), me_l + 1 - 2 * lax.rem(me_l, 2)

    def to_twin(src, dst, send, recv):
        return pltpu.make_async_remote_copy(src_ref=src, dst_ref=dst, send_sem=send, recv_sem=recv,
                                            device_id={"lev": twin}, device_id_type=MESH)

    def half(ref, which):
        width = ref.shape[-1] // 2
        return ref.at[:, :, pl.ds(pl.multiple_of(which * width, 128), width)]

    weights = ((r.w1s, r.w1r), (r.w2s, r.w2r))

    def weight_copy(i, j):
        src, dst = weights[i]
        return to_peer("tile", z.nt, j, half(src, core).at[0], half(dst, core).at[me_t], r.w_send.at[i, j - 1], r.w_recv.at[i, j - 1])

    def weight_pass(i):
        part = half(weights[i][1], core)
        return to_twin(part, part, r.wt_send.at[i], r.wt_recv.at[i])

    def weight_start(i):
        for j in range(1, z.nt):
            weight_copy(i, j).start()
        src, dst = weights[i]
        width = src.shape[-1] // 2
        own = pl.ds(pl.multiple_of(core * width, 128), width)
        dst[pl.ds(me_t, 1), :, own] = src[:, :, own]

    def weight_hand(i):
        for j in range(1, z.nt):
            weight_copy(i, j).wait_recv()
        weight_pass(i).start()

    def stream_copy(i, c, j):
        return to_peer("lev", z.nl, j, r.xs.at[i, lax.rem(me_l + j, z.nl), c], r.x1r.at[i // L, me_l * L + lax.rem(i, L), c],
                       r.s_send.at[i * NCH + c, j - 1], r.s_recv.at[i * NCH + c, j - 1])

    def stream_own(i, c):
        return pltpu.make_async_copy(r.xs.at[i, me_l, c], r.x1r.at[i // L, me_l * L + lax.rem(i, L), c], r.s_own.at[i * NCH + c])

    def back_copy(i, j):
        return to_peer("lev", z.nl, j, r.ys.at[i, pl.ds(lax.rem(me_l + j, z.nl) * L, L)],
                       r.dxr.at[i // NCH, :, me_l, lax.rem(i, NCH)], r.b_send.at[i, j - 1], r.b_recv.at[i, j - 1])

    def back_own(i):
        return pltpu.make_async_copy(r.ys.at[i, pl.ds(me_l * L, L)], r.dxr.at[i // NCH, :, me_l, lax.rem(i, NCH)], r.b_own.at[i])

    grads = ((r.g1s, r.g1t, r.g1h, r.g1r, r.h1s, r.h1r), (r.g2s, r.g2t, r.g2h, r.g2r, r.h2s, r.h2r))

    def core_copy(i):
        return to_twin(half(grads[i][0], 1 - core), grads[i][1], r.gt_send.at[i], r.gt_recv.at[i])

    def tile_copy(i, j):
        src, dst = grads[i][2], grads[i][3]
        return to_peer("tile", z.nt, j, src.at[lax.rem(me_t + j, z.nt)], dst.at[j - 1], r.g_send.at[i, j - 1], r.g_recv.at[i, j - 1])

    def lev_copy(i, j):
        return to_peer("lev", z.nl, j, grads[i][4], grads[i][5].at[j - 1], r.h_send.at[i, j - 1], r.h_recv.at[i, j - 1])

    def sum_cores(i):
        core_copy(i).wait_recv()
        gs, gt, gh = grads[i][:3]
        width = gt.shape[-1]
        mine = gs[:, :, pl.ds(pl.multiple_of(core * width, 128), width)]
        gh[...] = (mine.astype(F32) + gt[...].astype(F32)).astype(BF)
        for j in range(1, z.nt):
            tile_copy(i, j).start()

    def sum_tiles(i):
        gh, gr, hs = grads[i][2:5]
        total = gh[pl.ds(me_t, 1)][0].astype(F32)
        for j in range(1, z.nt):
            tile_copy(i, j).wait_recv()
            total = total + gr[j - 1].astype(F32)
        hs[...] = total.astype(BF)
        for j in range(1, z.nl):
            lev_copy(i, j).start()

    def sum_halves(own, got, out):
        mine, other = own[...].astype(F32), 0.0
        for j in range(1, z.nl):
            if j % 2 == 0:
                mine = mine + got[j - 1].astype(F32)
            else:
                other = other + got[j - 1].astype(F32)
        width = own.shape[-1]
        first = core == 0
        out[:, 0:width] = jnp.where(first, mine, other)
        out[:, width : 2 * width] = jnp.where(first, other, mine)

    def sum_lev(i, out):
        for j in range(1, z.nl):
            lev_copy(i, j).wait_recv()
        sum_halves(grads[i][4], grads[i][5], out)

    def leave(i):
        src, dst = ((r.sum1, r.osum1), (r.sum2, r.osum2), (r.vecv, r.ovec), (r.tabv, r.otab))[i]
        return pltpu.make_async_copy(src, dst, r.o_sem.at[i])

    def tab_core_copy():
        part = r.ts.at[:, pl.ds(pl.multiple_of((1 - core) * TABH, 128), TABH)]
        return to_twin(part, r.tt, r.tt_send.at[0], r.tt_recv.at[0])

    def tab_cores():
        tab_core_copy().wait_recv()
        mine = r.ts[:, pl.ds(pl.multiple_of(core * TABH, 128), TABH)]
        r.th[...] = (mine.astype(F32) + r.tt[...].astype(F32)).astype(BF)
        for j in range(1, z.nl):
            tab_copy(j).start()

    def tab_copy(j):
        return to_peer("lev", z.nl, j, r.th, r.tr.at[j - 1], r.t_send.at[j - 1], r.t_recv.at[j - 1])

    def norm_tile_copy(j):
        return to_peer("tile", z.nt, j, r.g3s.at[lax.rem(me_t + j, z.nt)], r.g3r.at[j - 1], r.n_send.at[j - 1], r.n_recv.at[j - 1])

    def norm_lev_copy(j):
        return to_peer("lev", z.nl, j, r.h3s, r.h3r.at[j - 1], r.m_send.at[j - 1], r.m_recv.at[j - 1])

    sem, count = announce((("lev", z.nl), ("tile", z.nt)))
    for i in range(S * L):
        load_x(i).start()
    for i in range(S * NCH):
        load_g(i).start()
    r.w1s[...] = jnp.zeros(r.w1s.shape, BF)
    r.w1s[0, 0 : z.rows, 0 : 3 * D] = r.wi[...]
    r.w1s[0, 0 : z.rows, 3 * D : 4 * D] = r.wo[...]
    for i, vec in enumerate((r.v0, r.v1, r.v2, r.v3, r.v4, r.v5)):
        r.w1s[0, z.rpad + i : z.rpad + i + 1, 0 : z.rows] = vec[...]
    r.w2s[0, :, 0 : 3 * D] = r.ci[...]
    r.w2s[0, :, 3 * D : 4 * D] = r.co[...]
    r.w2s[0, :, 4 * D : 4 * D + z.FF] = r.ew[...]
    r.w2s[0, :, 4 * D + z.FF :] = rows_to_lanes(r.rw[...].astype(F32), z.rows).astype(BF)
    entries = lane_pad(r.idx[...].astype(F32), 128, -1.0)
    entries = jnp.concatenate([entries, jnp.full((128 - WIN, 128), -1.0, F32)], axis=0)
    r.idxt[...] = jnp.transpose(entries).astype(jnp.int32)
    cells8 = lax.broadcasted_iota(jnp.int32, (LV * 8, HEADS * LV * 8), 0)
    lane8 = lax.broadcasted_iota(jnp.int32, (LV * 8, HEADS * LV * 8), 1)
    r.key[...] = jnp.where(cells8 % 8 == lane8 % 8, (cells8 // 8).astype(F32), -1.0)
    wrow = lax.broadcasted_iota(jnp.int32, (W, HEADS * LV * 8), 0)
    wlane = lax.broadcasted_iota(jnp.int32, (W, HEADS * LV * 8), 1)
    for part in range(W // 8):
        pick = (wrow == wlane % 8 + 8 * part).astype(F32).astype(BF)
        for s in range(S):
            r.low[s, part] = dot(r.lowest[s].astype(F32).astype(BF), pick, 0, 0)
    r.ts[...] = jnp.zeros(r.ts.shape, BF)
    pl.semaphore_wait(sem, count)
    weight_start(0)
    table = r.tab[...].astype(F32)
    pads = jnp.zeros((8 - HEADS, RELP), F32)
    table = jnp.concatenate(
        [jnp.concatenate([lane_pad(table[:, b * RELB : (b + 1) * RELB], RELP), pads], axis=0) for b in range(z.bands)], axis=0
    ).astype(BF)
    n8 = z.bands * 8
    for j in range(0, WIN, 2):
        both = jnp.concatenate([one_hot(r.idxt, j), one_hot(r.idxt, j + 1)], axis=1)
        vals = dot(table, both) * LOG2E
        r.bbuf[pl.ds(j, n8, stride=WIN), :] = vals[:, :128]
        r.bbuf[pl.ds(j + 1, n8, stride=WIN), :] = vals[:, 128:]
    def normalize(i, _):
        load_x(i).wait()
        r.xhv[i] = norm(r.xv[i].astype(F32).reshape(TOK, D))[0].reshape(W, WIN, D).astype(BF)
        return 0

    lax.fori_loop(0, S * L // 2, normalize, 0)
    weight_hand(0)
    lax.fori_loop(S * L // 2, S * L, normalize, 0)
    weight_start(1)
    for b in range(z.bands):
        r.bias[b] = jnp.concatenate(
            [r.bbuf[(b * 8 + h) * WIN : (b * 8 + h + 1) * WIN, :][:, :WIN] for h in range(HEADS)], axis=1
        )
    for ref in (r.dcin, r.dcout, r.dew, r.drw, r.dwin, r.dwout, r.dgs, r.dsum):
        ref[...] = jnp.zeros(ref.shape, F32)
    weight_pass(0).wait_recv()
    for t in range(z.nt):
        r.wide[t * z.rows : (t + 1) * z.rows, 0 : 4 * D] = r.w1r[t, 0 : z.rows, :].astype(F32)
    for i in range(3):
        r.win[i] = r.wide[:, i * D : (i + 1) * D].astype(BF)
    r.wout[...] = r.wide[:, 3 * D : 4 * D].astype(BF)
    r.gs[...] = jnp.concatenate([r.w1r[t, z.rpad : z.rpad + 8, :].astype(F32)[:, : z.rows] for t in range(z.nt)], axis=1)
    gain1, shift1, g2, s2, g3, s3 = (r.gs[i : i + 1, :] for i in range(6))

    def window_step(i, slot):
        n1 = (r.xhv[i].astype(F32).reshape(TOK, D) * gain1 + shift1).astype(BF)
        q, k, v = (dot(n1, r.win[m]) for m in range(3))
        mixed = []
        for b0 in range(0, W, BATCH_F):
            batch = range(b0, b0 + BATCH_F)
            cut = {w: slice(w * WIN, (w + 1) * WIN) for w in batch}
            kb = {w: k[cut[w]].astype(BF) for w in batch}
            vb = {w: v[cut[w]].astype(BF) for w in batch}
            for w in batch:
                r.qv[i, w] = q[cut[w]].astype(BF)
                r.kv[i, w] = kb[w]
                r.vv[i, w] = vb[w]
            sq = {w: spread(q[cut[w]], marks, SCALE * LOG2E) for w in batch}
            st = {w: scores(kb[w], sq[w]) + r.bias[w // NWLON] for w in batch}
            pb = {w: softmax2(st[w]).astype(BF) for w in batch}
            for w in batch:
                r.pv[i, w] = pb[w]
            mixed += [mix(pb[w], vb[w], bounds) for w in batch]
        o = jnp.concatenate(mixed, axis=0).astype(BF)
        r.ov[i] = o.astype(F32).reshape(W, WIN, D).astype(BF)
        x1 = r.xv[i].astype(F32).reshape(TOK, D) + dot(o, r.wout[...])
        for w in range(W):
            put(r.bbuf, 2 * TOK * slot, TOK, pl.ds(w, WIN, stride=W), x1[w * WIN : (w + 1) * WIN])
        for d in range(z.nl):
            for c in range(NCH):
                at = (d * NCH + c) * C
                fold(r.xs, (i, d, c), take(r.bbuf, 2 * TOK * slot, TOK, slice(at, at + C)))

    def window_before(i):
        @pl.when(i == S * L - 1)
        def _():
            weight_hand(1)

    def window_after(i):
        for c in range(NCH):
            for j in range(1, z.nl):
                stream_copy(i, c, j).start()
            stream_own(i, c).start()

    singles(S * L, window_before, window_step, window_after)

    weight_pass(1).wait_recv()
    for t in range(z.nt):
        r.wide[t * z.rows : (t + 1) * z.rows, :] = r.w2r[t].astype(F32)
        for i in range(z.FF // D):
            at = t * z.frows + i * z.rows
            r.widef[at : at + z.rows, :] = r.w2r[t].astype(F32)[:, 4 * D + z.FF + i * D : 4 * D + z.FF + (i + 1) * D]
    for i in range(3):
        r.cin[i] = r.wide[:, i * D : (i + 1) * D].astype(BF)
    r.cout[...] = r.wide[:, 3 * D : 4 * D].astype(BF)
    r.ewf[...] = r.wide[:, 4 * D : 4 * D + z.FF].astype(BF)
    r.rwf[...] = r.widef[...].astype(BF)
    r.bias[...] = jnp.zeros(r.bias.shape, F32)

    groups, R, GR = C // 8, LV * C, LV * 8
    halves = W // 8

    def cols(m, j):
        return m.reshape(LV, C, D)[:, j * 8 : (j + 1) * 8, :].reshape(GR, D)

    def join(parts):
        return jnp.concatenate([p.reshape(LV, 8, D) for p in parts], axis=1).reshape(R, D)

    def column_step(i, slot):
        s, ch = i // NCH, lax.rem(i, NCH)

        x1 = jnp.concatenate([unfold(r.x1r[s, m, ch]) for m in range(LV)], axis=0)
        xh2, r2 = norm(x1)
        n2 = (xh2 * g2 + s2).astype(BF)
        gb = r.gv[i].astype(F32).reshape(R, D).astype(BF)
        dh = dot(gb, r.rwf[...] * 0.5, 1, 1).astype(BF)
        q, k, v = (dot(n2, r.cin[m]) for m in range(3))
        key = r.key[...]
        mixed = []
        qb, kb, vb, pb = {}, {}, {}, {}
        for b0 in range(0, groups, BATCH_C):
            batch = range(b0, min(b0 + BATCH_C, groups))
            for j in batch:
                kb[j], vb[j] = cols(k, j).astype(BF), cols(v, j).astype(BF)
                qb[j] = spread(cols(q, j), marks, SCALE * LOG2E)
            st = {j: scores(kb[j], qb[j]) for j in batch}
            for j in batch:
                low = r.low[s, j % halves, pl.ds(ch * z.T + j // halves, 1), :]
                pb[j] = softmax2(jnp.where(key >= low, st[j], MASKED)).astype(BF)
            mixed += [mix(pb[j], vb[j], bounds) for j in batch]
        o2 = join(mixed).astype(BF)
        x2 = x1 + dot(o2, r.cout[...])
        xh3, r3 = norm(x2)
        n3 = (xh3 * g3 + s3).astype(BF)
        u = dot(n3, r.ewf[...] * 0.5).astype(BF)
        c = 0.7978845608028654
        a = BF(2 * c) + BF(8 * c * 0.044715) * (u * u)
        t = jnp.tanh(u * a)
        up = BF(1.0) + t
        hid = u * up
        du = dh * (up + hid * (BF(1.0) - t) * (BF(3.0) * a - BF(4.0 * c)))
        dn3 = dot(du, r.ewf[...], 1, 1)
        dx, a3, b3 = norm_back(xh3, r3, dn3, g3)
        dx2 = gb.astype(F32) + dx
        dx2b = dx2.astype(BF)
        r.gv[i] = (x2 + dot(hid, r.rwf[...])).reshape(LV, C, D).astype(BF)
        r.drw[...] = r.drw[...] + dot(hid, gb, 0, 0)
        r.dew[...] = r.dew[...] + dot(n3, du, 0, 0)
        r.dcout[...] = r.dcout[...] + dot(o2, dx2b, 0, 0)
        do = dot(dx2b, r.cout[...], 1, 1)
        dq, dk, dv = [], [], []
        for b0 in range(0, groups, BATCH_C):
            batch = range(b0, min(b0 + BATCH_C, groups))
            dob = {j: spread(cols(do, j), marks) for j in batch}
            dpt = {j: scores(vb[j], dob[j]) for j in batch}
            dv += [weigh(pb[j], dob[j]) for j in batch]
            dsb = {}
            for j in batch:
                pf = pb[j].astype(F32)
                dsb[j] = (pf * (dpt[j] - jnp.sum(dpt[j] * pf, 0, keepdims=True))).astype(BF)
            dk += [weigh(dsb[j], qb[j]) * (1.0 / LOG2E) for j in batch]
            dq += [mix(dsb[j], kb[j], bounds) * SCALE for j in batch]
        dn2 = 0.0
        packs = [join(part).astype(BF) for part in (dq, dk, dv)]
        for m, pack in enumerate(packs):
            dn2 = dn2 + dot(pack, r.cin[m], 1, 1)
        dx, a2, b2 = norm_back(xh2, r2, dn2, g2)
        for m, pack in enumerate(packs):
            r.dcin[m] = r.dcin[m] + dot(n2, pack, 0, 0)
        dx1 = dx2 + dx
        for m in range(LV):
            fold(r.ys, (i, m), dx1[m * C : (m + 1) * C])
        for m, part in enumerate((a2, b2, a3, b3)):
            r.dgs[m + 2 : m + 3, :] = r.dgs[m + 2 : m + 3, :] + part

    def column_before(i):
        s, ch = i // NCH, lax.rem(i, NCH)
        load_g(i).wait()
        for l in range(L):
            stream_own(s * L + l, ch).wait()
            for j in range(1, z.nl):
                stream_copy(s * L + l, ch, j).wait_recv()

    def column_after(i):
        store_out(i).start()
        for j in range(1, z.nl):
            back_copy(i, j).start()
        back_own(i).start()

    pairs(S * NCH, column_before, column_step, column_after)

    for t in range(z.nt):
        rows = slice(t * z.rows, (t + 1) * z.rows)
        for i in range(3):
            r.g2s[t, :, i * D : (i + 1) * D] = r.dcin[i, rows, :].astype(BF)
        r.g2s[t, :, 3 * D : 4 * D] = r.dcout[rows, :].astype(BF)
        r.g2s[t, :, 4 * D : 4 * D + z.FF] = r.dew[rows, :].astype(BF)
        r.g2s[t, :, 4 * D + z.FF :] = rows_to_lanes(r.drw[t * z.frows : (t + 1) * z.frows, :], z.rows).astype(BF)
    core_copy(1).start()
    for t in range(z.nt):
        r.g3s[t] = lane_pad(r.dgs[:, t * z.rows : (t + 1) * z.rows], 128).astype(BF)
    for j in range(1, z.nt):
        norm_tile_copy(j).start()

    def back_step(i, slot):
        s, l = i // L, lax.rem(i, L)

        for d in range(z.nl):
            for c in range(NCH):
                at = (d * NCH + c) * C
                put(r.bbuf, 2 * TOK * slot, TOK, slice(at, at + C), unfold(r.dxr[s, l, d, c]))
        xhs, dqs, dks, dvs, d1s, os = [], [], [], [], [], []
        for b0 in range(0, W, BATCH_B):
            batch = range(b0, b0 + BATCH_B)
            d1 = jnp.concatenate([take(r.bbuf, 2 * TOK * slot, TOK, pl.ds(w, WIN, stride=W)) for w in batch], axis=0)
            d1b = d1.astype(BF)
            do = dot(d1b, r.wout[...], 1, 1)
            os.append(r.ov[i, b0 : b0 + BATCH_B].astype(F32).reshape(BATCH_B * WIN, D).astype(BF))
            r.dwout[...] = r.dwout[...] + dot(os[-1], d1b, 0, 0)
            dob = {w: spread(do[(w - b0) * WIN : (w - b0 + 1) * WIN], marks) for w in batch}
            qb = {w: spread(r.qv[i, w].astype(F32), marks) for w in batch}
            dpt = {w: scores(r.vv[i, w], dob[w]) for w in batch}
            dv = [weigh(r.pv[i, w], dob[w]) for w in batch]
            dsb = {}
            for w in batch:
                pf = r.pv[i, w].astype(F32)
                ds = pf * (dpt[w] - jnp.sum(dpt[w] * pf, 0, keepdims=True))
                dsb[w] = ds.astype(BF)
                r.bias[w // NWLON] = r.bias[w // NWLON] + ds
            dk = [weigh(dsb[w], qb[w]) * SCALE for w in batch]
            dq = [mix(dsb[w], r.kv[i, w], bounds) * SCALE for w in batch]
            xhs.append(r.xhv[i, b0 : b0 + BATCH_B].astype(F32).reshape(BATCH_B * WIN, D).astype(BF))
            r.ov[i, b0 : b0 + BATCH_B] = d1.reshape(BATCH_B, WIN, D).astype(BF)
            d1s.append(d1b)
            for m, (part, parts, keep) in enumerate(((dq, dqs, r.qv), (dk, dks, r.kv), (dv, dvs, r.vv))):
                flat = jnp.concatenate(part, axis=0)
                r.dsum[m : m + 1, :] = r.dsum[m : m + 1, :] + jnp.sum(flat, 0, keepdims=True)
                keep[i, b0 : b0 + BATCH_B] = flat.reshape(BATCH_B, WIN, D).astype(BF)
                parts.append(flat.astype(BF))
        xh = jnp.concatenate(xhs, axis=0)
        for m, part in enumerate((dqs, dks, dvs)):
            r.dwin[m] = r.dwin[m] + dot(xh, jnp.concatenate(part, axis=0), 0, 0)

    def back_before(i):
        s, l = i // L, lax.rem(i, L)

        @pl.when(l == 0)
        def _():
            for c in range(NCH):
                back_own(s * NCH + c).wait()
                for j in range(1, z.nl):
                    back_copy(s * NCH + c, j).wait_recv()

        @pl.when(i == S * L // 2)
        def _():
            sum_cores(1)
            vec = r.g3s[pl.ds(me_t, 1)][0].astype(F32)
            for j in range(1, z.nt):
                norm_tile_copy(j).wait_recv()
                vec = vec + r.g3r[j - 1].astype(F32)
            r.h3s[...] = vec.astype(BF)
            for j in range(1, z.nl):
                norm_lev_copy(j).start()

    def nothing(i):
        pass

    pairs(S * L, back_before, back_step, nothing)

    tall = jnp.concatenate([gain1, shift1, jnp.zeros((126, D), F32)], axis=0)
    tall = jnp.transpose(lane_pad(tall, 256))[:D]
    to_gain, to_shift = 0.0, 0.0
    for i in range(3):
        w, m, c = r.win[i].astype(F32), r.dwin[i], r.dsum[i : i + 1, :]
        to_gain = to_gain + jnp.sum(w * m, 1, keepdims=True)
        to_shift = to_shift + jnp.sum(w * c, 1, keepdims=True)
        r.dwin[i] = tall[:, 0:1] * m + tall[:, 1:2] * c
    lane = lax.broadcasted_iota(jnp.int32, (D, 128), 1)
    flat = jnp.concatenate([jnp.where(lane == 0, to_gain, jnp.where(lane == 1, to_shift, 0.0)), jnp.zeros((256 - D, 128), F32)], axis=0)
    flat = jnp.transpose(flat)
    for t in range(z.nt):
        rows = slice(t * z.rows, (t + 1) * z.rows)
        for i in range(3):
            r.g1s[t, 0 : z.rows, i * D : (i + 1) * D] = r.dwin[i, rows, :].astype(BF)
        r.g1s[t, 0 : z.rows, 3 * D : 4 * D] = r.dwout[rows, :].astype(BF)
        r.g1s[t, z.rpad : z.rpad + 8, :] = lane_pad(flat[0:8, rows], 4 * D).astype(BF)
    core_copy(0).start()
    vec = r.h3s[...].astype(F32)
    for j in range(1, z.nl):
        norm_lev_copy(j).wait_recv()
        vec = vec + r.h3r[j - 1].astype(F32)
    r.vecv[...] = vec
    leave(2).start()

    pads = jnp.zeros((WIN, 128 - WIN), F32)
    for b in range(z.bands):
        for h in range(8):
            at = (b * 8 + h) * WIN
            if h < HEADS:
                r.bbuf[at : at + WIN, :] = jnp.concatenate([r.bias[b, :, h * WIN : (h + 1) * WIN], pads], axis=1)
            else:
                r.bbuf[at : at + WIN, :] = jnp.zeros((WIN, 128), F32)
    tab = jnp.zeros((n8, RELP), F32)
    for j in range(0, WIN, 2):
        if j == WIN // 3:
            sum_cores(0)
        if j == 2 * WIN // 3:
            sum_tiles(1)
        both = jnp.concatenate([one_hot(r.idxt, j), one_hot(r.idxt, j + 1)], axis=1)
        pair = jnp.concatenate([r.bbuf[pl.ds(j, n8, stride=WIN), :], r.bbuf[pl.ds(j + 1, n8, stride=WIN), :]], axis=1)
        tab = tab + dot(pair.astype(BF), both, 1, 1)
    for b in range(z.bands):
        r.ts[:, b * RELB : (b + 1) * RELB] = tab[b * 8 : (b + 1) * 8, :RELB].astype(BF)
    tab_core_copy().start()

    def norm_step(i, slot):
        x = r.xv[i].astype(F32).reshape(TOK, D)
        xh, rs = norm(x)
        dn = 0.0
        for m, kept in enumerate((r.qv, r.kv, r.vv)):
            dn = dn + dot(kept[i].astype(F32).reshape(TOK, D).astype(BF), r.win[m], 1, 1)
        dx = norm_back(xh, rs, dn, gain1, False)
        r.xv[i] = (r.ov[i].astype(F32).reshape(TOK, D) + dx).reshape(W, WIN, D).astype(BF)

    def norm_before(i):
        @pl.when(i == 1)
        def _():
            tab_cores()

        @pl.when(i == S * L - 1)
        def _():
            sum_tiles(0)

    def norm_after(i):
        store_x(i).start()

    singles(S * L, norm_before, norm_step, norm_after)

    sum_lev(1, r.sum2)
    leave(1).start()
    for j in range(1, z.nl):
        tab_copy(j).wait_recv()
    sum_halves(r.th, r.tr, r.tabv)
    leave(3).start()
    sum_lev(0, r.sum1)
    leave(0).start()
    tab_core_copy().wait_send()
    for i in range(2):
        weight_pass(i).wait_send()
        core_copy(i).wait_send()
        for j in range(1, z.nt):
            weight_copy(i, j).wait_send()
            tile_copy(i, j).wait_send()
        for j in range(1, z.nl):
            lev_copy(i, j).wait_send()
    for j in range(1, z.nt):
        norm_tile_copy(j).wait_send()
    for j in range(1, z.nl):
        norm_lev_copy(j).wait_send()
    for j in range(1, z.nl):
        tab_copy(j).wait_send()
        for i in range(S * L):
            for c in range(NCH):
                stream_copy(i, c, j).wait_send()
        for i in range(S * NCH):
            back_copy(i, j).wait_send()
    for i in range(S * L):
        store_x(i).wait()
    for i in range(S * NCH):
        store_out(i).wait()
    for i in range(4):
        leave(i).wait()


def finish_kernel(z, names, pieces, *refs):
    r = Sems()
    for name, ref in zip(names, refs):
        setattr(r, name, ref)
    loads, stores = [], []
    for src, mid, dst in ((r.out0, r.out_mid, r.out), (r.dx0, r.dx_mid, r.dx)):
        n = max(1, src.shape[1] // pieces)
        for s in range(src.shape[0]):
            for p in range(0, src.shape[1], n):
                at = (s, pl.ds(p, n))
                sem = len(stores)
                loads.append(pltpu.make_async_copy(src.at[at], mid.at[at], r.sem.at[0, sem]))
                stores.append(pltpu.make_async_copy(mid.at[at], dst.at[at], r.sem.at[1, sem]))
    parts = ((r.sum1_in, r.sum1), (r.sum2_in, r.sum2), (r.vec_in, r.vec), (r.tab_in, r.tab))
    small = [pltpu.make_async_copy(a, b, r.load_sem.at[i]) for i, (a, b) in enumerate(parts)]
    for c in loads + small:
        c.start()
    for a, b in zip(loads, stores):
        a.wait()
        b.start()
    for c in small:
        c.wait()
    small_names = ("owi", "owo", "oci", "oco", "oew", "orw", "otab", "o0", "o1", "o2", "o3", "o4", "o5")
    held = {name: getattr(r, name + "_held") for name in small_names}
    held["owi"][...] = r.sum1[0 : z.rows, 0 : 3 * D]
    held["owo"][...] = r.sum1[0 : z.rows, 3 * D : 4 * D]
    held["oci"][...] = r.sum2[:, 0 : 3 * D]
    held["oco"][...] = r.sum2[:, 3 * D : 4 * D]
    held["oew"][...] = r.sum2[:, 4 * D : 4 * D + z.FF]
    for i in range(z.FF // D):
        held["orw"][i * z.rows : (i + 1) * z.rows, :] = r.sum2[:, 4 * D + z.FF + i * D : 4 * D + z.FF + (i + 1) * D]
    for i in range(6):
        held[f"o{i}"][...] = r.vec[i : i + 1, 0 : z.rows] if i > 1 else r.sum1[z.rpad + i : z.rpad + i + 1, 0 : z.rows]
    held["otab"][...] = r.tab[0:HEADS, 0 : held["otab"].shape[1]]
    outs = [pltpu.make_async_copy(held[name], getattr(r, name), r.small_sem.at[i]) for i, name in enumerate(small_names)]
    for c in outs:
        c.start()
    for c in outs:
        c.wait()
    for c in stores:
        c.wait()


def dma(*shape):
    return pltpu.SemaphoreType.DMA(shape)


def body(mesh, inputs, out_grad, lowest_level, bias_index, first_gain, first_shift, window_in, window_out, earth_bias,
         second_gain, second_shift, column_in, column_out, third_gain, third_shift, expand_weight, reduce_weight):
    z = Sizes(mesh, inputs, out_grad, expand_weight)
    S, L, LV, W, C, CB, NCH, A, FF, nt, nl = z.S, z.L, z.LV, z.W, z.C, z.CB, z.NCH, HEADS * WIN, z.FF, z.nt, z.nl
    lanes = 4 * D + 2 * FF
    tab_lanes = z.bands * RELB
    tab_half = -(-tab_lanes // 256) * 128
    g = out_grad.transpose(0, 1, 3, 2, 4).reshape(S, LV, z.cells * W, D)
    row = lambda a: a.reshape(1, z.rows)
    ins = dict(x=inputs, g=g, lowest=lowest_level, idx=bias_index, tab=earth_bias.T, wi=window_in, wo=window_out,
               ci=column_in, co=column_out, ew=expand_weight, rw=reduce_weight, v0=row(first_gain), v1=row(first_shift),
               v2=row(second_gain), v3=row(second_shift), v4=row(third_gain), v5=row(third_shift))
    outs = dict(out=(g.shape, BF), dx=(inputs.shape, BF), osum1=((z.rpad + 8, 4 * D), F32), osum2=((z.rows, lanes), F32),
                ovec=((8, 128), F32), otab=((8, 2 * tab_half), F32))
    tokens = pltpu.VMEM((S * L, W, WIN, D), BF)
    slabs = ((z.rpad + 8, 4 * D), (z.rows, lanes))
    sums = ((z.rpad + 8, 4 * D), (z.rows, lanes))
    scratch = dict(xv=tokens, xhv=tokens, qv=tokens, kv=tokens, vv=tokens, ov=tokens, pv=pltpu.VMEM((S * L, W, WIN, A), BF),
                   gv=pltpu.VMEM((S * NCH, LV, C, D), BF), xs=pltpu.VMEM((S * L, nl, NCH, CB, 128), BF),
                   x1r=pltpu.VMEM((S, LV, NCH, CB, 128), BF), ys=pltpu.VMEM((S * NCH, LV, CB, 128), BF),
                   dxr=pltpu.VMEM((S, L, nl, NCH, CB, 128), BF),                    bias=pltpu.VMEM((z.bands, WIN, A), F32), bbuf=pltpu.VMEM((max(z.bands * 8 * WIN, 4 * W * WIN), 128), F32),
                   idxt=pltpu.VMEM((128, 128), jnp.int32), key=pltpu.VMEM((LV * 8, HEADS * LV * 8), F32),
                   low=pltpu.VMEM((S, W // 8, z.cells, HEADS * LV * 8), F32),
                   wide=pltpu.VMEM((D, lanes), F32), widef=pltpu.VMEM((FF, D), F32), gs=pltpu.VMEM((8, D), F32),
                   win=pltpu.VMEM((3, D, D), BF), wout=pltpu.VMEM((D, D), BF), cin=pltpu.VMEM((3, D, D), BF),
                   cout=pltpu.VMEM((D, D), BF), ewf=pltpu.VMEM((D, FF), BF), rwf=pltpu.VMEM((FF, D), BF),
                   dwin=pltpu.VMEM((3, D, D), F32), dwout=pltpu.VMEM((D, D), F32), dcin=pltpu.VMEM((3, D, D), F32),
                   dcout=pltpu.VMEM((D, D), F32), dew=pltpu.VMEM((D, FF), F32), drw=pltpu.VMEM((FF, D), F32), dgs=pltpu.VMEM((8, D), F32), dsum=pltpu.VMEM((8, D), F32),
                   ts=pltpu.VMEM((8, 2 * tab_half), BF), tt=pltpu.VMEM((8, tab_half), BF), th=pltpu.VMEM((8, tab_half), BF),
                   tr=pltpu.VMEM((nl - 1, 8, tab_half), BF))
    for i, sh in enumerate(slabs):
        scratch.update({f"w{i + 1}s": pltpu.VMEM((1,) + sh, BF), f"w{i + 1}r": pltpu.VMEM((nt,) + sh, BF)})
    for i, (n, m) in enumerate(sums):
        part = (n, m // 2)
        scratch.update({f"g{i + 1}s": pltpu.VMEM((nt, n, m), BF), f"g{i + 1}t": pltpu.VMEM((nt,) + part, BF),
                        f"g{i + 1}h": pltpu.VMEM((nt,) + part, BF), f"g{i + 1}r": pltpu.VMEM((nt - 1,) + part, BF),
                        f"h{i + 1}s": pltpu.VMEM(part, BF), f"h{i + 1}r": pltpu.VMEM((nl - 1,) + part, BF)})
    scratch.update(g3s=pltpu.VMEM((nt, 8, 128), BF), g3r=pltpu.VMEM((nt - 1, 8, 128), BF), h3s=pltpu.VMEM((8, 128), BF),
                   h3r=pltpu.VMEM((nl - 1, 8, 128), BF))
    scratch.update(x_sem=dma(S * L), dx_sem=dma(S * L), g_sem=dma(S * NCH), out_sem=dma(S * NCH), w_send=dma(2, nt - 1), w_recv=dma(2, nt - 1),
                   wt_send=dma(2), wt_recv=dma(2), s_send=dma(S * L * NCH, nl - 1), s_recv=dma(S * L * NCH, nl - 1), s_own=dma(S * L * NCH),
                   b_send=dma(S * NCH, nl - 1), b_recv=dma(S * NCH, nl - 1), b_own=dma(S * NCH),
                   gt_send=dma(2), gt_recv=dma(2), g_send=dma(2, nt - 1), g_recv=dma(2, nt - 1), h_send=dma(2, nl - 1), h_recv=dma(2, nl - 1),
                   tt_send=dma(1), tt_recv=dma(1), t_send=dma(nl - 1), t_recv=dma(nl - 1),
                   n_send=dma(nt - 1), n_recv=dma(nt - 1), m_send=dma(nl - 1), m_recv=dma(nl - 1))
    for name, out in (("sum1", "osum1"), ("sum2", "osum2"), ("vecv", "ovec"), ("tabv", "otab")):
        scratch[name] = pltpu.VMEM(*outs[out])
    scratch["o_sem"] = dma(4)
    hbm = ("x", "g") + tuple(outs)
    place = lambda name: pl.BlockSpec(memory_space=pl.ANY if name in hbm else pltpu.VMEM)
    done = dict(zip(outs, pl.pallas_call(
        functools.partial(layer_kernel, z, tuple(ins) + tuple(outs) + tuple(scratch)),
        in_specs=[place(name) for name in ins],
        out_specs=[place(name) for name in outs],
        out_shape=[jax.ShapeDtypeStruct(*o) for o in outs.values()],
        scratch_shapes=list(scratch.values()),
        compiler_params=pltpu.CompilerParams(vmem_limit_bytes=VMEM_LIMIT, collective_id=0, has_side_effects=True),
        name="layer",
    )(*ins.values())))
    last_in = dict(out0=done["out"], dx0=done["dx"], sum1_in=done["osum1"], sum2_in=done["osum2"], vec_in=done["ovec"], tab_in=done["otab"])
    last = dict(out=(g.shape, BF), dx=(inputs.shape, BF), owi=((z.rows, 3 * D), F32), owo=((z.rows, D), F32),
                oci=((z.rows, 3 * D), F32), oco=((z.rows, D), F32), oew=((z.rows, FF), F32), orw=((z.frows, D), F32),
                otab=((HEADS, tab_lanes), F32), **{f"o{i}": ((1, z.rows), F32) for i in range(6)})
    pieces = 1
    place = lambda name: pl.BlockSpec(memory_space=pl.ANY)
    small_out = [n for n in last if n not in ("out", "dx")]
    held = dict(sum1=done["osum1"], sum2=done["osum2"], vec=done["ovec"], tab=done["otab"])
    end = dict(zip(last, pl.pallas_call(
        functools.partial(finish_kernel, z, tuple(last_in) + tuple(last) + tuple(held) + tuple(n + "_held" for n in small_out) + ("out_mid", "dx_mid", "sem", "load_sem", "small_sem"), pieces),
        in_specs=[place(name) for name in last_in],
        out_specs=[place(name) for name in last],
        out_shape=[jax.ShapeDtypeStruct(*o) for o in last.values()],
        scratch_shapes=[pltpu.VMEM(a.shape, F32) for a in held.values()] + [pltpu.VMEM(*last[n]) for n in small_out]
        + [pltpu.VMEM(g.shape, BF), pltpu.VMEM(inputs.shape, BF), dma(2, 4 * S * pieces), dma(4), dma(len(small_out))],
        compiler_params=pltpu.CompilerParams(vmem_limit_bytes=VMEM_LIMIT),
        name="finish",
    )(*last_in.values())))
    output = end["out"].reshape(S, LV, z.cells, W, D).transpose(0, 1, 3, 2, 4)
    v = [end[f"o{i}"].reshape(z.rows) for i in range(6)]
    return (output, end["dx"], v[0], v[1], end["owi"], end["owo"], end["otab"].T, v[2], v[3],
            end["oci"], end["oco"], v[4], v[5], end["oew"], end["orw"])


def solution(mesh):
    t, t2 = P("tile"), P("tile", None)
    level_tokens = P(None, "lev", "tile", None, None)
    column_tokens = P(None, None, "tile", "lev", None)
    placed = (level_tokens, column_tokens, P(None, "tile", "lev"), P(), t, t, t2, t2, t2, t, t, t2, t2, t, t, t2, t2)
    outs = (column_tokens, level_tokens, t, t, t2, t2, t2, t, t, t2, t2, t, t, t2, t2)
    return jax.shard_map(functools.partial(body, mesh), mesh=mesh, in_specs=placed, out_specs=outs, check_vma=False)
```
